32 devices in a mesh: samp: 4 (over y, core), feat: 8 (over z, x).
Axes of the slice: x: 2, y: 2, z: 4, core: 2. Of those that a mesh axis runs over, the one named last changes fastest.
Arguments:
- samples: bfloat16 [4096, 4096], P('samp', 'feat'), may hold values from -8 to 8
- precision: float32 [32, 6, 128, 128], P('feat'), may hold values from -1.2 to 2
- col_blocks: int32 [32, 6], P('feat'), may hold values from -1 to 31, as said below
Outputs:
- updated: float32 [32, 6, 128, 128], P('feat')
The draws below stay inside these ranges and needn't reach their ends.
Inputs may be any that keep to these rules, and one draw needn't show every extreme that they name: `col_blocks`: slot 0 of block row j holds j; the other column blocks of a row follow in increasing order, then -1 fills the empty slots. The pattern is symmetric: row j names c exactly when row c names j. Block row j lies on index j // 4 of feat; for two different such indices, at most one block row of the one names a column block of the other, and the block rows of one index name column blocks of at most 6 other indices.
All inputs are finite; a program needn't handle non-finite values.
Results may differ from the reference program's by a relative error of at most 0.0028.
Values may be sent and summed in bfloat16 or wider, within the bound.
No kernel may reach another device: no remote copies, remote signals or barrier semaphores. Data moves between devices by JAX's collectives and lax.ppermute only.
A program may use at most 128 MiB of HBM per device.

```python
import jax
import jax.numpy as jnp
from jax import lax

BLOCK = 128
BR_DEV = 4
ITERS = 3
SPAN = 3
MAXB = 6
NB = 32
FEATURES = 4096
SAMPLES = 4096


def block_pattern(key):
    device_count = NB // BR_DEV
    reach_count = SPAN
    perm_key, rot_key, edge_key, pair_key = jax.random.split(key, 4)
    ordering = jax.random.permutation(perm_key, device_count)
    rotate = jax.random.randint(rot_key, (device_count,), 0, BR_DEV)
    labels = jnp.arange(device_count)
    offsets = jnp.arange(1, reach_count + 1)
    chosen = jax.random.randint(edge_key, (device_count, reach_count), 0, 2)
    forced = (labels[:, None] == 0) | (labels[:, None] == device_count - offsets[None, :])
    chosen = jnp.where(forced, 1, chosen)
    upper_end = (labels[:, None] + offsets[None, :]) % device_count
    lower_row = ordering[:, None] * BR_DEV + (offsets[None, :] + rotate[:, None]) % BR_DEV
    upper_row = ordering[upper_end] * BR_DEV + (offsets[None, :] + 2 + rotate[upper_end]) % BR_DEV
    adjacency = jnp.zeros((NB, NB), jnp.int32)
    adjacency = adjacency.at[lower_row.reshape(-1), upper_row.reshape(-1)].max(chosen.reshape(-1))
    adjacency = adjacency.at[upper_row.reshape(-1), lower_row.reshape(-1)].max(chosen.reshape(-1))
    pair_first = jnp.array([one for one in range(BR_DEV) for other in range(one + 1, BR_DEV)], jnp.int32)
    pair_second = jnp.array([other for one in range(BR_DEV) for other in range(one + 1, BR_DEV)], jnp.int32)
    inside = jax.random.randint(pair_key, (device_count, pair_first.shape[0]), 0, 6)
    inside = jnp.where(labels[:, None] == 0, 0, inside)
    picked = (inside == 0).astype(jnp.int32)
    rows_first = ordering[:, None] * BR_DEV + pair_first[None, :]
    rows_second = ordering[:, None] * BR_DEV + pair_second[None, :]
    adjacency = adjacency.at[rows_first.reshape(-1), rows_second.reshape(-1)].max(picked.reshape(-1))
    adjacency = adjacency.at[rows_second.reshape(-1), rows_first.reshape(-1)].max(picked.reshape(-1))
    col_ids = jnp.arange(NB)
    scores = jnp.where(col_ids[None, :] == col_ids[:, None], -1, jnp.where(adjacency > 0, col_ids[None, :], NB + col_ids[None, :]))
    ranked = jnp.argsort(scores, axis=1, stable=True)[:, :MAXB]
    present = (jnp.take_along_axis(adjacency, ranked, axis=1) > 0) | (ranked == col_ids[:, None])
    return jnp.where(present, ranked, -1).astype(jnp.int32)


def draw_col_blocks(key, part):
    return block_pattern(jax.random.fold_in(key, 11))


def draw_precision(key, part):
    pattern = block_pattern(jax.random.fold_in(key, 11))
    value_key, diag_key = jax.random.split(jax.random.fold_in(key, 12), 2)
    shape = (NB, MAXB, BLOCK, BLOCK)
    entries = jax.random.truncated_normal(value_key, -4.0, 4.0, shape, jnp.float32) * 0.3
    diagonal = jax.random.uniform(diag_key, (NB, 1, BLOCK, 1), jnp.float32, 1.0, 2.0)
    row_ids = jnp.arange(NB)[:, None]
    on_diagonal = (pattern == row_ids)[:, :, None, None] & jnp.eye(BLOCK, dtype=bool)[None, None]
    values = jnp.where(on_diagonal, diagonal, entries)
    return jnp.where((pattern >= 0)[:, :, None, None], values, 0.0).astype(jnp.float32)


def draw_samples(key, part):
    value_key, scale_key = jax.random.split(jax.random.fold_in(key, 13), 2)
    shape = (SAMPLES, FEATURES)
    scales = jnp.exp(jax.random.uniform(scale_key, (1, FEATURES), jnp.float32, -0.69, 0.69))
    base = jax.random.truncated_normal(value_key, -4.0, 4.0, shape, jnp.float32)
    return (base * scales).astype(jnp.bfloat16)


def setup_inputs(seed: int = 0) -> dict:
    key_of = jax.random.split(jax.random.key(seed), 4)
    return {
        "samples": draw_samples(jax.random.fold_in(key_of[3], 71), 0),
        "precision": draw_precision(jax.random.fold_in(key_of[3], 71), 0),
        "col_blocks": draw_col_blocks(jax.random.fold_in(key_of[3], 71), 0),
    }


step_size = 0.2
penalty = 0.25

def reference(samples, precision, col_blocks):
    sample_total = samples.shape[0]
    block_count = col_blocks.shape[0]
    slot_count = col_blocks.shape[1]
    block_size = precision.shape[2]
    filled = col_blocks >= 0
    safe_cols = jnp.where(filled, col_blocks, 0).astype(jnp.int32)
    xblocks = samples.reshape(sample_total, block_count, block_size)
    row_ids = jnp.arange(block_count, dtype=jnp.int32)
    identity_mask = jnp.eye(block_size, dtype=bool)
    on_diagonal = (col_blocks == row_ids[:, None])[:, :, None, None] & identity_mask[None, None]
    keep_mask = filled[:, :, None, None]
    matching = col_blocks[safe_cols] == row_ids[:, None, None]
    mate_slot = jnp.argmax(matching, axis=2).astype(jnp.int32)
    current = jnp.where(keep_mask, precision, jnp.float32(0.0))
    for iteration in range(ITERS):
        weights = current.astype(jnp.bfloat16)

        def row_terms(block_row):
            picked = jnp.take(xblocks, safe_cols[block_row], axis=1).reshape(sample_total, slot_count * block_size)
            weight_row = jnp.transpose(weights[block_row], (0, 2, 1)).reshape(slot_count * block_size, block_size)
            projected = jnp.dot(picked, weight_row, preferred_element_type=jnp.float32).astype(jnp.bfloat16)
            gram_row = jnp.dot(projected.T, picked, preferred_element_type=jnp.float32)
            return gram_row.reshape(block_size, slot_count, block_size).transpose(1, 0, 2)
        gram_blocks = lax.map(row_terms, row_ids) / sample_total
        mirror = gram_blocks[safe_cols, mate_slot]
        gradient = 0.5 * (gram_blocks + jnp.swapaxes(mirror, 2, 3))
        stepped = current - step_size * gradient
        shrunk = jnp.sign(stepped) * jnp.maximum(jnp.abs(stepped) - step_size * penalty, 0.0)
        rooted = 0.5 * (stepped + jnp.sqrt(stepped * stepped + 4.0 * step_size))
        current = jnp.where(keep_mask, jnp.where(on_diagonal, rooted, shrunk), jnp.float32(0.0))
    return current
```

```python
import functools

import jax
import jax.numpy as jnp
from jax import lax
from jax.experimental import pallas as pl
from jax.experimental.pallas import tpu as pltpu
from jax.sharding import PartitionSpec as P

ITERS = 3
STEP = 0.2
SHRINK = 0.05

SMEM = pl.BlockSpec(memory_space=pltpu.SMEM)
VMEM = pl.BlockSpec(memory_space=pltpu.VMEM)


def params(mib):
    return pltpu.CompilerParams(vmem_limit_bytes=mib << 20)


def dot_nt(a, b):
    return lax.dot_general(a, b, (((1,), (1,)), ((), ())), preferred_element_type=jnp.float32)


def dot_nn(a, b):
    return lax.dot_general(a, b, (((1,), (0,)), ((), ())), preferred_element_type=jnp.float32)


def for_each(lo, hi, body):
    if hi - lo <= 8:
        for i in range(lo, hi):
            body(i)
    else:
        pl.loop(lo, hi)(body)


class Local:
    def __init__(self, cb_ref, block_rows, rounds):
        self.cb = cb_ref
        self.block_rows = block_rows
        self.slots = cb_ref.shape[1]
        self.me = lax.axis_index("feat")
        self.rounds = rounds

    def slot(self, j, k):
        c = self.cb[j, k]
        filled = c >= 0
        safe = jnp.maximum(c, 0)
        holder = lax.div(safe, self.block_rows)
        return filled, filled & (holder == self.me), lax.rem(safe, self.block_rows), holder

    def place(self, holder):
        return lax.bitwise_xor(holder, self.me) if self.rounds else holder

    def fill_links(self, tab_ref):
        for p in range(tab_ref.shape[1]):
            tab_ref[0, p] = -1
            tab_ref[1, p] = -1
        for j in range(self.block_rows):
            for k in range(1, self.slots):
                filled, own, _, holder = self.slot(j, k)

                @pl.when(filled & jnp.logical_not(own))
                def _(j=j, k=k, holder=holder):
                    p = self.place(holder)
                    tab_ref[0, p] = j
                    tab_ref[1, p] = k

    def count(self, j):
        total = jnp.int32(0)
        for k in range(self.slots):
            total = total + (self.cb[j, k] >= 0).astype(jnp.int32)
        return total

    def mate(self, row, j):
        found = jnp.int32(0)
        for m in range(1, self.slots):
            found = jnp.where(self.cb[row, m] == self.me * self.block_rows + j, m, found)
        return found


def pack_kernel(rounds, cb_ref, x_ref, own_ref, *rest):
    *send_refs, tab_ref = rest
    block_rows, block, _ = own_ref.shape
    here = Local(cb_ref, block_rows, rounds)
    here.fill_links(tab_ref)
    for b in range(block_rows):
        own_ref[b] = x_ref[:, b * block : (b + 1) * block].T
    if rounds:
        for r, send_ref in enumerate(send_refs, 1):
            send_ref[...] = own_ref[jnp.maximum(tab_ref[0, r], 0)]
    else:
        (send_ref,) = send_refs

        def copy(p):
            send_ref[p] = own_ref[jnp.maximum(tab_ref[0, p], 0)]

        for_each(0, send_ref.shape[0], copy)


def put_halves(core, value, index, keep_ref, send_ref):
    half = value.shape[0] // 2
    top, bottom = value[:half], value[half:]
    keep_ref[index] = jnp.where(core == 0, top, bottom)
    send_ref[index] = jnp.where(core == 0, bottom, top)


def own_gram_kernel(own_ref, keep_ref, send_ref):
    block_rows = own_ref.shape[0]
    core = lax.rem(lax.axis_index("samp"), 2)
    for a in range(block_rows):
        for b in range(block_rows):
            put_halves(core, dot_nt(own_ref[a], own_ref[b]), (a, b), keep_ref, send_ref)


def gram_kernel(rounds, first, last, cb_ref, own_ref, *rest):
    *arrived_refs, keep_ref, send_ref, tab_ref, all_ref = rest
    block_rows = own_ref.shape[0]
    core = lax.rem(lax.axis_index("samp"), 2)
    here = Local(cb_ref, block_rows, rounds)
    here.fill_links(tab_ref)
    all_ref[:block_rows] = own_ref[...]
    if rounds:
        for i, ref in enumerate(arrived_refs):
            all_ref[block_rows + i] = ref[...]
    else:
        all_ref[block_rows:] = arrived_refs[0][...]
    base = 1 if rounds else 0

    def body(p):
        row = tab_ref[0, p]

        @pl.when(row >= 0)
        def _():
            mine = all_ref[block_rows + p - base]
            for k in range(here.slots):
                filled, own, b, holder = here.slot(row, k)
                q = here.place(holder)

                @pl.when(filled & (own | (q <= p)))
                def _():
                    source = jnp.where(own, b, block_rows + q - base)
                    put_halves(core, dot_nt(mine, all_ref[source]), (p - first, k), keep_ref, send_ref)

    for_each(first, last, body)


def joined(core, mine, other):
    top = jnp.where(core == 0, mine, other)
    bottom = jnp.where(core == 0, other, mine)
    return jnp.concatenate([top, bottom], axis=0)


def products(here, block, w_ref, gram_ref, low_ref, v_ref):
    for j in range(here.block_rows):
        count = here.count(j)
        for wide in range(2, here.slots + 1, 2):

            @pl.when((count == wide) | (count == wide - 1))
            def _(j=j, wide=wide):
                width = wide * block
                v_ref[j, :, :width] = dot_nn(w_ref[j, :, :width], gram_ref[j, :width, :width])

        for k in range(here.slots):

            @pl.when(k < count)
            def _(j=j, k=k):
                at = slice(k * block, (k + 1) * block)
                v_ref[j, :, at] += dot_nn(w_ref[j, :, at], low_ref[j, k])


def step_and_send(here, block, scale, v_ref, next_ref, out_ref):
    for j in range(here.block_rows):
        for k in range(here.slots):
            filled, own, b, holder = here.slot(j, k)
            at = slice(k * block, (k + 1) * block)

            @pl.when(own)
            def _(j=j, k=k, b=b, at=at):
                m = here.mate(b, j) if k else 0
                column = pl.ds(pl.multiple_of(m * block, block), block)
                mirrored = v_ref[b, :, column].T
                next_ref[j, k] = next_ref[j, k] - scale * (v_ref[j, :, at] + mirrored)

            @pl.when(filled & jnp.logical_not(own))
            def _(j=j, k=k, holder=holder, at=at):
                value = v_ref[j, :, at]
                next_ref[j, k] = next_ref[j, k] - scale * value
                out_ref[holder] = value.T.astype(out_ref.dtype)


def first_kernel(rounds, groups, scale, cb_ref, prec_ref, *rest):
    count = 2 * (1 + len(groups))
    pieces, rest = rest[:count], rest[count:]
    gram_ref, low_ref, next_ref, out_ref, tab_ref, w_ref, v_ref = rest
    block_rows, slots, block, _ = prec_ref.shape
    core = lax.rem(lax.axis_index("samp"), 2)
    here = Local(cb_ref, block_rows, rounds)
    here.fill_links(tab_ref)
    mine_ref, other_ref = pieces[:2]

    def place_block(row, k, l, value):
        at_k = pl.ds(pl.multiple_of(k * block, block), block)
        at_l = pl.ds(pl.multiple_of(l * block, block), block)
        high = value.astype(jnp.bfloat16)
        gram_ref[row, at_k, at_l] = high
        return high, at_k, at_l

    def place_low(row, k, value, high):
        low_ref[row, k] = (value - high.astype(jnp.float32)).astype(jnp.bfloat16)

    for j in range(block_rows):
        n = here.count(j)

        def along(k, carry, j=j, n=n):
            _, own_k, a, _ = here.slot(j, k)

            @pl.when(own_k)
            def _():
                def across(l, carry):
                    _, own_l, b, _ = here.slot(j, l)

                    @pl.when(own_l)
                    def _():
                        value = joined(core, mine_ref[a, b], other_ref[a, b])
                        high, _, _ = place_block(j, k, l, value)

                        @pl.when(k == l)
                        def _():
                            place_low(j, k, value, high)

                    return carry

                lax.fori_loop(0, n, across, 0)

            return carry

        lax.fori_loop(0, n, along, 0)
        for odd in range(1, slots, 2):

            @pl.when(n == odd)
            def _(j=j, odd=odd):
                gram_ref[j, odd * block : (odd + 1) * block, :] = jnp.zeros(
                    (block, slots * block), gram_ref.dtype
                )

    for (first, last), mine_ref, other_ref in zip(groups, pieces[2::2], pieces[3::2]):

        def body(p, first=first, mine_ref=mine_ref, other_ref=other_ref):
            row, k = tab_ref[0, p], tab_ref[1, p]

            @pl.when(row >= 0)
            def _():
                for l in range(slots):
                    filled, own, _, holder = here.slot(row, l)

                    @pl.when(filled & (own | (here.place(holder) <= p)))
                    def _(l=l):
                        value = joined(core, mine_ref[p - first, l], other_ref[p - first, l])
                        high, at_k, at_l = place_block(row, k, l, value)

                        @pl.when(k == l)
                        def _():
                            place_low(row, k, value, high)

                        @pl.when(k != l)
                        def _():
                            gram_ref[row, at_l, at_k] = value.T.astype(jnp.bfloat16)

        for_each(first, last, body)

    for j in range(block_rows):
        for k in range(slots):
            filled = here.cb[j, k] >= 0

            @pl.when(filled)
            def _(j=j, k=k):
                value = prec_ref[j, k]
                next_ref[j, k] = value
                w_ref[j, :, k * block : (k + 1) * block] = value.astype(jnp.bfloat16)

            @pl.when(jnp.logical_not(filled))
            def _(j=j, k=k):
                next_ref[j, k] = jnp.zeros((block, block), jnp.float32)
                w_ref[j, :, k * block : (k + 1) * block] = jnp.zeros((block, block), jnp.bfloat16)

    products(here, block, w_ref, gram_ref, low_ref, v_ref)
    step_and_send(here, block, scale, v_ref, next_ref, out_ref)


def prox_blocks(here, block, scale, stepped_ref, in_ref, next_ref, w_ref):
    eye = lax.broadcasted_iota(jnp.int32, (block, block), 0) == lax.broadcasted_iota(
        jnp.int32, (block, block), 1
    )

    def finish(j, k, m):
        value = m - jnp.clip(m, -SHRINK, SHRINK)
        if k == 0:
            value = jnp.where(eye, 0.5 * (m + jnp.sqrt(m * m + 4.0 * STEP)), value)
        next_ref[j, k] = value
        if w_ref is not None:
            w_ref[j, :, k * block : (k + 1) * block] = value.astype(jnp.bfloat16)

    for j in range(here.block_rows):
        for k in range(here.slots):
            filled, own, _, holder = here.slot(j, k)

            @pl.when(own)
            def _(j=j, k=k):
                finish(j, k, stepped_ref[j, k])

            @pl.when(filled & jnp.logical_not(own))
            def _(j=j, k=k, holder=holder):
                finish(j, k, stepped_ref[j, k] - scale * in_ref[holder].astype(jnp.float32))

            @pl.when(jnp.logical_not(filled))
            def _(j=j, k=k):
                next_ref[j, k] = jnp.zeros((block, block), jnp.float32)
                if w_ref is not None:
                    w_ref[j, :, k * block : (k + 1) * block] = jnp.zeros((block, block), jnp.bfloat16)


def middle_kernel(scale, cb_ref, stepped_ref, in_ref, gram_ref, low_ref, next_ref, out_ref, w_ref, v_ref):
    block_rows, _, block, _ = stepped_ref.shape
    here = Local(cb_ref, block_rows, False)
    prox_blocks(here, block, scale, stepped_ref, in_ref, next_ref, w_ref)
    products(here, block, w_ref, gram_ref, low_ref, v_ref)
    step_and_send(here, block, scale, v_ref, next_ref, out_ref)


def last_kernel(scale, cb_ref, stepped_ref, in_ref, next_ref):
    block_rows, _, block, _ = stepped_ref.shape
    prox_blocks(Local(cb_ref, block_rows, False), block, scale, stepped_ref, in_ref, next_ref, None)


def call(kernel, inputs, outs, scratch, mib, smem=1, flops=0):
    moved = sum(x.size * x.dtype.itemsize for x in (*inputs, *outs))
    return pl.pallas_call(
        kernel,
        out_shape=outs,
        in_specs=[SMEM] * smem + [VMEM] * (len(inputs) - smem),
        out_specs=[VMEM] * len(outs),
        scratch_shapes=scratch,
        compiler_params=params(mib),
        cost_estimate=pl.CostEstimate(flops=flops, bytes_accessed=moved, transcendentals=0),
    )(*inputs)


def swap(x, bit):
    count = lax.axis_size("samp")
    return lax.ppermute(x, "samp", [(i, i ^ bit) for i in range(count)])


def sum_over_samp(keep, send):
    half = keep + swap(send, 1)
    bit = 2
    while bit < lax.axis_size("samp"):
        half = half + swap(half, bit)
        bit *= 2
    return half, swap(half, 1)


def local(samples, precision, col_blocks):
    row_count = samples.shape[0]
    block_rows, slots, block, _ = precision.shape
    peers = lax.axis_size("feat")
    scale = 0.5 * STEP / (row_count * lax.axis_size("samp"))
    rounds = peers <= 8
    groups = [(1, 4), (4, 6), (6, 8)] if rounds and peers == 8 else [(1 if rounds else 0, peers)]

    def shape(dims, dtype):
        return jax.ShapeDtypeStruct(dims, dtype)

    bf16, f32 = samples.dtype, jnp.float32
    tab = pltpu.SMEM((2, peers), jnp.int32)
    strip = (block, row_count)
    sends = [shape(strip, bf16)] * (peers - 1) if rounds else [shape((peers, *strip), bf16)]
    own, *sends = call(
        functools.partial(pack_kernel, rounds),
        (col_blocks, samples),
        [shape((block_rows, *strip), bf16), *sends],
        [tab],
        48,
    )
    if rounds:
        arrived = [
            lax.ppermute(x, "feat", [(i, i ^ r) for i in range(peers)])
            for r, x in enumerate(sends, 1)
        ]
    else:
        arrived = [lax.all_to_all(sends[0], "feat", 0, 0, tiled=True)]
    pieces = []
    halves = shape((block_rows, block_rows, block // 2, block), f32)
    pieces += sum_over_samp(*call(own_gram_kernel, (own,), [halves] * 2, [], 48, smem=0))
    for first, last in groups:
        known = arrived[: last - 1] if rounds else arrived
        halves = shape((last - first, slots, block // 2, block), f32)
        held = pltpu.VMEM((block_rows + (last - 1 if rounds else peers), *strip), bf16)
        pieces += sum_over_samp(
            *call(
                functools.partial(gram_kernel, rounds, first, last),
                (col_blocks, own, *known),
                [halves] * 2,
                [tab, held],
                60,
            )
        )
    blocks = shape(precision.shape, f32)
    swapped = shape((peers, block, block), bf16)
    work = [
        pltpu.VMEM((block_rows, block, slots * block), bf16),
        pltpu.VMEM((block_rows, block, slots * block), f32),
    ]
    gram, low, stepped, out = call(
        functools.partial(first_kernel, rounds, groups, scale),
        (col_blocks, precision, *pieces),
        [
            shape((block_rows, slots * block, slots * block), bf16),
            shape(precision.shape, bf16),
            blocks,
            swapped,
        ],
        [tab, *work],
        60,
    )
    for iteration in range(ITERS):
        mirrored = lax.all_to_all(out, "feat", 0, 0, tiled=True)
        if iteration + 1 < ITERS:
            stepped, out = call(
                functools.partial(middle_kernel, scale),
                (col_blocks, stepped, mirrored, gram, low),
                [blocks, swapped],
                work,
                60,
            )
    (updated,) = call(
        functools.partial(last_kernel, scale), (col_blocks, stepped, mirrored), [blocks], [], 48
    )
    return updated


def solution(mesh):
    return jax.shard_map(
        local,
        mesh=mesh,
        in_specs=(P("samp", "feat"), P("feat", None, None, None), P("feat", None)),
        out_specs=P("feat", None, None, None),
        check_vma=False,
    )
```

```python
import functools
import math

import jax
import jax.numpy as jnp
from jax import lax
from jax.experimental import pallas as pl
from jax.experimental.pallas import tpu as pltpu
from jax.sharding import PartitionSpec as P

ITERS = 3
STEP = 0.2
SHRINK = 0.05

SMEM = pl.BlockSpec(memory_space=pltpu.SMEM)
VMEM = pl.BlockSpec(memory_space=pltpu.VMEM)


def dot_nt(a, b):
    return lax.dot_general(a, b, (((1,), (1,)), ((), ())), preferred_element_type=jnp.float32)


def dot_nn(a, b):
    return lax.dot_general(a, b, (((1,), (0,)), ((), ())), preferred_element_type=jnp.float32)


def for_each(lo, hi, body):
    if hi - lo <= 8:
        for i in range(lo, hi):
            body(i)
    else:
        pl.loop(lo, hi)(body)


class Local:
    def __init__(self, cb_ref, block_rows, rounds):
        self.cb = cb_ref
        self.block_rows = block_rows
        self.slots = cb_ref.shape[1]
        self.me = lax.axis_index("feat")
        self.core = lax.rem(lax.axis_index("samp"), 2)
        self.rounds = rounds

    def slot(self, j, k):
        c = self.cb[j, k]
        filled = c >= 0
        safe = jnp.maximum(c, 0)
        holder = lax.div(safe, self.block_rows)
        return filled, filled & (holder == self.me), lax.rem(safe, self.block_rows), holder

    def place(self, holder):
        return lax.bitwise_xor(holder, self.me) if self.rounds else holder

    def fill_links(self, tab_ref):
        for p in range(tab_ref.shape[1]):
            tab_ref[0, p] = -1
            tab_ref[1, p] = -1
        @pl.loop(0, self.block_rows)
        def _(j):
            for k in range(1, self.slots):
                filled, own, _, holder = self.slot(j, k)

                @pl.when(filled & jnp.logical_not(own))
                def _(k=k, holder=holder):
                    p = self.place(holder)
                    tab_ref[0, p] = j
                    tab_ref[1, p] = k

    def count(self, j):
        total = jnp.int32(0)
        for k in range(self.slots):
            total = total + (self.cb[j, k] >= 0).astype(jnp.int32)
        return total

    def mate(self, row, j):
        found = jnp.int32(0)
        for m in range(1, self.slots):
            found = jnp.where(self.cb[row, m] == self.me * self.block_rows + j, m, found)
        return found


def aligned(index, block):
    return pl.ds(pl.multiple_of(index * block, block), block)


def pack_kernel(rounds, cb_ref, x_ref, own_ref, *rest):
    *send_refs, tab_ref = rest
    block_rows, block, _ = own_ref.shape
    here = Local(cb_ref, block_rows, rounds)
    here.fill_links(tab_ref)
    for b in range(block_rows):
        own_ref[b] = x_ref[:, b * block : (b + 1) * block].T
    if rounds:
        for r, send_ref in enumerate(send_refs, 1):
            send_ref[...] = own_ref[jnp.maximum(tab_ref[0, r], 0)]
    else:
        (send_ref,) = send_refs

        def copy(p):
            send_ref[p] = own_ref[jnp.maximum(tab_ref[0, p], 0)]

        for_each(0, send_ref.shape[0], copy)


def eye_of(block):
    return lax.broadcasted_iota(jnp.int32, (block, block), 0) == lax.broadcasted_iota(
        jnp.int32, (block, block), 1
    )


def low_diagonal(value, high):
    rest = value - high.astype(jnp.float32)
    return jnp.sum(jnp.where(eye_of(value.shape[0]), rest, 0.0), axis=0, keepdims=True)


def put_block(out_ref, i, position, value, diagonal):
    block = value.shape[0]
    high = value.astype(jnp.bfloat16)
    out_ref[i, aligned(position, block)] = high

    @pl.when(diagonal)
    def _():
        low = jnp.broadcast_to(low_diagonal(value, high), (16, block))
        out_ref[i, out_ref.shape[1] - 16 :] = low.astype(jnp.bfloat16)


def own_gram_kernel(mine_ref, other_ref, out_ref):
    block_rows = mine_ref.shape[0]
    core = lax.rem(lax.axis_index("samp"), 2)
    for i in range(block_rows // 2):
        a = 2 * i + core
        for b in range(block_rows):
            value = dot_nt(mine_ref[a], mine_ref[b]) + dot_nt(other_ref[a], other_ref[b])
            put_block(out_ref, i, b, value, a == b)


def position_of(k, l):
    return jnp.where(l == k, 0, jnp.where(l == 0, k, l))


def gram_kernel(rounds, first, last, cb_ref, mine_ref, other_ref, *rest):
    *arrived_refs, out_ref, tab_ref, held_ref = rest
    block_rows = mine_ref.shape[0]
    here = Local(cb_ref, block_rows, rounds)
    here.fill_links(tab_ref)
    count = len(arrived_refs) // 2
    known = last if rounds else tab_ref.shape[1]

    def pair(q):
        if rounds:
            return arrived_refs[q - 1][...], arrived_refs[count + q - 1][...]
        return arrived_refs[0][q], arrived_refs[1][q]

    def body(p):
        row, k = tab_ref[0, p], tab_ref[1, p]

        @pl.when((row >= 0) & (lax.rem(p, 2) == here.core))
        def _():
            held_ref[0], held_ref[1] = pair(p)
            i = (p - first) // 2

            def put(l, a, b):
                value = dot_nt(held_ref[0], a) + dot_nt(held_ref[1], b)
                put_block(out_ref, i, position_of(k, l), value, l == k)

            @pl.loop(0, here.slots)
            def _(l):
                _, own, b, _ = here.slot(row, l)

                @pl.when(own)
                def _():
                    put(l, mine_ref[b], other_ref[b])

            def with_arrival(q):
                @pl.when((tab_ref[0, q] == row) & (q <= p))
                def _():
                    put(tab_ref[1, q], *pair(q))

            if rounds:
                for q in range(1, p + 1):
                    with_arrival(q)
            else:
                pl.loop(0, known)(with_arrival)

    if rounds:
        for p in range(max(first, 1), last):
            body(p)
    else:
        pl.loop(first, last)(body)


def read_part(parts, mine, index):
    half = len(parts) // 2
    terms = [
        jnp.where(mine, a[index], b[index]).astype(jnp.float32)
        for a, b in zip(parts[:half], parts[half:])
    ]
    while len(terms) > 1:
        terms = [a + b for a, b in zip(terms[::2], terms[1::2])]
    return terms[0]


def place_block(gram_ref, low_ref, row, k, l, value, lows):
    block = value.shape[0]
    high = value.astype(jnp.bfloat16)
    gram_ref[row, aligned(k, block), aligned(l, block)] = high

    @pl.when(k == l)
    def _():
        low_ref[row, pl.ds(k, 1)] = low_diagonal(value, high) + lows()


def place_arrivals(here, first, last, parts, tab_ref, gram_ref, low_ref):
    block = parts[0].shape[2]
    slots = here.slots

    def body(p):
        row, k = tab_ref[0, p], tab_ref[1, p]

        @pl.when(row >= 0)
        def _():
            mine = lax.rem(p, 2) == here.core
            i = (p - first) // 2

            def lows():
                return read_part(parts, mine, (i, pl.ds(slots * block, 1)))

            @pl.loop(0, slots)
            def _(l):
                filled, own, _, holder = here.slot(row, l)

                @pl.when(filled & (own | (here.place(holder) <= p)))
                def _():
                    value = read_part(parts, mine, (i, aligned(position_of(k, l), block)))
                    place_block(gram_ref, low_ref, row, k, l, value, lows)

                    @pl.when(k != l)
                    def _():
                        flipped = value.T.astype(jnp.bfloat16)
                        gram_ref[row, aligned(l, block), aligned(k, block)] = flipped

    pl.loop(first, last)(body)


def place_own(here, block, parts, gram_ref, low_ref):
    slots = here.slots
    @pl.loop(0, here.block_rows)
    def _(j):
        n = here.count(j)

        def along(k, carry):
            _, own_k, a, _ = here.slot(j, k)

            @pl.when(own_k)
            def _():
                mine = lax.rem(a, 2) == here.core
                i = lax.div(a, 2)

                def lows():
                    return read_part(parts, mine, (i, pl.ds(here.block_rows * block, 1)))

                def across(l, carry):
                    _, own_l, b, _ = here.slot(j, l)

                    @pl.when(own_l)
                    def _():
                        value = read_part(parts, mine, (i, aligned(b, block)))
                        place_block(gram_ref, low_ref, j, k, l, value, lows)

                    return carry

                lax.fori_loop(0, n, across, 0)

            return carry

        lax.fori_loop(0, n, along, 0)
        for odd in range(1, slots, 2):

            @pl.when(n == odd)
            def _(odd=odd):
                gram_ref[j, odd * block : (odd + 1) * block, :] = jnp.zeros(
                    (block, slots * block), gram_ref.dtype
                )


def gather_kernel(rounds, groups, ways, cb_ref, *rest):
    count = 2 * ways
    parts, (gram_ref, low_ref, tab_ref) = rest[:-3], rest[-3:]
    block_rows, wide, _ = gram_ref.shape
    here = Local(cb_ref, block_rows, rounds)
    here.fill_links(tab_ref)
    place_own(here, wide // here.slots, parts[:count], gram_ref, low_ref)
    for g, (first, last) in enumerate(groups, 1):
        place_arrivals(here, first, last, parts[g * count : (g + 1) * count], tab_ref, gram_ref, low_ref)


def products(here, block, w_ref, gram_ref, low_ref, v_ref):
    @pl.loop(0, here.block_rows)
    def _(j):
        count = here.count(j)
        for wide in range(2, here.slots + 1, 2):

            @pl.when((count == wide) | (count == wide - 1))
            def _(wide=wide):
                width = wide * block
                v_ref[j, :, :width] = dot_nn(w_ref[j, :, :width], gram_ref[j, :width, :width])
                for k in range(wide):
                    at = slice(k * block, (k + 1) * block)
                    v_ref[j, :, at] += w_ref[j, :, at].astype(jnp.float32) * low_ref[j, k : k + 1]


def step_and_send(here, block, scale, v_ref, next_ref, out_ref):
    @pl.loop(0, here.block_rows)
    def _(j):
        for k in range(here.slots):
            filled, own, b, holder = here.slot(j, k)
            at = slice(k * block, (k + 1) * block)

            @pl.when(own)
            def _(k=k, b=b, at=at):
                m = here.mate(b, j) if k else 0
                mirrored = v_ref[b, :, aligned(m, block)].T
                next_ref[j, k] = next_ref[j, k] - scale * (v_ref[j, :, at] + mirrored)

            @pl.when(filled & jnp.logical_not(own))
            def _(k=k, holder=holder, at=at):
                value = v_ref[j, :, at]
                next_ref[j, k] = next_ref[j, k] - scale * value
                out_ref[holder] = value.astype(out_ref.dtype).T


def first_kernel(rounds, group, ways, scale, cb_ref, prec_ref, gram_in_ref, low_in_ref, *rest):
    parts, rest = rest[: 2 * ways], rest[2 * ways :]
    gram_ref, low_ref, next_ref, out_ref, tab_ref, w_ref, v_ref = rest
    block_rows, slots, block, _ = prec_ref.shape
    here = Local(cb_ref, block_rows, rounds)
    here.fill_links(tab_ref)
    low_ref[...] = low_in_ref[...]

    @pl.loop(0, block_rows * slots)
    def _(i):
        at = (lax.div(i, slots), aligned(lax.rem(i, slots), block))
        gram_ref[at] = gram_in_ref[at]

    place_arrivals(here, *group, parts, tab_ref, gram_ref, low_ref)
    @pl.loop(0, block_rows)
    def _(j):
        for k in range(slots):
            filled = here.cb[j, k] >= 0
            value = jnp.where(filled, prec_ref[j, k], 0.0)
            next_ref[j, k] = value
            w_ref[j, :, k * block : (k + 1) * block] = value.astype(jnp.bfloat16)
    products(here, block, w_ref, gram_ref, low_ref, v_ref)
    step_and_send(here, block, scale, v_ref, next_ref, out_ref)


def prox_blocks(here, block, scale, stepped_ref, in_ref, next_ref, w_ref):
    eye = eye_of(block)

    def finish(j, k, m):
        value = m - jnp.clip(m, -SHRINK, SHRINK)
        if k == 0:
            value = jnp.where(eye, 0.5 * (m + jnp.sqrt(m * m + 4.0 * STEP)), value)
        next_ref[j, k] = value
        if w_ref is not None:
            w_ref[j, :, k * block : (k + 1) * block] = value.astype(jnp.bfloat16)

    @pl.loop(0, here.block_rows)
    def _(j):
        for k in range(here.slots):
            filled, own, _, holder = here.slot(j, k)

            @pl.when(own)
            def _(k=k):
                finish(j, k, stepped_ref[j, k])

            @pl.when(filled & jnp.logical_not(own))
            def _(k=k, holder=holder):
                finish(j, k, stepped_ref[j, k] - scale * in_ref[holder].astype(jnp.float32))

            @pl.when(jnp.logical_not(filled))
            def _(k=k):
                next_ref[j, k] = jnp.zeros((block, block), jnp.float32)
                if w_ref is not None:
                    w_ref[j, :, k * block : (k + 1) * block] = jnp.zeros((block, block), jnp.bfloat16)


def middle_kernel(scale, cb_ref, stepped_ref, in_ref, gram_ref, low_ref, next_ref, out_ref, w_ref, v_ref):
    block_rows, _, block, _ = stepped_ref.shape
    here = Local(cb_ref, block_rows, False)
    prox_blocks(here, block, scale, stepped_ref, in_ref, next_ref, w_ref)
    products(here, block, w_ref, gram_ref, low_ref, v_ref)
    step_and_send(here, block, scale, v_ref, next_ref, out_ref)


def last_kernel(scale, cb_ref, stepped_ref, in_ref, next_ref):
    block_rows, _, block, _ = stepped_ref.shape
    prox_blocks(Local(cb_ref, block_rows, False), block, scale, stepped_ref, in_ref, next_ref, None)


def call(kernel, inputs, outs, scratch, smem=1):
    arrays = (*inputs, *outs, *scratch)
    size = sum(math.prod(x.shape) * jnp.dtype(x.dtype).itemsize for x in arrays)
    return pl.pallas_call(
        kernel,
        out_shape=outs,
        in_specs=[SMEM] * smem + [VMEM] * (len(inputs) - smem),
        out_specs=[VMEM] * len(outs),
        scratch_shapes=scratch,
        compiler_params=pltpu.CompilerParams(vmem_limit_bytes=size + (6 << 20)),
        cost_estimate=pl.CostEstimate(flops=1, bytes_accessed=1, transcendentals=0),
    )(*inputs)


def swap(x, bit):
    count = lax.axis_size("samp")
    return lax.ppermute(x, "samp", [(i, i ^ bit) for i in range(count)])


def everywhere(x):
    mine = [x] + [swap(x, bit) for bit in range(2, lax.axis_size("samp"), 2)]
    return mine + [swap(part, 1) for part in mine]


def after(x, *earlier):
    return lax.optimization_barrier((x, *earlier))[0]


def local(samples, precision, col_blocks):
    row_count = samples.shape[0]
    block_rows, slots, block, _ = precision.shape
    peers = lax.axis_size("feat")
    ways = lax.axis_size("samp") // 2
    scale = 0.5 * STEP / (row_count * lax.axis_size("samp"))
    rounds = peers == 8
    groups = [(0, 4), (4, 6), (6, 8)] if rounds else [(0, peers)]

    def shape(dims, dtype):
        return jax.ShapeDtypeStruct(dims, dtype)

    bf16, f32 = samples.dtype, jnp.float32
    tab = pltpu.SMEM((2, peers), jnp.int32)
    strip = (block, row_count)
    sends = [shape(strip, bf16)] * (peers - 1) if rounds else [shape((peers, *strip), bf16)]
    own, *sends = call(
        functools.partial(pack_kernel, rounds),
        (col_blocks, samples),
        [shape((block_rows, *strip), bf16), *sends],
        [tab],
    )

    def exchange(x, r):
        return lax.ppermute(x, "feat", [(i, i ^ r) for i in range(peers)])

    if rounds:
        arrived = [exchange(sends[r - 1], r) for r in range(1, 6)]
        arrived += [exchange(after(sends[r - 1], arrived[r - 3]), r) for r in (6, 7)]
    else:
        arrived = [lax.all_to_all(sends[0], "feat", 0, 0, tiled=True)]
    own_pair = (own, swap(own, 1))
    over = [swap(x, 1) for x in arrived]
    lists = [
        everywhere(
            call(
                own_gram_kernel,
                own_pair,
                [shape((block_rows // 2, block_rows * block + 16, block), bf16)],
                [],
                smem=0,
            )[0]
        )
    ]
    for first, last in groups:
        known = last - 1 if rounds else 1
        lists.append(
            everywhere(
                call(
                    functools.partial(gram_kernel, rounds, first, last),
                    (col_blocks, *own_pair, *arrived[:known], *over[:known]),
                    [shape(((last - first) // 2, slots * block + 16, block), bf16)],
                    [tab, pltpu.VMEM((2, *strip), bf16)],
                )[0]
            )
        )
    grams = [
        shape((block_rows, slots * block, slots * block), bf16),
        shape((block_rows, 8, block), f32),
    ]
    blocks = shape(precision.shape, f32)
    swapped = shape((peers, block, block), bf16)
    work = [
        pltpu.VMEM((block_rows, block, slots * block), bf16),
        pltpu.VMEM((block_rows, block, slots * block), f32),
    ]
    gram, low = call(
        functools.partial(gather_kernel, rounds, groups[:-1], ways),
        (col_blocks, *sum(lists[:-1], [])),
        grams,
        [tab],
    )
    gram, low, stepped, out = call(
        functools.partial(first_kernel, rounds, groups[-1], ways, scale),
        (col_blocks, precision, gram, low, *lists[-1]),
        [*grams, blocks, swapped],
        [tab, *work],
    )
    for iteration in range(ITERS):
        mirrored = lax.all_to_all(out, "feat", 0, 0, tiled=True)
        if iteration + 1 < ITERS:
            stepped, out = call(
                functools.partial(middle_kernel, scale),
                (col_blocks, stepped, mirrored, gram, low),
                [blocks, swapped],
                work,
            )
    (updated,) = call(functools.partial(last_kernel, scale), (col_blocks, stepped, mirrored), [blocks], [])
    return updated


def solution(mesh):
    return jax.shard_map(
        local,
        mesh=mesh,
        in_specs=(P("samp", "feat"), P("feat", None, None, None), P("feat", None)),
        out_specs=P("feat", None, None, None),
        check_vma=False,
    )
```

```python
import functools
import math

import jax
import jax.numpy as jnp
from jax import lax
from jax.experimental import pallas as pl
from jax.experimental.pallas import tpu as pltpu
from jax.sharding import PartitionSpec as P

ITERS = 3
STEP = 0.2
SHRINK = 0.05

SMEM = pl.BlockSpec(memory_space=pltpu.SMEM)
VMEM = pl.BlockSpec(memory_space=pltpu.VMEM)


def dot_nt(a, b):
    return lax.dot_general(a, b, (((1,), (1,)), ((), ())), preferred_element_type=jnp.float32)


def dot_nn(a, b):
    return lax.dot_general(a, b, (((1,), (0,)), ((), ())), preferred_element_type=jnp.float32)


def for_each(lo, hi, body):
    if hi - lo <= 8:
        for i in range(lo, hi):
            body(i)
    else:
        pl.loop(lo, hi)(body)


class Local:
    def __init__(self, cb_ref, block_rows, rounds):
        self.cb = cb_ref
        self.block_rows = block_rows
        self.slots = cb_ref.shape[1]
        self.me = lax.axis_index("feat")
        self.core = lax.rem(lax.axis_index("samp"), 2)
        self.rounds = rounds

    def slot(self, j, k):
        c = self.cb[j, k]
        filled = c >= 0
        safe = jnp.maximum(c, 0)
        holder = lax.div(safe, self.block_rows)
        return filled, filled & (holder == self.me), lax.rem(safe, self.block_rows), holder

    def place(self, holder):
        return lax.bitwise_xor(holder, self.me) if self.rounds else holder

    def fill_links(self, tab_ref):
        for p in range(tab_ref.shape[1]):
            tab_ref[0, p] = -1
            tab_ref[1, p] = -1
        @pl.loop(0, self.block_rows)
        def _(j):
            for k in range(1, self.slots):
                filled, own, _, holder = self.slot(j, k)

                @pl.when(filled & jnp.logical_not(own))
                def _(k=k, holder=holder):
                    p = self.place(holder)
                    tab_ref[0, p] = j
                    tab_ref[1, p] = k

    def count(self, j):
        total = jnp.int32(0)
        for k in range(self.slots):
            total = total + (self.cb[j, k] >= 0).astype(jnp.int32)
        return total

    def mate(self, row, j):
        found = jnp.int32(0)
        for m in range(1, self.slots):
            found = jnp.where(self.cb[row, m] == self.me * self.block_rows + j, m, found)
        return found


def aligned(index, block):
    return pl.ds(pl.multiple_of(index * block, block), block)


def pack_kernel(rounds, cb_ref, x_ref, own_ref, *rest):
    *send_refs, tab_ref = rest
    block_rows, block, _ = own_ref.shape
    here = Local(cb_ref, block_rows, rounds)
    here.fill_links(tab_ref)
    for b in range(block_rows):
        own_ref[b] = x_ref[:, b * block : (b + 1) * block].T
    if rounds:
        for r, send_ref in enumerate(send_refs, 1):
            send_ref[...] = own_ref[jnp.maximum(tab_ref[0, r], 0)]
    else:
        (send_ref,) = send_refs

        def copy(p):
            send_ref[p] = own_ref[jnp.maximum(tab_ref[0, p], 0)]

        for_each(0, send_ref.shape[0], copy)


def eye_of(block):
    return lax.broadcasted_iota(jnp.int32, (block, block), 0) == lax.broadcasted_iota(
        jnp.int32, (block, block), 1
    )


def low_diagonal(value, high):
    rest = value - high.astype(jnp.float32)
    return jnp.sum(jnp.where(eye_of(value.shape[0]), rest, 0.0), axis=0, keepdims=True)


def put_block(out_ref, i, position, value, diagonal):
    block = value.shape[0]
    high = value.astype(jnp.bfloat16)
    out_ref[i, aligned(position, block)] = high

    @pl.when(diagonal)
    def _():
        low = jnp.broadcast_to(low_diagonal(value, high), (16, block))
        out_ref[i, out_ref.shape[1] - 16 :] = low.astype(jnp.bfloat16)


def own_pairs(block_rows):
    pairs = [(a, b) for a in range(block_rows) for b in range(a, block_rows)]
    return list(zip(pairs[::2], pairs[1::2]))


def own_gram_kernel(mine_ref, other_ref, out_ref):
    core = lax.rem(lax.axis_index("samp"), 2)
    for i, ((a, b), (c, d)) in enumerate(own_pairs(mine_ref.shape[0])):
        x, y = jnp.where(core == 0, a, c), jnp.where(core == 0, b, d)
        value = dot_nt(mine_ref[x], mine_ref[y]) + dot_nt(other_ref[x], other_ref[y])
        put_block(out_ref, i, 0, value, x == y)


def position_of(k, l):
    return jnp.where(l == k, 0, jnp.where(l == 0, k, l))


def gram_kernel(rounds, first, last, cb_ref, mine_ref, other_ref, *rest):
    *arrived_refs, out_ref, tab_ref, held_ref = rest
    block_rows = mine_ref.shape[0]
    here = Local(cb_ref, block_rows, rounds)
    here.fill_links(tab_ref)
    count = len(arrived_refs) // 2
    known = last if rounds else tab_ref.shape[1]

    def pair(q):
        if rounds:
            return arrived_refs[q - 1][...], arrived_refs[count + q - 1][...]
        return arrived_refs[0][q], arrived_refs[1][q]

    def body(p):
        row, k = tab_ref[0, p], tab_ref[1, p]

        @pl.when(row >= 0)
        def _():
            held_ref[0], held_ref[1] = pair(p)

            def put(l, a, b):
                value = dot_nt(held_ref[0], a) + dot_nt(held_ref[1], b)
                put_block(out_ref, p - first, position_of(k, l) // 2, value, l == k)

            def ours(l):
                return lax.rem(position_of(k, l), 2) == here.core

            @pl.loop(0, here.slots)
            def _(l):
                _, own, b, _ = here.slot(row, l)

                @pl.when(own & ours(l))
                def _():
                    put(l, mine_ref[b], other_ref[b])

            def with_arrival(q):
                l = tab_ref[1, q]

                @pl.when((tab_ref[0, q] == row) & (q <= p) & ours(l))
                def _():
                    put(l, *pair(q))

            if rounds:
                for q in range(1, p + 1):
                    with_arrival(q)
            else:
                pl.loop(0, known)(with_arrival)

    if rounds:
        for p in range(first, last):
            body(p)
    else:
        pl.loop(first, last)(body)


def read_part(parts, mine, index):
    half = len(parts) // 2
    terms = [
        jnp.where(mine, a[index], b[index]).astype(jnp.float32)
        for a, b in zip(parts[:half], parts[half:])
    ]
    while len(terms) > 1:
        terms = [a + b for a, b in zip(terms[::2], terms[1::2])]
    return terms[0]


def place_block(gram_ref, low_ref, row, k, l, value, lows):
    block = value.shape[0]
    high = value.astype(jnp.bfloat16)
    gram_ref[row, aligned(k, block), aligned(l, block)] = high

    @pl.when(k == l)
    def _():
        low_ref[row, pl.ds(k, 1)] = low_diagonal(value, high) + lows()


def place_arrivals(here, first, last, parts, tab_ref, gram_ref, low_ref):
    block = parts[0].shape[2]
    slots = here.slots

    def body(p):
        row, k = tab_ref[0, p], tab_ref[1, p]

        @pl.when(row >= 0)
        def _():
            i = p - first

            def lows():
                return read_part(parts, here.core == 0, (i, pl.ds(slots // 2 * block, 1)))

            @pl.loop(0, slots)
            def _(l):
                filled, own, _, holder = here.slot(row, l)

                @pl.when(filled & (own | (here.place(holder) <= p)))
                def _():
                    position = position_of(k, l)
                    mine = lax.rem(position, 2) == here.core
                    value = read_part(parts, mine, (i, aligned(position // 2, block)))
                    place_block(gram_ref, low_ref, row, k, l, value, lows)

                    @pl.when(k != l)
                    def _():
                        flipped = value.T.astype(jnp.bfloat16)
                        gram_ref[row, aligned(l, block), aligned(k, block)] = flipped

    pl.loop(first, last)(body)


def place_own(here, block, parts, gram_ref, low_ref, sum_ref, row_ref):
    slots, block_rows = here.slots, here.block_rows

    for i, two in enumerate(own_pairs(block_rows)):
        for core, (a, b) in enumerate(two):
            value = read_part(parts, here.core == core, (i, slice(0, block)))
            high = value.astype(jnp.bfloat16)
            sum_ref[a, b] = high
            if a == b:
                lows = read_part(parts, here.core == core, (i, slice(block, block + 1)))
                row_ref[a : a + 1] = low_diagonal(value, high) + lows
            else:
                sum_ref[b, a] = high.T

    @pl.loop(0, block_rows)
    def _(j):
        n = here.count(j)

        def along(k, carry):
            _, own_k, a, _ = here.slot(j, k)

            @pl.when(own_k)
            def _():
                low_ref[j, pl.ds(k, 1)] = row_ref[pl.ds(a, 1)]
                for l in range(slots):
                    _, own_l, b, _ = here.slot(j, l)

                    @pl.when(own_l)
                    def _(l=l, b=b):
                        gram_ref[j, aligned(k, block), l * block : (l + 1) * block] = sum_ref[a, b]

            return carry

        lax.fori_loop(0, n, along, 0)
        for odd in range(1, slots, 2):

            @pl.when(n == odd)
            def _(odd=odd):
                gram_ref[j, odd * block : (odd + 1) * block, :] = jnp.zeros(
                    (block, slots * block), gram_ref.dtype
                )


def gather_kernel(rounds, groups, ways, cb_ref, *rest):
    *parts, gram_ref, low_ref, tab_ref, sum_ref, row_ref = rest
    block_rows, wide, _ = gram_ref.shape
    here = Local(cb_ref, block_rows, rounds)
    here.fill_links(tab_ref)
    place_own(here, wide // here.slots, parts[: 2 * ways], gram_ref, low_ref, sum_ref, row_ref)
    for g, (first, last) in enumerate(groups, 1):
        at = slice(2 * ways * g, 2 * ways * (g + 1))
        place_arrivals(here, first, last, parts[at], tab_ref, gram_ref, low_ref)


def products(here, block, w_ref, gram_ref, low_ref, v_ref):
    @pl.loop(0, here.block_rows)
    def _(j):
        count = here.count(j)
        for wide in range(2, here.slots + 1, 2):

            @pl.when((count == wide) | (count == wide - 1))
            def _(wide=wide):
                width = wide * block
                v_ref[j, :, :width] = dot_nn(w_ref[j, :, :width], gram_ref[j, :width, :width])
                for k in range(wide):
                    at = slice(k * block, (k + 1) * block)
                    v_ref[j, :, at] += w_ref[j, :, at].astype(jnp.float32) * low_ref[j, k : k + 1]


def step_and_send(here, block, scale, v_ref, next_ref, out_ref):
    @pl.loop(0, here.block_rows)
    def _(j):
        for k in range(here.slots):
            filled, own, b, holder = here.slot(j, k)
            at = slice(k * block, (k + 1) * block)

            @pl.when(own)
            def _(k=k, b=b, at=at):
                m = here.mate(b, j) if k else 0
                mirrored = v_ref[b, :, aligned(m, block)].T
                next_ref[j, k] = next_ref[j, k] - scale * (v_ref[j, :, at] + mirrored)

            @pl.when(filled & jnp.logical_not(own))
            def _(k=k, holder=holder, at=at):
                value = v_ref[j, :, at]
                next_ref[j, k] = next_ref[j, k] - scale * value
                out_ref[holder] = value.astype(out_ref.dtype).T


def first_kernel(rounds, group, ways, scale, cb_ref, prec_ref, gram_in_ref, low_in_ref, *rest):
    parts, rest = rest[: 2 * ways], rest[2 * ways :]
    gram_ref, low_ref, next_ref, out_ref, tab_ref, w_ref, v_ref = rest
    block_rows, slots, block, _ = prec_ref.shape
    here = Local(cb_ref, block_rows, rounds)
    here.fill_links(tab_ref)
    low_ref[...] = low_in_ref[...]

    @pl.loop(0, block_rows * slots)
    def _(i):
        at = (lax.div(i, slots), aligned(lax.rem(i, slots), block))
        gram_ref[at] = gram_in_ref[at]

    place_arrivals(here, *group, parts, tab_ref, gram_ref, low_ref)
    @pl.loop(0, block_rows)
    def _(j):
        for k in range(slots):
            filled = here.cb[j, k] >= 0
            value = jnp.where(filled, prec_ref[j, k], 0.0)
            next_ref[j, k] = value
            w_ref[j, :, k * block : (k + 1) * block] = value.astype(jnp.bfloat16)
    products(here, block, w_ref, gram_ref, low_ref, v_ref)
    step_and_send(here, block, scale, v_ref, next_ref, out_ref)


def prox_blocks(here, block, scale, stepped_ref, in_ref, next_ref, w_ref):
    eye = eye_of(block)

    def finish(j, k, m):
        value = m - jnp.clip(m, -SHRINK, SHRINK)
        if k == 0:
            value = jnp.where(eye, 0.5 * (m + jnp.sqrt(m * m + 4.0 * STEP)), value)
        next_ref[j, k] = value
        if w_ref is not None:
            w_ref[j, :, k * block : (k + 1) * block] = value.astype(jnp.bfloat16)

    @pl.loop(0, here.block_rows)
    def _(j):
        for k in range(here.slots):
            filled, own, _, holder = here.slot(j, k)

            @pl.when(own)
            def _(k=k):
                finish(j, k, stepped_ref[j, k])

            @pl.when(filled & jnp.logical_not(own))
            def _(k=k, holder=holder):
                finish(j, k, stepped_ref[j, k] - scale * in_ref[holder].astype(jnp.float32))

            @pl.when(jnp.logical_not(filled))
            def _(k=k):
                next_ref[j, k] = jnp.zeros((block, block), jnp.float32)
                if w_ref is not None:
                    w_ref[j, :, k * block : (k + 1) * block] = jnp.zeros((block, block), jnp.bfloat16)


def middle_kernel(scale, cb_ref, stepped_ref, in_ref, gram_ref, low_ref, next_ref, out_ref, w_ref, v_ref):
    block_rows, _, block, _ = stepped_ref.shape
    here = Local(cb_ref, block_rows, False)
    prox_blocks(here, block, scale, stepped_ref, in_ref, next_ref, w_ref)
    products(here, block, w_ref, gram_ref, low_ref, v_ref)
    step_and_send(here, block, scale, v_ref, next_ref, out_ref)


def last_kernel(scale, cb_ref, stepped_ref, in_ref, next_ref):
    block_rows, _, block, _ = stepped_ref.shape
    prox_blocks(Local(cb_ref, block_rows, False), block, scale, stepped_ref, in_ref, next_ref, None)


def call(kernel, inputs, outs, scratch, smem=1, cost=1):
    arrays = (*inputs, *outs, *scratch)
    size = sum(math.prod(x.shape) * jnp.dtype(x.dtype).itemsize for x in arrays)
    return pl.pallas_call(
        kernel,
        out_shape=outs,
        in_specs=[SMEM] * smem + [VMEM] * (len(inputs) - smem),
        out_specs=[VMEM] * len(outs),
        scratch_shapes=scratch,
        compiler_params=pltpu.CompilerParams(vmem_limit_bytes=size + (6 << 20)),
        cost_estimate=pl.CostEstimate(flops=1, bytes_accessed=cost, transcendentals=0),
    )(*inputs)


def swap(x, bit):
    count = lax.axis_size("samp")
    return lax.ppermute(x, "samp", [(i, i ^ bit) for i in range(count)])


def from_ys(x):
    return [x] + [swap(x, bit) for bit in range(2, lax.axis_size("samp"), 2)]


def both_cores(parts):
    return (*parts, *(swap(x, 1) for x in parts))


def after(x, *earlier):
    return lax.optimization_barrier((x, *earlier))[0]


def fenced(col_blocks, part, *args):
    def nothing(*args):
        return jax.tree.map(lambda x: jnp.zeros(x.shape, x.dtype), jax.eval_shape(part, *args))

    return lax.cond(col_blocks[0, 0] >= 0, part, nothing, *args)


def local(samples, precision, col_blocks):
    row_count = samples.shape[0]
    block_rows, slots, block, _ = precision.shape
    peers = lax.axis_size("feat")
    ways = lax.axis_size("samp") // 2
    scale = 0.5 * STEP / (row_count * lax.axis_size("samp"))
    rounds = peers == 8 and ways == 2
    groups = [(1, 6), (6, 8)] if rounds else [(0, peers)]

    def shape(dims, dtype):
        return jax.ShapeDtypeStruct(dims, dtype)

    bf16, f32 = samples.dtype, jnp.float32
    tab = pltpu.SMEM((2, peers), jnp.int32)
    strip = (block, row_count)
    sends = [shape(strip, bf16)] * (peers - 1) if rounds else [shape((peers, *strip), bf16)]
    own, *sends = call(
        functools.partial(pack_kernel, rounds),
        (col_blocks, samples),
        [shape((block_rows, *strip), bf16), *sends],
        [tab],
    )

    def exchange(x, r):
        return lax.ppermute(x, "feat", [(i, i ^ r) for i in range(peers)])

    grams = [
        shape((block_rows, slots * block, slots * block), bf16),
        shape((block_rows, 8, block), f32),
    ]

    def own_list(own, other):
        return call(
            own_gram_kernel,
            (own, other),
            [shape((block_rows * (block_rows + 1) // 4, block + 16, block), bf16)],
            [],
            smem=0,
        )[0]

    def arrival_list(first, last, own_pair, arrived, over):
        return call(
            functools.partial(gram_kernel, rounds, first, last),
            (col_blocks, *own_pair, *arrived, *over),
            [shape((last - first, slots // 2 * block + 16, block), bf16)],
            [tab, pltpu.VMEM((2, *strip), bf16)],
        )[0]

    def gather(*lists):
        return call(
            functools.partial(gather_kernel, rounds, groups[:-1], ways),
            (col_blocks, *sum(lists, ())),
            grams,
            [
                tab,
                pltpu.VMEM((block_rows, block_rows, block, block), bf16),
                pltpu.VMEM((8, block), f32),
            ],
        )

    def over_of(blocks, earlier):
        return [swap(after(x, earlier), 1) for x in blocks]

    if rounds:
        other = swap(own, 1)
        own_pair = (own, other)
        ready = [*sends[:2], after(sends[2], other), *sends[3:]]
        arrived = [exchange(ready[r - 1], r) for r in (1, 2, 3, 4, 5)]
        step = fenced(col_blocks, own_list, own, other)
        over = over_of(arrived, step)
        arrived += [exchange(after(sends[r - 1], arrived[r - 3]), r) for r in (6, 7)]

        def most(own_pair, arrived, over, own_list):
            own_y, own_core = swap(own_list, 2), swap(own_list, 1)
            out = after(arrival_list(1, 6, own_pair, arrived, over), own_y, own_core)
            out_y, own_both = swap(out, 2), swap(after(own_y, out), 1)
            out_core = swap(after(out, own_both), 1)
            out_both = swap(after(out_y, out_core), 1)
            return (own_list, own_y, own_core, own_both), (out, out_y, out_core, out_both)

        own_lists, lists = fenced(col_blocks, most, own_pair, arrived[:5], over, step)
        over += over_of(arrived[5:], lists[0])
        step = arrival_list(6, 8, own_pair, arrived, over)
        gram, low = fenced(col_blocks, gather, own_lists, after(lists, step))
        last_list = both_cores([step, after(from_ys(step)[1], gram)])
    else:
        other = swap(own, 1)
        arrived = lax.all_to_all(sends[0], "feat", 0, 0, tiled=True)
        gram, low = gather(both_cores(from_ys(own_list(own, other))))
        last_list = both_cores(
            from_ys(arrival_list(0, peers, (own, other), [arrived], [swap(arrived, 1)]))
        )
    blocks = shape(precision.shape, f32)
    swapped = shape((peers, block, block), bf16)
    work = [
        pltpu.VMEM((block_rows, block, slots * block), bf16),
        pltpu.VMEM((block_rows, block, slots * block), f32),
    ]
    gram, low, stepped, out = call(
        functools.partial(first_kernel, rounds, groups[-1], ways, scale),
        (col_blocks, precision, gram, low, *last_list),
        [*grams, blocks, swapped],
        [tab, *work],
    )
    for iteration in range(ITERS):
        mirrored = lax.all_to_all(out, "feat", 0, 0, tiled=True)
        if iteration + 1 < ITERS:
            stepped, out = call(
                functools.partial(middle_kernel, scale),
                (col_blocks, stepped, mirrored, gram, low),
                [blocks, swapped],
                work,
            )
    (updated,) = call(functools.partial(last_kernel, scale), (col_blocks, stepped, mirrored), [blocks], [])
    return updated


def solution(mesh):
    return jax.shard_map(
        local,
        mesh=mesh,
        in_specs=(P("samp", "feat"), P("feat", None, None, None), P("feat", None)),
        out_specs=P("feat", None, None, None),
        check_vma=False,
    )
```

```python
import functools
import math

import jax
import jax.numpy as jnp
from jax import lax
from jax.experimental import pallas as pl
from jax.experimental.pallas import tpu as pltpu
from jax.sharding import PartitionSpec as P

ITERS = 3
STEP = 0.2
SHRINK = 0.05

SMEM = pl.BlockSpec(memory_space=pltpu.SMEM)
VMEM = pl.BlockSpec(memory_space=pltpu.VMEM)


def dot_nt(a, b):
    return lax.dot_general(a, b, (((1,), (1,)), ((), ())), preferred_element_type=jnp.float32)


def dot_nn(a, b):
    return lax.dot_general(a, b, (((1,), (0,)), ((), ())), preferred_element_type=jnp.float32)


class Pattern:
    def __init__(self, table, block_rows, slots):
        self.table = table
        self.block_rows = block_rows
        self.slots = slots

    def link(self, place):
        return self.table[0, place], self.table[1, place]

    def sent(self, peer):
        return self.table[2, peer], self.table[3, peer]

    def source(self, j, k):
        return self.table[4, j * self.slots + k]

    def peer(self, j, k):
        return self.table[5, j * self.slots + k]

    def mate(self, j, k):
        return self.table[6, j * self.slots + k], self.table[7, j * self.slots + k]

    def known(self, source, place):
        return (source >= 0) & (source - self.block_rows <= place)


def find(cb_ref, block_rows, rounds, c):
    me = lax.axis_index("feat")
    safe = jnp.maximum(c, 0)
    holder = lax.div(safe, block_rows)
    place = lax.bitwise_xor(holder, me) if rounds else holder
    return c >= 0, (c >= 0) & (holder == me), lax.rem(safe, block_rows), holder, place


def pattern_kernel(rounds, peers, cb_ref, table_ref):
    block_rows, slots = cb_ref.shape
    me = lax.axis_index("feat")
    for p in range(peers):
        table_ref[0, p] = -1
        table_ref[1, p] = -1
        table_ref[2, p] = 0
        table_ref[3, p] = slots

    @pl.loop(0, block_rows)
    def _(j):
        for k in range(slots):
            filled, own, b, holder, place = find(cb_ref, block_rows, rounds, cb_ref[j, k])
            m = jnp.int32(0)
            for other in range(1, slots):
                m = jnp.where(cb_ref[b, other] == me * block_rows + j, other, m)
            i = j * slots + k
            table_ref[4, i] = jnp.where(filled, jnp.where(own, b, block_rows + place), -1)
            table_ref[5, i] = jnp.where(filled & jnp.logical_not(own), holder, me)
            table_ref[6, i] = jnp.where(own, b, 0)
            table_ref[7, i] = jnp.where(own, m, slots)

            @pl.when(filled & jnp.logical_not(own))
            def _(k=k, holder=holder, place=place):
                table_ref[0, place] = j
                table_ref[1, place] = k
                table_ref[2, holder] = j
                table_ref[3, holder] = k


def aligned(index, block):
    return pl.ds(pl.multiple_of(index * block, block), block)


def span(k, block):
    return slice(k * block, (k + 1) * block)


def pack_kernel(rounds, cb_ref, x_ref, own_ref, *rest):
    *send_refs, row_ref = rest
    block_rows, block, _ = own_ref.shape
    peers = row_ref.shape[0]
    for p in range(peers):
        row_ref[p] = 0

    @pl.loop(0, block_rows)
    def _(j):
        for k in range(1, cb_ref.shape[1]):
            filled, own, _, _, place = find(cb_ref, block_rows, rounds, cb_ref[j, k])

            @pl.when(filled & jnp.logical_not(own))
            def _(place=place):
                row_ref[place] = j

    for b in range(block_rows):
        own_ref[b] = x_ref[:, span(b, block)].T
    if rounds:
        for r, send_ref in enumerate(send_refs, 1):
            send_ref[...] = own_ref[row_ref[r]]
    else:
        (send_ref,) = send_refs

        @pl.loop(0, peers)
        def _(p):
            send_ref[p] = own_ref[row_ref[p]]


def eye_of(block):
    return lax.broadcasted_iota(jnp.int32, (block, block), 0) == lax.broadcasted_iota(
        jnp.int32, (block, block), 1
    )


def low_diagonal(value, high):
    rest = value - high.astype(jnp.float32)
    return jnp.sum(jnp.where(eye_of(value.shape[0]), rest, 0.0), axis=0, keepdims=True)


def put_low(out_ref, i, value, high):
    low = jnp.broadcast_to(low_diagonal(value, high), (16, value.shape[1]))
    out_ref[i, out_ref.shape[1] - 16 :] = low.astype(jnp.bfloat16)


def own_pairs(block_rows):
    pairs = [(a, b) for a in range(block_rows) for b in range(a, block_rows)]
    return list(zip(pairs[::2], pairs[1::2]))


def own_gram_kernel(mine_ref, other_ref, out_ref):
    core = lax.rem(lax.axis_index("samp"), 2)
    block = mine_ref.shape[1]
    for i, ((a, b), (c, d)) in enumerate(own_pairs(mine_ref.shape[0])):
        x, y = jnp.where(core == 0, a, c), jnp.where(core == 0, b, d)
        value = dot_nt(mine_ref[x], mine_ref[y]) + dot_nt(other_ref[x], other_ref[y])
        high = value.astype(jnp.bfloat16)
        out_ref[i, :block] = high
        put_low(out_ref, i, value, high)


def slot_at(k, position):
    return k if position == 0 else jnp.where(k == position, 0, position)


def gram_kernel(rounds, first, last, table_ref, mine_ref, other_ref, *rest):
    *arrived_refs, out_ref, beside_ref = rest
    block_rows, block, samples = mine_ref.shape
    slots = 2 * (beside_ref.shape[1] // block)
    core = lax.rem(lax.axis_index("samp"), 2)
    here = Pattern(table_ref, block_rows, slots)
    count = len(arrived_refs) // 2

    def arrival(q):
        if rounds:
            return arrived_refs[q - 1][...], arrived_refs[count + q - 1][...]
        return arrived_refs[0][q], arrived_refs[1][q]

    def body(p):
        row, k = here.link(p)

        @pl.when(row >= 0)
        def _():
            for i in range(slots // 2):
                l = jnp.where(core == 0, slot_at(k, 2 * i), slot_at(k, 2 * i + 1))
                source = here.source(row, l)
                at = span(i, block)
                near = jnp.clip(source, 0, block_rows - 1)
                beside_ref[0, at] = mine_ref[near]
                beside_ref[1, at] = other_ref[near]

                def from_arrival(q, at=at, source=source):
                    @pl.when(source == block_rows + q)
                    def _():
                        beside_ref[0, at], beside_ref[1, at] = arrival(q)

                if rounds:
                    for q in range(1, p + 1):
                        from_arrival(q)
                else:

                    @pl.when((source >= block_rows) & (source <= block_rows + p))
                    def _(at=at, source=source):
                        beside_ref[0, at], beside_ref[1, at] = arrival(source - block_rows)

            mine, other = arrival(p)
            value = dot_nt(beside_ref[0], mine) + dot_nt(beside_ref[1], other)
            high = value.astype(jnp.bfloat16)
            out_ref[p - first, : slots // 2 * block] = high
            put_low(out_ref, p - first, value[:block], high[:block])

    if rounds:
        for p in range(first, last):
            body(p)
    else:
        pl.loop(first, last)(body)


def read_part(parts, mine, index):
    half = len(parts) // 2
    terms = [
        jnp.where(mine, a[index], b[index]).astype(jnp.float32)
        for a, b in zip(parts[:half], parts[half:])
    ]
    while len(terms) > 1:
        terms = [a + b for a, b in zip(terms[::2], terms[1::2])]
    return terms[0]


def place_arrivals(here, first, last, parts, gram_ref, low_ref):
    block = parts[0].shape[2]
    slots = here.slots
    core = lax.rem(lax.axis_index("samp"), 2)

    @pl.loop(first, last)
    def _(p):
        row, k = here.link(p)

        @pl.when(row >= 0)
        def _():
            i = p - first
            for position in range(slots):
                l = slot_at(k, position)
                mine = core == position % 2
                value = read_part(parts, mine, (i, span(position // 2, block)))
                value = jnp.where(here.known(here.source(row, l), p), value, 0.0)
                high = value.astype(jnp.bfloat16)
                gram_ref[row, aligned(l, block), aligned(k, block)] = high
                if position:
                    gram_ref[row, aligned(k, block), aligned(l, block)] = high.T
                else:
                    lows = read_part(parts, mine, (i, pl.ds(slots // 2 * block, 1)))
                    low_ref[row, pl.ds(k, 1)] = low_diagonal(value, high) + lows


def gather_own_kernel(slots, table_ref, *rest):
    *parts, gram_ref, low_ref, sum_ref, row_ref = rest
    block_rows = gram_ref.shape[0]
    block = parts[0].shape[2]
    core = lax.rem(lax.axis_index("samp"), 2)
    here = Pattern(table_ref, block_rows, slots)
    sum_ref[block_rows] = jnp.zeros(sum_ref.shape[1:], sum_ref.dtype)
    row_ref[...] = jnp.zeros(row_ref.shape, row_ref.dtype)
    low_ref[...] = jnp.zeros(low_ref.shape, low_ref.dtype)
    for a in range(block_rows):
        sum_ref[a, block_rows] = jnp.zeros((block, block), sum_ref.dtype)
    for i, two in enumerate(own_pairs(block_rows)):
        for maker, (a, b) in enumerate(two):
            value = read_part(parts, core == maker, (i, slice(0, block)))
            high = value.astype(jnp.bfloat16)
            sum_ref[a, b] = high
            if a == b:
                lows = read_part(parts, core == maker, (i, slice(block, block + 1)))
                row_ref[a : a + 1] = low_diagonal(value, high) + lows
            else:
                sum_ref[b, a] = high.T

    @pl.loop(0, block_rows)
    def _(j):
        sources = [here.source(j, k) for k in range(slots)]
        rows = [
            jnp.where((x >= 0) & (x < block_rows), x, block_rows) for x in sources
        ]
        for k, a in enumerate(rows):
            low_ref[j, k : k + 1] = row_ref[pl.ds(a, 1)]
            for l, b in enumerate(rows):
                gram_ref[j, span(k, block), span(l, block)] = sum_ref[a, b]


def gather_kernel(groups, ways, slots, table_ref, gram_in_ref, low_in_ref, *rest):
    *parts, gram_ref, low_ref, sem = rest
    copy = pltpu.make_async_copy(gram_in_ref, gram_ref, sem)
    copy.start()
    low_ref[...] = low_in_ref[...]
    here = Pattern(table_ref, gram_ref.shape[0], slots)
    copy.wait()
    for g, (first, last) in enumerate(groups):
        at = slice(2 * ways * g, 2 * ways * (g + 1))
        place_arrivals(here, first, last, parts[at], gram_ref, low_ref)


def multiply_and_step(here, scale, w_ref, gram_ref, low_ref, v_ref, next_ref, out_ref):
    block_rows, slots, block, _ = next_ref.shape
    v_ref[:, :, slots * block :] = jnp.zeros((block_rows, block, block), jnp.float32)

    @pl.loop(0, block_rows)
    def _(j):
        value = dot_nn(w_ref[j], gram_ref[j])
        for k in range(slots):
            at = span(k, block)
            low = w_ref[j, :, at].astype(jnp.float32) * low_ref[j, k : k + 1]
            v_ref[j, :, at] = value[:, at] + low

    for p in range(out_ref.shape[0]) if out_ref.shape[0] <= 8 else ():
        row, column = here.sent(p)
        out_ref[p] = v_ref[row, :, aligned(column, block)].astype(out_ref.dtype).T
    if out_ref.shape[0] > 8:

        @pl.loop(0, out_ref.shape[0])
        def _(p):
            row, column = here.sent(p)
            out_ref[p] = v_ref[row, :, aligned(column, block)].astype(out_ref.dtype).T

    @pl.loop(0, block_rows)
    def _(j):
        for k in range(slots):
            row, column = here.mate(j, k)
            mirrored = v_ref[row, :, aligned(column, block)].T
            next_ref[j, k] = next_ref[j, k] - scale * (v_ref[j, :, span(k, block)] + mirrored)


def first_kernel(group, ways, scale, table_ref, prec_ref, gram_in_ref, low_in_ref, *rest):
    parts, rest = rest[: 2 * ways], rest[2 * ways :]
    gram_ref, low_ref, next_ref, out_ref, w_ref, v_ref, sem = rest
    copy = pltpu.make_async_copy(gram_in_ref, gram_ref, sem)
    copy.start()
    low_ref[...] = low_in_ref[...]
    block_rows, slots, block, _ = prec_ref.shape
    here = Pattern(table_ref, block_rows, slots)

    @pl.loop(0, block_rows)
    def _(j):
        for k in range(slots):
            value = jnp.where(here.source(j, k) >= 0, prec_ref[j, k], 0.0)
            next_ref[j, k] = value
            w_ref[j, :, span(k, block)] = value.astype(jnp.bfloat16)

    copy.wait()
    place_arrivals(here, *group, parts, gram_ref, low_ref)
    multiply_and_step(here, scale, w_ref, gram_ref, low_ref, v_ref, next_ref, out_ref)


def soft(m):
    return m - jnp.clip(m, -SHRINK, SHRINK)


def next_omega(here, j, scale, stepped_ref, in_ref, put):
    block = stepped_ref.shape[2]
    for k in range(here.slots):
        m = stepped_ref[j, k]
        if k == 0:
            root = 0.5 * (m + jnp.sqrt(m * m + 4.0 * STEP))
            put(k, jnp.where(eye_of(block), root, soft(m)))
        else:
            arrived = in_ref[here.peer(j, k)].astype(jnp.float32)
            put(k, soft(m - scale * arrived))


def middle_kernel(scale, table_ref, stepped_ref, in_ref, gram_ref, low_ref, next_ref, out_ref, w_ref, v_ref):
    block_rows, slots, block, _ = stepped_ref.shape
    here = Pattern(table_ref, block_rows, slots)

    @pl.loop(0, block_rows)
    def _(j):
        def put(k, value):
            next_ref[j, k] = value
            w_ref[j, :, span(k, block)] = value.astype(jnp.bfloat16)

        next_omega(here, j, scale, stepped_ref, in_ref, put)

    multiply_and_step(here, scale, w_ref, gram_ref, low_ref, v_ref, next_ref, out_ref)


def last_kernel(scale, table_ref, stepped_ref, in_ref, next_ref):
    block_rows, slots, block, _ = stepped_ref.shape
    here = Pattern(table_ref, block_rows, slots)

    @pl.loop(0, block_rows)
    def _(j):
        def put(k, value):
            next_ref[j, k] = value

        next_omega(here, j, scale, stepped_ref, in_ref, put)


def call(kernel, inputs, outs, scratch, smem=1, left=(), sems=(), out_space=VMEM):
    arrays = (*inputs, *outs, *scratch)
    size = sum(math.prod(x.shape) * jnp.dtype(x.dtype).itemsize for x in arrays)
    specs = [SMEM] * smem + [VMEM] * (len(inputs) - smem)
    for i in left:
        specs[i] = pl.BlockSpec(memory_space=pl.ANY)
    return pl.pallas_call(
        kernel,
        out_shape=outs,
        in_specs=specs,
        out_specs=[out_space] * len(outs),
        scratch_shapes=[*scratch, *sems],
        compiler_params=pltpu.CompilerParams(vmem_limit_bytes=size + (6 << 20)),
        cost_estimate=pl.CostEstimate(flops=1, bytes_accessed=1, transcendentals=0),
    )(*inputs)


def swap(x, bit):
    count = lax.axis_size("samp")
    return lax.ppermute(x, "samp", [(i, i ^ bit) for i in range(count)])


def from_ys(x):
    return [x] + [swap(x, bit) for bit in range(2, lax.axis_size("samp"), 2)]


def both_cores(parts):
    return (*parts, *(swap(x, 1) for x in parts))


def after(x, *earlier):
    return lax.optimization_barrier((x, *earlier))[0]


def fenced(col_blocks, part, *args):
    def nothing(*args):
        return jax.tree.map(lambda x: jnp.zeros(x.shape, x.dtype), jax.eval_shape(part, *args))

    return lax.cond(col_blocks[0, 0] >= 0, part, nothing, *args)


def local(samples, precision, col_blocks):
    row_count = samples.shape[0]
    block_rows, slots, block, _ = precision.shape
    peers = lax.axis_size("feat")
    ways = lax.axis_size("samp") // 2
    scale = 0.5 * STEP / (row_count * lax.axis_size("samp"))
    rounds = peers == 8 and ways == 2
    groups = [(1, 6), (6, 8)] if rounds else [(0, peers)]

    def shape(dims, dtype):
        return jax.ShapeDtypeStruct(dims, dtype)

    bf16, f32 = samples.dtype, jnp.float32
    strip = (block, row_count)
    sem = pltpu.SemaphoreType.DMA(())
    sends = [shape(strip, bf16)] * (peers - 1) if rounds else [shape((peers, *strip), bf16)]
    own, *sends = call(
        functools.partial(pack_kernel, rounds),
        (col_blocks, samples),
        [shape((block_rows, *strip), bf16), *sends],
        [pltpu.SMEM((peers,), jnp.int32)],
    )

    def exchange(x, r):
        return lax.ppermute(x, "feat", [(i, i ^ r) for i in range(peers)])

    grams = [
        shape((block_rows, slots * block, slots * block), bf16),
        shape((block_rows, 8, block), f32),
    ]

    def pattern():
        width = max(peers, block_rows * slots)
        return call(
            functools.partial(pattern_kernel, rounds, peers),
            (col_blocks,),
            [shape((8, width), jnp.int32)],
            [],
            out_space=SMEM,
        )[0]

    def own_list(own, other):
        return call(
            own_gram_kernel,
            (own, other),
            [shape((block_rows * (block_rows + 1) // 4, block + 16, block), bf16)],
            [],
            smem=0,
        )[0]

    def arrival_list(first, last, table, own_pair, arrived, over):
        return call(
            functools.partial(gram_kernel, rounds, first, last),
            (table, *own_pair, *arrived, *over),
            [shape((last - first, slots // 2 * block + 16, block), bf16)],
            [pltpu.VMEM((2, slots // 2 * block, row_count), bf16)],
        )[0]

    def gather_own(table, *parts):
        return call(
            functools.partial(gather_own_kernel, slots),
            (table, *parts),
            grams,
            [
                pltpu.VMEM((block_rows + 1, block_rows + 1, block, block), bf16),
                pltpu.VMEM((8, block), f32),
            ],
        )

    def gather(table, gram, low, *lists):
        return call(
            functools.partial(gather_kernel, groups[:-1], ways, slots),
            (table, gram, low, *sum(lists, ())),
            grams,
            [],
            left=[1],
            sems=[sem],
        )

    def over_of(blocks, earlier):
        return [swap(after(x, earlier), 1) for x in blocks]

    if rounds:
        other = swap(own, 1)
        own_pair = (own, other)
        ready = [*sends[:2], after(sends[2], other), *sends[3:]]
        arrived = [exchange(ready[r - 1], r) for r in (1, 2, 3, 4, 5)]

        def begin(own, other):
            return own_list(own, other), pattern()

        step, table = fenced(col_blocks, begin, own, other)
        over = over_of(arrived, step)
        arrived += [exchange(after(sends[r - 1], arrived[r - 3]), r) for r in (6, 7)]

        def own_part(table, own_list, own_y):
            return gather_own(table, own_list, own_y, swap(own_list, 1), swap(own_y, 1))

        def most(table, own_pair, arrived, over, own_list):
            own_y = swap(own_list, 2)
            out = after(arrival_list(1, 6, table, own_pair, arrived, over), own_y)
            out_y, own_y = swap(out, 2), after(own_y, out)
            gram, low = fenced(col_blocks, own_part, table, own_list, own_y)
            out_core = swap(after(out, gram), 1)
            out_both = swap(after(out_y, gram), 1)
            return gram, low, (out, out_y, out_core, out_both)

        gram, low, *lists = fenced(col_blocks, most, table, own_pair, arrived[:5], over, step)
        over += over_of(arrived[5:], gram)
        step = arrival_list(6, 8, table, own_pair, arrived, over)
        gram, low = gather(table, after(gram, step), low, *lists)
        last_list = both_cores([step, after(from_ys(step)[1], gram)])
    else:
        other = swap(own, 1)
        table = pattern()
        arrived = lax.all_to_all(sends[0], "feat", 0, 0, tiled=True)
        gram, low = gather_own(table, *both_cores(from_ys(own_list(own, other))))
        last_list = both_cores(
            from_ys(arrival_list(0, peers, table, (own, other), [arrived], [swap(arrived, 1)]))
        )
    blocks = shape(precision.shape, f32)
    swapped = shape((peers, block, block), bf16)
    work = [
        pltpu.VMEM((block_rows, block, slots * block), bf16),
        pltpu.VMEM((block_rows, block, (slots + 1) * block), f32),
    ]
    gram, low, stepped, out = call(
        functools.partial(first_kernel, groups[-1], ways, scale),
        (table, precision, gram, low, *last_list),
        [*grams, blocks, swapped],
        work,
        left=[2],
        sems=[sem],
    )
    for iteration in range(ITERS):
        mirrored = lax.all_to_all(out, "feat", 0, 0, tiled=True)
        if iteration + 1 < ITERS:
            stepped, out = call(
                functools.partial(middle_kernel, scale),
                (table, stepped, mirrored, gram, low),
                [blocks, swapped],
                work,
            )
    (updated,) = call(functools.partial(last_kernel, scale), (table, stepped, mirrored), [blocks], [])
    return updated


def solution(mesh):
    return jax.shard_map(
        local,
        mesh=mesh,
        in_specs=(P("samp", "feat"), P("feat", None, None, None), P("feat", None)),
        out_specs=P("feat", None, None, None),
        check_vma=False,
    )
```

```python
import functools
import math

import jax
import jax.numpy as jnp
from jax import lax
from jax.experimental import pallas as pl
from jax.experimental.pallas import tpu as pltpu
from jax.sharding import PartitionSpec as P

ITERS = 3
STEP = 0.2
TURNS = ((2, 7), (3, 5), (2, 6), (1, 4))
SHRINK = 0.05

SMEM = pl.BlockSpec(memory_space=pltpu.SMEM)
VMEM = pl.BlockSpec(memory_space=pltpu.VMEM)


def dot_nt(a, b):
    return lax.dot_general(a, b, (((1,), (1,)), ((), ())), preferred_element_type=jnp.float32)


def dot_nn(a, b):
    return lax.dot_general(a, b, (((1,), (0,)), ((), ())), preferred_element_type=jnp.float32)


class Pattern:
    def __init__(self, table, block_rows, slots):
        self.table = table
        self.block_rows = block_rows
        self.slots = slots

    def link(self, place):
        return self.table[0, place], self.table[1, place]

    def sent(self, peer):
        return self.table[2, peer], self.table[3, peer]

    def source(self, j, k):
        return self.table[4, j * self.slots + k]

    def peer(self, j, k):
        return self.table[5, j * self.slots + k]

    def mate(self, j, k):
        return self.table[6, j * self.slots + k], self.table[7, j * self.slots + k]

    def known(self, source, place):
        return (source >= 0) & (source - self.block_rows <= place)


def find(cb_ref, block_rows, rounds, c):
    me = lax.axis_index("feat")
    safe = jnp.maximum(c, 0)
    holder = lax.div(safe, block_rows)
    place = lax.bitwise_xor(holder, me) if rounds else holder
    return c >= 0, (c >= 0) & (holder == me), lax.rem(safe, block_rows), holder, place


def pattern_kernel(rounds, peers, cb_ref, table_ref):
    block_rows, slots = cb_ref.shape
    me = lax.axis_index("feat")
    for p in range(peers):
        table_ref[0, p] = -1
        table_ref[1, p] = -1
        table_ref[2, p] = 0
        table_ref[3, p] = slots

    @pl.loop(0, block_rows)
    def _(j):
        for k in range(slots):
            filled, own, b, holder, place = find(cb_ref, block_rows, rounds, cb_ref[j, k])
            m = jnp.int32(0)
            for other in range(1, slots):
                m = jnp.where(cb_ref[b, other] == me * block_rows + j, other, m)
            i = j * slots + k
            table_ref[4, i] = jnp.where(filled, jnp.where(own, b, block_rows + place), -1)
            peer, nobody = (place, 0) if rounds else (holder, me)
            table_ref[5, i] = jnp.where(filled & jnp.logical_not(own), peer, nobody)
            table_ref[6, i] = jnp.where(own, b, 0)
            table_ref[7, i] = jnp.where(own, m, slots)

            @pl.when(filled & jnp.logical_not(own))
            def _(k=k, peer=peer, place=place):
                table_ref[0, place] = j
                table_ref[1, place] = k
                table_ref[2, peer] = j
                table_ref[3, peer] = k


def aligned(index, block):
    return pl.ds(pl.multiple_of(index * block, block), block)


def span(k, block):
    return slice(k * block, (k + 1) * block)


def pack_kernel(rounds, cb_ref, x_ref, own_ref, *rest):
    *send_refs, row_ref = rest
    block_rows, block, _ = own_ref.shape
    peers = row_ref.shape[0]
    for p in range(peers):
        row_ref[p] = 0

    @pl.loop(0, block_rows)
    def _(j):
        for k in range(1, cb_ref.shape[1]):
            filled, own, _, _, place = find(cb_ref, block_rows, rounds, cb_ref[j, k])

            @pl.when(filled & jnp.logical_not(own))
            def _(place=place):
                row_ref[place] = j

    for b in range(block_rows):
        own_ref[b] = x_ref[:, span(b, block)].T
    if rounds:
        for r, send_ref in enumerate(send_refs, 1):
            send_ref[...] = own_ref[row_ref[r]]
    else:
        (send_ref,) = send_refs

        @pl.loop(0, peers)
        def _(p):
            send_ref[p] = own_ref[row_ref[p]]


def eye_of(block):
    return lax.broadcasted_iota(jnp.int32, (block, block), 0) == lax.broadcasted_iota(
        jnp.int32, (block, block), 1
    )


def low_diagonal(value, high):
    rest = value - high.astype(jnp.float32)
    return jnp.sum(jnp.where(eye_of(value.shape[0]), rest, 0.0), axis=0, keepdims=True)


def put_low(out_ref, i, value, high):
    low = jnp.broadcast_to(low_diagonal(value, high), (16, value.shape[1]))
    out_ref[i, out_ref.shape[1] - 16 :] = low.astype(jnp.bfloat16)


def own_pairs(block_rows):
    pairs = [(a, b) for a in range(block_rows) for b in range(a, block_rows)]
    return list(zip(pairs[::2], pairs[1::2]))


def own_gram_kernel(mine_ref, other_ref, out_ref):
    core = lax.rem(lax.axis_index("samp"), 2)
    block = mine_ref.shape[1]
    for i, ((a, b), (c, d)) in enumerate(own_pairs(mine_ref.shape[0])):
        x, y = jnp.where(core == 0, a, c), jnp.where(core == 0, b, d)
        value = dot_nt(mine_ref[x], mine_ref[y]) + dot_nt(other_ref[x], other_ref[y])
        high = value.astype(jnp.bfloat16)
        out_ref[i, :block] = high
        put_low(out_ref, i, value, high)


def slot_at(k, position):
    return k if position == 0 else jnp.where(k == position, 0, position)


def gram_kernel(rounds, first, last, table_ref, mine_ref, other_ref, *rest):
    *arrived_refs, out_ref, beside_ref = rest
    block_rows, block, samples = mine_ref.shape
    slots = 2 * (beside_ref.shape[1] // block)
    core = lax.rem(lax.axis_index("samp"), 2)
    here = Pattern(table_ref, block_rows, slots)
    count = len(arrived_refs) // 2

    def arrival(q):
        if rounds:
            return arrived_refs[q - 1][...], arrived_refs[count + q - 1][...]
        return arrived_refs[0][q], arrived_refs[1][q]

    def body(p):
        row, k = here.link(p)

        @pl.when(row >= 0)
        def _():
            for i in range(slots // 2):
                l = jnp.where(core == 0, slot_at(k, 2 * i), slot_at(k, 2 * i + 1))
                source = here.source(row, l)
                at = span(i, block)
                near = jnp.clip(source, 0, block_rows - 1)
                beside_ref[0, at] = mine_ref[near]
                beside_ref[1, at] = other_ref[near]

                def from_arrival(q, at=at, source=source):
                    @pl.when(source == block_rows + q)
                    def _():
                        beside_ref[0, at], beside_ref[1, at] = arrival(q)

                if rounds:
                    for q in range(1, p + 1):
                        from_arrival(q)
                else:

                    @pl.when((source >= block_rows) & (source <= block_rows + p))
                    def _(at=at, source=source):
                        beside_ref[0, at], beside_ref[1, at] = arrival(source - block_rows)

            mine, other = arrival(p)
            value = dot_nt(beside_ref[0], mine) + dot_nt(beside_ref[1], other)
            high = value.astype(jnp.bfloat16)
            out_ref[p - first, : slots // 2 * block] = high
            put_low(out_ref, p - first, value[:block], high[:block])

    if rounds:
        for p in range(first, last):
            body(p)
    else:
        pl.loop(first, last)(body)


def read_part(parts, mine, index):
    half = len(parts) // 2
    terms = [
        jnp.where(mine, a[index], b[index]).astype(jnp.float32)
        for a, b in zip(parts[:half], parts[half:])
    ]
    while len(terms) > 1:
        terms = [a + b for a, b in zip(terms[::2], terms[1::2])]
    return terms[0]


def place_arrivals(here, first, last, parts, gram_ref, low_ref):
    block = parts[0].shape[2]
    slots = here.slots
    core = lax.rem(lax.axis_index("samp"), 2)

    @pl.loop(first, last)
    def _(p):
        row, k = here.link(p)

        @pl.when(row >= 0)
        def _():
            i = p - first
            for position in range(slots):
                l = slot_at(k, position)
                mine = core == position % 2
                value = read_part(parts, mine, (i, span(position // 2, block)))
                value = jnp.where(here.known(here.source(row, l), p), value, 0.0)
                high = value.astype(jnp.bfloat16)
                gram_ref[row, aligned(l, block), aligned(k, block)] = high
                if position:
                    gram_ref[row, aligned(k, block), aligned(l, block)] = high.T
                else:
                    lows = read_part(parts, mine, (i, pl.ds(slots // 2 * block, 1)))
                    low_ref[row, pl.ds(k, 1)] = low_diagonal(value, high) + lows


def gather_own_kernel(slots, table_ref, *rest):
    *parts, gram_ref, low_ref, sum_ref, row_ref = rest
    block_rows = gram_ref.shape[0]
    block = parts[0].shape[2]
    core = lax.rem(lax.axis_index("samp"), 2)
    here = Pattern(table_ref, block_rows, slots)
    sum_ref[block_rows] = jnp.zeros(sum_ref.shape[1:], sum_ref.dtype)
    row_ref[...] = jnp.zeros(row_ref.shape, row_ref.dtype)
    low_ref[...] = jnp.zeros(low_ref.shape, low_ref.dtype)
    for a in range(block_rows):
        sum_ref[a, block_rows] = jnp.zeros((block, block), sum_ref.dtype)
    for i, two in enumerate(own_pairs(block_rows)):
        for maker, (a, b) in enumerate(two):
            value = read_part(parts, core == maker, (i, slice(0, block)))
            high = value.astype(jnp.bfloat16)
            sum_ref[a, b] = high
            if a == b:
                lows = read_part(parts, core == maker, (i, slice(block, block + 1)))
                row_ref[a : a + 1] = low_diagonal(value, high) + lows
            else:
                sum_ref[b, a] = high.T

    @pl.loop(0, block_rows)
    def _(j):
        sources = [here.source(j, k) for k in range(slots)]
        rows = [
            jnp.where((x >= 0) & (x < block_rows), x, block_rows) for x in sources
        ]
        for k, a in enumerate(rows):
            low_ref[j, k : k + 1] = row_ref[pl.ds(a, 1)]
            for l, b in enumerate(rows):
                gram_ref[j, span(k, block), span(l, block)] = sum_ref[a, b]


def gather_kernel(groups, ways, slots, table_ref, gram_in_ref, low_in_ref, *rest):
    *parts, gram_ref, low_ref, sem = rest
    copy = pltpu.make_async_copy(gram_in_ref, gram_ref, sem)
    copy.start()
    low_ref[...] = low_in_ref[...]
    here = Pattern(table_ref, gram_ref.shape[0], slots)
    copy.wait()
    for g, (first, last) in enumerate(groups):
        at = slice(2 * ways * g, 2 * ways * (g + 1))
        place_arrivals(here, first, last, parts[at], gram_ref, low_ref)


def send(here, v_ref, out_refs):
    block = v_ref.shape[1]

    def put(out_ref, index, peer):
        row, column = here.sent(peer)
        out_ref[index] = v_ref[row, :, aligned(column, block)].astype(out_ref.dtype).T

    if len(out_refs) > 1:
        core = lax.rem(lax.axis_index("samp"), 2)
        for out_ref, (a, b) in zip(out_refs, TURNS):
            put(out_ref, ..., jnp.where(core == 0, a, b))
    else:

        @pl.loop(0, out_refs[0].shape[0])
        def _(p):
            put(out_refs[0], p, p)


def receive(in_refs, all_ref):
    core = lax.rem(lax.axis_index("samp"), 2)
    mine_ref, other_ref = in_refs
    for turn, (a, b) in enumerate(TURNS):
        mine, other = mine_ref[turn], other_ref[turn]
        all_ref[a] = jnp.where(core == 0, mine, other)
        all_ref[b] = jnp.where(core == 0, other, mine)
    all_ref[0] = jnp.zeros(all_ref.shape[1:], all_ref.dtype)


def multiply_and_step(here, scale, w_ref, gram_ref, low_ref, v_ref, next_ref, out_refs):
    block_rows, slots, block, _ = next_ref.shape
    v_ref[:, :, slots * block :] = jnp.zeros((block_rows, block, block), jnp.float32)

    @pl.loop(0, block_rows)
    def _(j):
        value = dot_nn(w_ref[j], gram_ref[j])
        for k in range(slots):
            at = span(k, block)
            low = w_ref[j, :, at].astype(jnp.float32) * low_ref[j, k : k + 1]
            v_ref[j, :, at] = value[:, at] + low

    send(here, v_ref, out_refs)

    @pl.loop(0, block_rows)
    def _(j):
        for k in range(slots):
            row, column = here.mate(j, k)
            mirrored = v_ref[row, :, aligned(column, block)].T
            next_ref[j, k] = next_ref[j, k] - scale * (v_ref[j, :, span(k, block)] + mirrored)


def first_kernel(group, ways, scale, table_ref, prec_ref, gram_in_ref, low_in_ref, *rest):
    parts, rest = rest[: 2 * ways], rest[2 * ways :]
    gram_ref, low_ref, next_ref, *out_refs, w_ref, v_ref, sem = rest
    copy = pltpu.make_async_copy(gram_in_ref, gram_ref, sem)
    copy.start()
    low_ref[...] = low_in_ref[...]
    block_rows, slots, block, _ = prec_ref.shape
    here = Pattern(table_ref, block_rows, slots)

    @pl.loop(0, block_rows)
    def _(j):
        for k in range(slots):
            value = jnp.where(here.source(j, k) >= 0, prec_ref[j, k], 0.0)
            next_ref[j, k] = value
            w_ref[j, :, span(k, block)] = value.astype(jnp.bfloat16)

    copy.wait()
    place_arrivals(here, *group, parts, gram_ref, low_ref)
    multiply_and_step(here, scale, w_ref, gram_ref, low_ref, v_ref, next_ref, out_refs)


def soft(m):
    return m - jnp.clip(m, -SHRINK, SHRINK)


def next_omega(here, j, scale, stepped_ref, in_ref, put):
    block = stepped_ref.shape[2]
    for k in range(here.slots):
        m = stepped_ref[j, k]
        if k == 0:
            root = 0.5 * (m + jnp.sqrt(m * m + 4.0 * STEP))
            put(k, jnp.where(eye_of(block), root, soft(m)))
        else:
            arrived = in_ref[here.peer(j, k)].astype(jnp.float32)
            put(k, soft(m - scale * arrived))


def middle_kernel(count, scale, table_ref, stepped_ref, *rest):
    in_refs, rest = rest[:count], rest[count:]
    gram_ref, low_ref, next_ref, *out_refs, w_ref, v_ref, all_ref = rest
    block_rows, slots, block, _ = stepped_ref.shape
    here = Pattern(table_ref, block_rows, slots)
    if count > 1:
        receive(in_refs, all_ref)

    @pl.loop(0, block_rows)
    def _(j):
        def put(k, value):
            next_ref[j, k] = value
            w_ref[j, :, span(k, block)] = value.astype(jnp.bfloat16)

        next_omega(here, j, scale, stepped_ref, all_ref if count > 1 else in_refs[0], put)

    multiply_and_step(here, scale, w_ref, gram_ref, low_ref, v_ref, next_ref, out_refs)


def last_kernel(count, scale, table_ref, stepped_ref, *rest):
    *in_refs, next_ref, all_ref = rest
    block_rows, slots, block, _ = stepped_ref.shape
    here = Pattern(table_ref, block_rows, slots)
    if count > 1:
        receive(in_refs, all_ref)

    @pl.loop(0, block_rows)
    def _(j):
        def put(k, value):
            next_ref[j, k] = value

        next_omega(here, j, scale, stepped_ref, all_ref if count > 1 else in_refs[0], put)


def call(kernel, inputs, outs, scratch, smem=1, left=(), sems=(), out_space=VMEM):
    arrays = (*inputs, *outs, *scratch)
    size = sum(math.prod(x.shape) * jnp.dtype(x.dtype).itemsize for x in arrays)
    specs = [SMEM] * smem + [VMEM] * (len(inputs) - smem)
    for i in left:
        specs[i] = pl.BlockSpec(memory_space=pl.ANY)
    return pl.pallas_call(
        kernel,
        out_shape=outs,
        in_specs=specs,
        out_specs=[out_space] * len(outs),
        scratch_shapes=[*scratch, *sems],
        compiler_params=pltpu.CompilerParams(vmem_limit_bytes=size + (6 << 20)),
        cost_estimate=pl.CostEstimate(flops=1, bytes_accessed=1, transcendentals=0),
    )(*inputs)


def swap(x, bit):
    count = lax.axis_size("samp")
    return lax.ppermute(x, "samp", [(i, i ^ bit) for i in range(count)])


def from_ys(x):
    return [x] + [swap(x, bit) for bit in range(2, lax.axis_size("samp"), 2)]


def both_cores(parts):
    return (*parts, *(swap(x, 1) for x in parts))


def after(x, *earlier):
    return lax.optimization_barrier((x, *earlier))[0]


def fenced(always, part, *args):
    def nothing(*args):
        return jax.tree.map(lambda x: jnp.zeros(x.shape, x.dtype), jax.eval_shape(part, *args))

    return lax.cond(always, part, nothing, *args)


def local(samples, precision, col_blocks):
    row_count = samples.shape[0]
    block_rows, slots, block, _ = precision.shape
    peers = lax.axis_size("feat")
    ways = lax.axis_size("samp") // 2
    scale = 0.5 * STEP / (row_count * lax.axis_size("samp"))
    rounds = peers == 8 and ways == 2
    groups = [(1, 6), (6, 8)] if rounds else [(0, peers)]

    def shape(dims, dtype):
        return jax.ShapeDtypeStruct(dims, dtype)

    bf16, f32 = samples.dtype, jnp.float32
    strip = (block, row_count)
    sem = pltpu.SemaphoreType.DMA(())
    sends = [shape(strip, bf16)] * (peers - 1) if rounds else [shape((peers, *strip), bf16)]
    own, *sends = call(
        functools.partial(pack_kernel, rounds),
        (col_blocks, samples),
        [shape((block_rows, *strip), bf16), *sends],
        [pltpu.SMEM((peers,), jnp.int32)],
    )

    def exchange(x, r):
        return lax.ppermute(x, "feat", [(i, i ^ r) for i in range(peers)])

    grams = [
        shape((block_rows, slots * block, slots * block), bf16),
        shape((block_rows, 8, block), f32),
    ]

    def pattern():
        width = max(peers, block_rows * slots)
        return call(
            functools.partial(pattern_kernel, rounds, peers),
            (col_blocks,),
            [shape((8, width), jnp.int32)],
            [],
            out_space=SMEM,
        )[0]

    def own_list(own, other):
        return call(
            own_gram_kernel,
            (own, other),
            [shape((block_rows * (block_rows + 1) // 4, block + 16, block), bf16)],
            [],
            smem=0,
        )[0]

    def arrival_list(first, last, table, own_pair, arrived, over):
        return call(
            functools.partial(gram_kernel, rounds, first, last),
            (table, *own_pair, *arrived, *over),
            [shape((last - first, slots // 2 * block + 16, block), bf16)],
            [pltpu.VMEM((2, slots // 2 * block, row_count), bf16)],
        )[0]

    def gather_own(table, *parts):
        return call(
            functools.partial(gather_own_kernel, slots),
            (table, *parts),
            grams,
            [
                pltpu.VMEM((block_rows + 1, block_rows + 1, block, block), bf16),
                pltpu.VMEM((8, block), f32),
            ],
        )

    def gather(table, gram, low, *lists):
        return call(
            functools.partial(gather_kernel, groups[:-1], ways, slots),
            (table, gram, low, *sum(lists, ())),
            grams,
            [],
            left=[1],
            sems=[sem],
        )

    def over_of(blocks, earlier):
        return [swap(after(x, earlier), 1) for x in blocks]

    always = col_blocks[0, 0] >= 0
    if rounds:
        other = swap(own, 1)
        own_pair = (own, other)
        ready = [*sends[:2], after(sends[2], other), *sends[3:]]
        arrived = [exchange(ready[r - 1], r) for r in (1, 2, 3, 4, 5)]

        def begin(own, other):
            return own_list(own, other), pattern()

        step, table = fenced(always, begin, own, other)
        over = over_of(arrived, step)
        arrived += [exchange(after(sends[r - 1], arrived[r - 3]), r) for r in (6, 7)]

        def own_part(table, own_list, own_y):
            return gather_own(table, own_list, own_y, swap(own_list, 1), swap(own_y, 1))

        def most(table, own_pair, arrived, over, own_list):
            own_y = swap(own_list, 2)
            out = after(arrival_list(1, 6, table, own_pair, arrived, over), own_y)
            out_y, own_y = swap(out, 2), after(own_y, out)
            gram, low = fenced(always, own_part, table, own_list, own_y)
            out_core = swap(after(out, gram), 1)
            out_both = swap(after(out_y, gram), 1)
            return gram, low, (out, out_y, out_core, out_both)

        gram, low, *lists = fenced(always, most, table, own_pair, arrived[:5], over, step)
        over += over_of(arrived[5:], gram)
        step = arrival_list(6, 8, table, own_pair, arrived, over)
        gram, low = gather(table, after(gram, step), low, *lists)
        last_list = both_cores([step, after(from_ys(step)[1], gram)])
    else:
        other = swap(own, 1)
        table = pattern()
        arrived = lax.all_to_all(sends[0], "feat", 0, 0, tiled=True)
        gram, low = gather_own(table, *both_cores(from_ys(own_list(own, other))))
        last_list = both_cores(
            from_ys(arrival_list(0, peers, table, (own, other), [arrived], [swap(arrived, 1)]))
        )
    blocks = shape(precision.shape, f32)
    swapped = [shape((block, block) if rounds else (peers, block, block), bf16)]
    if rounds:
        swapped *= len(TURNS)
    all_in = pltpu.VMEM((peers, block, block) if rounds else (8, 128), bf16)

    def trade(out):
        if not rounds:
            return [lax.all_to_all(out[0], "feat", 0, 0, tiled=True)]
        got = []
        for x, turn in zip(out, TURNS):
            pairs = [
                (s * peers + f, s * peers + (f ^ turn[s % 2]))
                for s in range(lax.axis_size("samp"))
                for f in range(peers)
            ]
            got.append(lax.ppermute(x, ("samp", "feat"), pairs))
        got = jnp.stack(got)
        return [got, swap(got, 1)]

    work = [
        pltpu.VMEM((block_rows, block, slots * block), bf16),
        pltpu.VMEM((block_rows, block, (slots + 1) * block), f32),
    ]
    gram, low, stepped, *out = call(
        functools.partial(first_kernel, groups[-1], ways, scale),
        (table, precision, gram, low, *last_list),
        [*grams, blocks, *swapped],
        work,
        left=[2],
        sems=[sem],
    )
    for iteration in range(ITERS):
        mirrored = trade(out)
        if iteration + 1 < ITERS:
            stepped, *out = call(
                functools.partial(middle_kernel, len(mirrored), scale),
                (table, stepped, *mirrored, gram, low),
                [blocks, *swapped],
                [*work, all_in],
            )
    (updated,) = call(
        functools.partial(last_kernel, len(mirrored), scale),
        (table, stepped, *mirrored),
        [blocks],
        [all_in],
    )
    return updated


def solution(mesh):
    return jax.shard_map(
        local,
        mesh=mesh,
        in_specs=(P("samp", "feat"), P("feat", None, None, None), P("feat", None)),
        out_specs=P("feat", None, None, None),
        check_vma=False,
    )
```

```python
import functools
import math

import jax
import jax.numpy as jnp
from jax import lax
from jax.experimental import pallas as pl
from jax.experimental.pallas import tpu as pltpu
from jax.sharding import PartitionSpec as P

ITERS = 3
STEP = 0.2
TURNS = ((2, 7), (3, 5), (2, 6), (1, 4))
SHRINK = 0.05

SMEM = pl.BlockSpec(memory_space=pltpu.SMEM)
VMEM = pl.BlockSpec(memory_space=pltpu.VMEM)


def dot_nt(a, b):
    return lax.dot_general(a, b, (((1,), (1,)), ((), ())), preferred_element_type=jnp.float32)


def dot_nn(a, b):
    return lax.dot_general(a, b, (((1,), (0,)), ((), ())), preferred_element_type=jnp.float32)


class Pattern:
    def __init__(self, table, block_rows, slots):
        self.table = table
        self.block_rows = block_rows
        self.slots = slots

    def link(self, place):
        return self.table[0, place], self.table[1, place]

    def sent(self, peer):
        return self.table[2, peer], self.table[3, peer]

    def source(self, j, k):
        return self.table[4, j * self.slots + k]

    def peer(self, j, k):
        return self.table[5, j * self.slots + k]

    def mate(self, j, k):
        return self.table[6, j * self.slots + k], self.table[7, j * self.slots + k]

    def known(self, source, place):
        return (source >= 0) & (source - self.block_rows <= place)


def find(cb_ref, block_rows, rounds, c):
    me = lax.axis_index("feat")
    safe = jnp.maximum(c, 0)
    holder = lax.div(safe, block_rows)
    place = lax.bitwise_xor(holder, me) if rounds else holder
    return c >= 0, (c >= 0) & (holder == me), lax.rem(safe, block_rows), holder, place


def pattern_kernel(rounds, peers, cb_ref, table_ref):
    block_rows, slots = cb_ref.shape
    me = lax.axis_index("feat")
    for p in range(peers):
        table_ref[0, p] = -1
        table_ref[1, p] = -1
        table_ref[2, p] = 0
        table_ref[3, p] = slots

    @pl.loop(0, block_rows)
    def _(j):
        for k in range(slots):
            filled, own, b, holder, place = find(cb_ref, block_rows, rounds, cb_ref[j, k])
            m = jnp.int32(0)
            for other in range(1, slots):
                m = jnp.where(cb_ref[b, other] == me * block_rows + j, other, m)
            i = j * slots + k
            table_ref[4, i] = jnp.where(filled, jnp.where(own, b, block_rows + place), -1)
            peer, nobody = (place, 0) if rounds else (holder, me)
            table_ref[5, i] = jnp.where(filled & jnp.logical_not(own), peer, nobody)
            table_ref[6, i] = jnp.where(own, b, 0)
            table_ref[7, i] = jnp.where(own, m, slots)

            @pl.when(filled & jnp.logical_not(own))
            def _(k=k, peer=peer, place=place):
                table_ref[0, place] = j
                table_ref[1, place] = k
                table_ref[2, peer] = j
                table_ref[3, peer] = k


def aligned(index, block):
    return pl.ds(pl.multiple_of(index * block, block), block)


def span(k, block):
    return slice(k * block, (k + 1) * block)


def pack_kernel(rounds, cb_ref, x_ref, own_ref, *rest):
    *send_refs, row_ref = rest
    block_rows, block, _ = own_ref.shape
    peers = row_ref.shape[0]
    for p in range(peers):
        row_ref[p] = 0

    @pl.loop(0, block_rows)
    def _(j):
        for k in range(1, cb_ref.shape[1]):
            filled, own, _, _, place = find(cb_ref, block_rows, rounds, cb_ref[j, k])

            @pl.when(filled & jnp.logical_not(own))
            def _(place=place):
                row_ref[place] = j

    for b in range(block_rows):
        own_ref[b] = x_ref[:, span(b, block)].T
    if rounds:
        for r, send_ref in enumerate(send_refs, 1):
            send_ref[...] = own_ref[row_ref[r]]
    else:
        (send_ref,) = send_refs

        @pl.loop(0, peers)
        def _(p):
            send_ref[p] = own_ref[row_ref[p]]


def eye_of(block):
    return lax.broadcasted_iota(jnp.int32, (block, block), 0) == lax.broadcasted_iota(
        jnp.int32, (block, block), 1
    )


def low_diagonal(value, high):
    rest = value - high.astype(jnp.float32)
    return jnp.sum(jnp.where(eye_of(value.shape[0]), rest, 0.0), axis=0, keepdims=True)


def put_low(out_ref, i, value, high):
    low = jnp.broadcast_to(low_diagonal(value, high), (16, value.shape[1]))
    out_ref[i, out_ref.shape[1] - 16 :] = low.astype(jnp.bfloat16)


def own_pairs(block_rows):
    pairs = [(a, b) for a in range(block_rows) for b in range(a, block_rows)]
    return list(zip(pairs[::2], pairs[1::2]))


def own_gram_kernel(mine_ref, other_ref, out_ref):
    core = lax.rem(lax.axis_index("samp"), 2)
    block = mine_ref.shape[1]
    for i, ((a, b), (c, d)) in enumerate(own_pairs(mine_ref.shape[0])):
        x, y = jnp.where(core == 0, a, c), jnp.where(core == 0, b, d)
        value = dot_nt(mine_ref[x], mine_ref[y]) + dot_nt(other_ref[x], other_ref[y])
        high = value.astype(jnp.bfloat16)
        out_ref[i, :block] = high
        put_low(out_ref, i, value, high)


def slot_at(k, position):
    return k if position == 0 else jnp.where(k == position, 0, position)


def gram_kernel(rounds, first, last, table_ref, mine_ref, other_ref, *rest):
    *arrived_refs, out_ref, beside_ref = rest
    block_rows, block, samples = mine_ref.shape
    slots = 2 * (beside_ref.shape[1] // block)
    core = lax.rem(lax.axis_index("samp"), 2)
    here = Pattern(table_ref, block_rows, slots)
    count = len(arrived_refs) // 2

    def arrival(q):
        if rounds:
            return arrived_refs[q - 1][...], arrived_refs[count + q - 1][...]
        return arrived_refs[0][q], arrived_refs[1][q]

    def body(p):
        row, k = here.link(p)

        @pl.when(row >= 0)
        def _():
            for i in range(slots // 2):
                l = jnp.where(core == 0, slot_at(k, 2 * i), slot_at(k, 2 * i + 1))
                source = here.source(row, l)
                at = span(i, block)
                near = jnp.clip(source, 0, block_rows - 1)
                beside_ref[0, at] = mine_ref[near]
                beside_ref[1, at] = other_ref[near]

                def from_arrival(q, at=at, source=source):
                    @pl.when(source == block_rows + q)
                    def _():
                        beside_ref[0, at], beside_ref[1, at] = arrival(q)

                if rounds:
                    for q in range(1, p + 1):
                        from_arrival(q)
                else:

                    @pl.when((source >= block_rows) & (source <= block_rows + p))
                    def _(at=at, source=source):
                        beside_ref[0, at], beside_ref[1, at] = arrival(source - block_rows)

            mine, other = arrival(p)
            value = dot_nt(beside_ref[0], mine) + dot_nt(beside_ref[1], other)
            high = value.astype(jnp.bfloat16)
            out_ref[p - first, : slots // 2 * block] = high
            put_low(out_ref, p - first, value[:block], high[:block])

    if rounds:
        for p in range(first, last):
            body(p)
    else:
        pl.loop(first, last)(body)


def read_part(parts, mine, index):
    half = len(parts) // 2
    terms = [
        jnp.where(mine, a[index], b[index]).astype(jnp.float32)
        for a, b in zip(parts[:half], parts[half:])
    ]
    while len(terms) > 1:
        terms = [a + b for a, b in zip(terms[::2], terms[1::2])]
    return terms[0]


def place_arrivals(here, first, last, parts, gram_ref, low_ref):
    block = parts[0].shape[2]
    slots = here.slots
    core = lax.rem(lax.axis_index("samp"), 2)

    @pl.loop(first, last)
    def _(p):
        row, k = here.link(p)

        @pl.when(row >= 0)
        def _():
            i = p - first
            for position in range(slots):
                l = slot_at(k, position)
                mine = core == position % 2
                value = read_part(parts, mine, (i, span(position // 2, block)))
                value = jnp.where(here.known(here.source(row, l), p), value, 0.0)
                high = value.astype(jnp.bfloat16)
                gram_ref[row, aligned(l, block), aligned(k, block)] = high
                if position:
                    gram_ref[row, aligned(k, block), aligned(l, block)] = high.T
                else:
                    lows = read_part(parts, mine, (i, pl.ds(slots // 2 * block, 1)))
                    low_ref[row, pl.ds(k, 1)] = low_diagonal(value, high) + lows


def gather_own_kernel(slots, table_ref, *rest):
    *parts, gram_ref, low_ref, sum_ref, row_ref = rest
    block_rows = gram_ref.shape[0]
    block = parts[0].shape[2]
    core = lax.rem(lax.axis_index("samp"), 2)
    here = Pattern(table_ref, block_rows, slots)
    sum_ref[block_rows] = jnp.zeros(sum_ref.shape[1:], sum_ref.dtype)
    row_ref[...] = jnp.zeros(row_ref.shape, row_ref.dtype)
    low_ref[...] = jnp.zeros(low_ref.shape, low_ref.dtype)
    for a in range(block_rows):
        sum_ref[a, block_rows] = jnp.zeros((block, block), sum_ref.dtype)
    for i, two in enumerate(own_pairs(block_rows)):
        for maker, (a, b) in enumerate(two):
            value = read_part(parts, core == maker, (i, slice(0, block)))
            high = value.astype(jnp.bfloat16)
            sum_ref[a, b] = high
            if a == b:
                lows = read_part(parts, core == maker, (i, slice(block, block + 1)))
                row_ref[a : a + 1] = low_diagonal(value, high) + lows
            else:
                sum_ref[b, a] = high.T

    @pl.loop(0, block_rows)
    def _(j):
        sources = [here.source(j, k) for k in range(slots)]
        rows = [
            jnp.where((x >= 0) & (x < block_rows), x, block_rows) for x in sources
        ]
        for k, a in enumerate(rows):
            low_ref[j, k : k + 1] = row_ref[pl.ds(a, 1)]
            for l, b in enumerate(rows):
                gram_ref[j, span(k, block), span(l, block)] = sum_ref[a, b]


def gather_kernel(groups, ways, slots, table_ref, gram_in_ref, low_in_ref, *rest):
    *parts, gram_ref, low_ref, sem = rest
    copy = pltpu.make_async_copy(gram_in_ref, gram_ref, sem)
    copy.start()
    low_ref[...] = low_in_ref[...]
    here = Pattern(table_ref, gram_ref.shape[0], slots)
    copy.wait()
    for g, (first, last) in enumerate(groups):
        at = slice(2 * ways * g, 2 * ways * (g + 1))
        place_arrivals(here, first, last, parts[at], gram_ref, low_ref)


def send(here, v_ref, out_refs):
    block = v_ref.shape[1]

    def put(out_ref, index, peer):
        row, column = here.sent(peer)
        out_ref[index] = v_ref[row, :, aligned(column, block)].astype(out_ref.dtype).T

    if len(out_refs) > 1:
        core = lax.rem(lax.axis_index("samp"), 2)
        for out_ref, (a, b) in zip(out_refs, TURNS):
            put(out_ref, ..., jnp.where(core == 0, a, b))
    else:

        @pl.loop(0, out_refs[0].shape[0])
        def _(p):
            put(out_refs[0], p, p)


def receive(in_refs, all_ref):
    core = lax.rem(lax.axis_index("samp"), 2)
    mine_ref, other_ref = in_refs
    for turn, (a, b) in enumerate(TURNS):
        mine, other = mine_ref[turn], other_ref[turn]
        all_ref[a] = jnp.where(core == 0, mine, other)
        all_ref[b] = jnp.where(core == 0, other, mine)
    all_ref[0] = jnp.zeros(all_ref.shape[1:], all_ref.dtype)


def multiply_and_send(here, w_ref, gram_ref, low_ref, v_ref, out_refs):
    block_rows, slots, block = here.block_rows, here.slots, v_ref.shape[1]
    v_ref[:, :, slots * block :] = jnp.zeros((block_rows, block, block), jnp.float32)

    @pl.loop(0, block_rows)
    def _(j):
        value = dot_nn(w_ref[j], gram_ref[j])
        for k in range(slots):
            at = span(k, block)
            low = w_ref[j, :, at].astype(jnp.float32) * low_ref[j, k : k + 1]
            v_ref[j, :, at] = value[:, at] + low

    send(here, v_ref, out_refs)


def step_kernel(first, scale, table_ref, omega_ref, v_ref, stepped_ref):
    block_rows, slots, block, _ = omega_ref.shape
    here = Pattern(table_ref, block_rows, slots)

    @pl.loop(0, block_rows)
    def _(j):
        for k in range(slots):
            row, column = here.mate(j, k)
            omega = omega_ref[j, k]
            if first:
                omega = jnp.where(here.source(j, k) >= 0, omega, 0.0)
            mirrored = v_ref[row, :, aligned(column, block)].T
            stepped_ref[j, k] = omega - scale * (v_ref[j, :, span(k, block)] + mirrored)


def first_kernel(group, ways, table_ref, prec_ref, gram_in_ref, low_in_ref, *rest):
    parts, rest = rest[: 2 * ways], rest[2 * ways :]
    gram_ref, low_ref, v_ref, *out_refs, w_ref, sem = rest
    copy = pltpu.make_async_copy(gram_in_ref, gram_ref, sem)
    copy.start()
    low_ref[...] = low_in_ref[...]
    block_rows, slots, block, _ = prec_ref.shape
    here = Pattern(table_ref, block_rows, slots)

    @pl.loop(0, block_rows)
    def _(j):
        for k in range(slots):
            value = jnp.where(here.source(j, k) >= 0, prec_ref[j, k], 0.0)
            w_ref[j, :, span(k, block)] = value.astype(jnp.bfloat16)

    copy.wait()
    place_arrivals(here, *group, parts, gram_ref, low_ref)
    multiply_and_send(here, w_ref, gram_ref, low_ref, v_ref, out_refs)


def soft(m):
    return m - jnp.clip(m, -SHRINK, SHRINK)


def next_omega(here, j, scale, stepped_ref, in_ref, put):
    block = stepped_ref.shape[2]
    for k in range(here.slots):
        m = stepped_ref[j, k]
        if k == 0:
            root = 0.5 * (m + jnp.sqrt(m * m + 4.0 * STEP))
            put(k, jnp.where(eye_of(block), root, soft(m)))
        else:
            arrived = in_ref[here.peer(j, k)].astype(jnp.float32)
            put(k, soft(m - scale * arrived))


def middle_kernel(count, scale, table_ref, stepped_ref, *rest):
    in_refs, rest = rest[:count], rest[count:]
    gram_ref, low_ref, next_ref, v_ref, *out_refs, w_ref, all_ref = rest
    block_rows, slots, block, _ = stepped_ref.shape
    here = Pattern(table_ref, block_rows, slots)
    if count > 1:
        receive(in_refs, all_ref)

    @pl.loop(0, block_rows)
    def _(j):
        def put(k, value):
            next_ref[j, k] = value
            w_ref[j, :, span(k, block)] = value.astype(jnp.bfloat16)

        next_omega(here, j, scale, stepped_ref, all_ref if count > 1 else in_refs[0], put)

    multiply_and_send(here, w_ref, gram_ref, low_ref, v_ref, out_refs)


def last_kernel(count, scale, table_ref, stepped_ref, *rest):
    *in_refs, next_ref, all_ref = rest
    block_rows, slots, block, _ = stepped_ref.shape
    here = Pattern(table_ref, block_rows, slots)
    if count > 1:
        receive(in_refs, all_ref)

    @pl.loop(0, block_rows)
    def _(j):
        def put(k, value):
            next_ref[j, k] = value

        next_omega(here, j, scale, stepped_ref, all_ref if count > 1 else in_refs[0], put)


def call(kernel, inputs, outs, scratch, smem=1, left=(), sems=(), out_space=VMEM):
    arrays = (*inputs, *outs, *scratch)
    size = sum(math.prod(x.shape) * jnp.dtype(x.dtype).itemsize for x in arrays)
    specs = [SMEM] * smem + [VMEM] * (len(inputs) - smem)
    for i in left:
        specs[i] = pl.BlockSpec(memory_space=pl.ANY)
    return pl.pallas_call(
        kernel,
        out_shape=outs,
        in_specs=specs,
        out_specs=[out_space] * len(outs),
        scratch_shapes=[*scratch, *sems],
        compiler_params=pltpu.CompilerParams(vmem_limit_bytes=size + (6 << 20)),
        cost_estimate=pl.CostEstimate(flops=1, bytes_accessed=1, transcendentals=0),
    )(*inputs)


def swap(x, bit):
    count = lax.axis_size("samp")
    return lax.ppermute(x, "samp", [(i, i ^ bit) for i in range(count)])


def from_ys(x):
    return [x] + [swap(x, bit) for bit in range(2, lax.axis_size("samp"), 2)]


def both_cores(parts):
    return (*parts, *(swap(x, 1) for x in parts))


def after(x, *earlier):
    return lax.optimization_barrier((x, *earlier))[0]


def fenced(always, part, *args):
    def nothing(*args):
        return jax.tree.map(lambda x: jnp.zeros(x.shape, x.dtype), jax.eval_shape(part, *args))

    return lax.cond(always, part, nothing, *args)


def local(samples, precision, col_blocks):
    row_count = samples.shape[0]
    block_rows, slots, block, _ = precision.shape
    peers = lax.axis_size("feat")
    ways = lax.axis_size("samp") // 2
    scale = 0.5 * STEP / (row_count * lax.axis_size("samp"))
    rounds = peers == 8 and ways == 2
    groups = [(1, 6), (6, 8)] if rounds else [(0, peers)]

    def shape(dims, dtype):
        return jax.ShapeDtypeStruct(dims, dtype)

    bf16, f32 = samples.dtype, jnp.float32
    strip = (block, row_count)
    sem = pltpu.SemaphoreType.DMA(())
    sends = [shape(strip, bf16)] * (peers - 1) if rounds else [shape((peers, *strip), bf16)]
    own, *sends = call(
        functools.partial(pack_kernel, rounds),
        (col_blocks, samples),
        [shape((block_rows, *strip), bf16), *sends],
        [pltpu.SMEM((peers,), jnp.int32)],
    )

    def exchange(x, r):
        return lax.ppermute(x, "feat", [(i, i ^ r) for i in range(peers)])

    grams = [
        shape((block_rows, slots * block, slots * block), bf16),
        shape((block_rows, 8, block), f32),
    ]

    def pattern():
        width = max(peers, block_rows * slots)
        return call(
            functools.partial(pattern_kernel, rounds, peers),
            (col_blocks,),
            [shape((8, width), jnp.int32)],
            [],
            out_space=SMEM,
        )[0]

    def own_list(own, other):
        return call(
            own_gram_kernel,
            (own, other),
            [shape((block_rows * (block_rows + 1) // 4, block + 16, block), bf16)],
            [],
            smem=0,
        )[0]

    def arrival_list(first, last, table, own_pair, arrived, over):
        return call(
            functools.partial(gram_kernel, rounds, first, last),
            (table, *own_pair, *arrived, *over),
            [shape((last - first, slots // 2 * block + 16, block), bf16)],
            [pltpu.VMEM((2, slots // 2 * block, row_count), bf16)],
        )[0]

    def gather_own(table, *parts):
        return call(
            functools.partial(gather_own_kernel, slots),
            (table, *parts),
            grams,
            [
                pltpu.VMEM((block_rows + 1, block_rows + 1, block, block), bf16),
                pltpu.VMEM((8, block), f32),
            ],
        )

    def gather(table, gram, low, *lists):
        return call(
            functools.partial(gather_kernel, groups[:-1], ways, slots),
            (table, gram, low, *sum(lists, ())),
            grams,
            [],
            left=[1],
            sems=[sem],
        )

    def over_of(blocks, earlier):
        return [swap(after(x, earlier), 1) for x in blocks]

    always = col_blocks[0, 0] >= 0
    if rounds:
        other = swap(own, 1)
        own_pair = (own, other)
        ready = [*sends[:2], after(sends[2], other), *sends[3:]]
        arrived = [exchange(ready[r - 1], r) for r in (1, 2, 3, 4, 5)]

        def begin(own, other):
            return own_list(own, other), pattern()

        step, table = fenced(always, begin, own, other)
        over = over_of(arrived, step)
        arrived += [exchange(after(sends[r - 1], arrived[r - 3]), r) for r in (6, 7)]

        def own_part(table, own_list, own_y):
            return gather_own(table, own_list, own_y, swap(own_list, 1), swap(own_y, 1))

        def most(table, own_pair, arrived, over, own_list):
            own_y = swap(own_list, 2)
            out = after(arrival_list(1, 6, table, own_pair, arrived, over), own_y)
            out_y, own_y = swap(out, 2), after(own_y, out)
            gram, low = fenced(always, own_part, table, own_list, own_y)
            out_core = swap(after(out, gram), 1)
            out_both = swap(after(out_y, gram), 1)
            return gram, low, (out, out_y, out_core, out_both)

        gram, low, *lists = fenced(always, most, table, own_pair, arrived[:5], over, step)
        over += over_of(arrived[5:], gram)
        step = arrival_list(6, 8, table, own_pair, arrived, over)
        gram, low = gather(table, after(gram, step), low, *lists)
        last_list = both_cores([step, after(from_ys(step)[1], gram)])
    else:
        other = swap(own, 1)
        table = pattern()
        arrived = lax.all_to_all(sends[0], "feat", 0, 0, tiled=True)
        gram, low = gather_own(table, *both_cores(from_ys(own_list(own, other))))
        last_list = both_cores(
            from_ys(arrival_list(0, peers, table, (own, other), [arrived], [swap(arrived, 1)]))
        )
    blocks = shape(precision.shape, f32)
    swapped = [shape((block, block) if rounds else (peers, block, block), bf16)]
    if rounds:
        swapped *= len(TURNS)
    all_in = pltpu.VMEM((peers, block, block) if rounds else (8, 128), bf16)

    def trade(out):
        if not rounds:
            return [lax.all_to_all(out[0], "feat", 0, 0, tiled=True)]
        got = []
        for x, turn in zip(out, TURNS):
            pairs = [
                (s * peers + f, s * peers + (f ^ turn[s % 2]))
                for s in range(lax.axis_size("samp"))
                for f in range(peers)
            ]
            got.append(lax.ppermute(x, ("samp", "feat"), pairs))
        got = jnp.stack(got)
        return [got, swap(got, 1)]

    weights = pltpu.VMEM((block_rows, block, slots * block), bf16)
    wide = shape((block_rows, block, (slots + 1) * block), f32)
    gram, low, v, *out = call(
        functools.partial(first_kernel, groups[-1], ways),
        (table, precision, gram, low, *last_list),
        [*grams, wide, *swapped],
        [weights],
        left=[2],
        sems=[sem],
    )
    omega = precision
    for iteration in range(ITERS):
        mirrored = trade(out)
        (stepped,) = call(
            functools.partial(step_kernel, iteration == 0, scale), (table, omega, v), [blocks], []
        )
        if iteration + 1 < ITERS:
            omega, v, *out = call(
                functools.partial(middle_kernel, len(mirrored), scale),
                (table, stepped, *mirrored, gram, low),
                [blocks, wide, *swapped],
                [weights, all_in],
            )
    (updated,) = call(
        functools.partial(last_kernel, len(mirrored), scale),
        (table, stepped, *mirrored),
        [blocks],
        [all_in],
    )
    return updated


def solution(mesh):
    return jax.shard_map(
        local,
        mesh=mesh,
        in_specs=(P("samp", "feat"), P("feat", None, None, None), P("feat", None)),
        out_specs=P("feat", None, None, None),
        check_vma=False,
    )
```

```python
import functools
import math

import jax
import jax.numpy as jnp
from jax import lax
from jax.experimental import pallas as pl
from jax.experimental.pallas import tpu as pltpu
from jax.sharding import PartitionSpec as P

ITERS = 3
STEP = 0.2
TURNS = ((2, 7), (3, 5), (2, 6), (1, 4))
SHRINK = 0.05

SMEM = pl.BlockSpec(memory_space=pltpu.SMEM)
VMEM = pl.BlockSpec(memory_space=pltpu.VMEM)


def dot_nt(a, b):
    return lax.dot_general(a, b, (((1,), (1,)), ((), ())), preferred_element_type=jnp.float32)


def dot_nn(a, b):
    return lax.dot_general(a, b, (((1,), (0,)), ((), ())), preferred_element_type=jnp.float32)


class Pattern:
    def __init__(self, table, block_rows, slots):
        self.table = table
        self.block_rows = block_rows
        self.slots = slots

    def link(self, place):
        return self.table[0, place], self.table[1, place]

    def sent(self, peer):
        return self.table[2, peer], self.table[3, peer]

    def source(self, j, k):
        return self.table[4, j * self.slots + k]

    def peer(self, j, k):
        return self.table[5, j * self.slots + k]

    def mate(self, j, k):
        return self.table[6, j * self.slots + k], self.table[7, j * self.slots + k]

    def known(self, source, place):
        return (source >= 0) & (source - self.block_rows <= place)


def find(cb_ref, block_rows, rounds, c):
    me = lax.axis_index("feat")
    safe = jnp.maximum(c, 0)
    holder = lax.div(safe, block_rows)
    place = lax.bitwise_xor(holder, me) if rounds else holder
    return c >= 0, (c >= 0) & (holder == me), lax.rem(safe, block_rows), holder, place


def pattern_kernel(rounds, peers, cb_ref, table_ref):
    block_rows, slots = cb_ref.shape
    me = lax.axis_index("feat")
    for p in range(peers):
        table_ref[0, p] = -1
        table_ref[1, p] = -1
        table_ref[2, p] = 0
        table_ref[3, p] = slots

    @pl.loop(0, block_rows)
    def _(j):
        for k in range(slots):
            filled, own, b, holder, place = find(cb_ref, block_rows, rounds, cb_ref[j, k])
            m = jnp.int32(0)
            for other in range(1, slots):
                m = jnp.where(cb_ref[b, other] == me * block_rows + j, other, m)
            i = j * slots + k
            table_ref[4, i] = jnp.where(filled, jnp.where(own, b, block_rows + place), -1)
            peer, nobody = (place, 0) if rounds else (holder, me)
            table_ref[5, i] = jnp.where(filled & jnp.logical_not(own), peer, nobody)
            table_ref[6, i] = jnp.where(own, b, 0)
            table_ref[7, i] = jnp.where(own, m, slots)

            @pl.when(filled & jnp.logical_not(own))
            def _(k=k, peer=peer, place=place):
                table_ref[0, place] = j
                table_ref[1, place] = k
                table_ref[2, peer] = j
                table_ref[3, peer] = k


def aligned(index, block):
    return pl.ds(pl.multiple_of(index * block, block), block)


def span(k, block):
    return slice(k * block, (k + 1) * block)


def pack_kernel(rounds, cb_ref, x_ref, own_ref, *rest):
    *send_refs, row_ref = rest
    block_rows, block, _ = own_ref.shape
    peers = row_ref.shape[0]
    for p in range(peers):
        row_ref[p] = 0

    @pl.loop(0, block_rows)
    def _(j):
        for k in range(1, cb_ref.shape[1]):
            filled, own, _, _, place = find(cb_ref, block_rows, rounds, cb_ref[j, k])

            @pl.when(filled & jnp.logical_not(own))
            def _(place=place):
                row_ref[place] = j

    for b in range(block_rows):
        own_ref[b] = x_ref[:, span(b, block)].T
    if rounds:
        for r, send_ref in enumerate(send_refs, 1):
            send_ref[...] = own_ref[row_ref[r]]
    else:
        (send_ref,) = send_refs

        @pl.loop(0, peers)
        def _(p):
            send_ref[p] = own_ref[row_ref[p]]


def eye_of(block):
    return lax.broadcasted_iota(jnp.int32, (block, block), 0) == lax.broadcasted_iota(
        jnp.int32, (block, block), 1
    )


def low_diagonal(value, high):
    rest = value - high.astype(jnp.float32)
    return jnp.sum(jnp.where(eye_of(value.shape[0]), rest, 0.0), axis=0, keepdims=True)


def put_low(out_ref, i, value, high):
    low = jnp.broadcast_to(low_diagonal(value, high), (16, value.shape[1]))
    out_ref[i, out_ref.shape[1] - 16 :] = low.astype(jnp.bfloat16)


def own_pairs(block_rows):
    pairs = [(a, b) for a in range(block_rows) for b in range(a, block_rows)]
    return list(zip(pairs[::2], pairs[1::2]))


def own_gram_kernel(mine_ref, other_ref, out_ref):
    core = lax.rem(lax.axis_index("samp"), 2)
    block = mine_ref.shape[1]
    for i, ((a, b), (c, d)) in enumerate(own_pairs(mine_ref.shape[0])):
        x, y = jnp.where(core == 0, a, c), jnp.where(core == 0, b, d)
        value = dot_nt(mine_ref[x], mine_ref[y]) + dot_nt(other_ref[x], other_ref[y])
        high = value.astype(jnp.bfloat16)
        out_ref[i, :block] = high
        put_low(out_ref, i, value, high)


def slot_at(k, position):
    return k if position == 0 else jnp.where(k == position, 0, position)


def gram_kernel(rounds, first, last, table_ref, mine_ref, other_ref, *rest):
    *arrived_refs, out_ref, beside_ref = rest
    block_rows, block, samples = mine_ref.shape
    slots = 2 * (beside_ref.shape[1] // block)
    core = lax.rem(lax.axis_index("samp"), 2)
    here = Pattern(table_ref, block_rows, slots)
    count = len(arrived_refs) // 2

    def arrival(q):
        if rounds:
            return arrived_refs[q - 1][...], arrived_refs[count + q - 1][...]
        return arrived_refs[0][q], arrived_refs[1][q]

    def body(p):
        row, k = here.link(p)

        @pl.when(row >= 0)
        def _():
            for i in range(slots // 2):
                l = jnp.where(core == 0, slot_at(k, 2 * i), slot_at(k, 2 * i + 1))
                source = here.source(row, l)
                at = span(i, block)
                near = jnp.clip(source, 0, block_rows - 1)
                beside_ref[0, at] = mine_ref[near]
                beside_ref[1, at] = other_ref[near]

                def from_arrival(q, at=at, source=source):
                    @pl.when(source == block_rows + q)
                    def _():
                        beside_ref[0, at], beside_ref[1, at] = arrival(q)

                if rounds:
                    for q in range(1, p + 1):
                        from_arrival(q)
                else:

                    @pl.when((source >= block_rows) & (source <= block_rows + p))
                    def _(at=at, source=source):
                        beside_ref[0, at], beside_ref[1, at] = arrival(source - block_rows)

            mine, other = arrival(p)
            value = dot_nt(beside_ref[0], mine) + dot_nt(beside_ref[1], other)
            high = value.astype(jnp.bfloat16)
            out_ref[p - first, : slots // 2 * block] = high
            put_low(out_ref, p - first, value[:block], high[:block])

    if rounds:
        for p in range(first, last):
            body(p)
    else:
        pl.loop(first, last)(body)


def read_part(parts, mine, index):
    half = len(parts) // 2
    terms = [
        jnp.where(mine, a[index], b[index]).astype(jnp.float32)
        for a, b in zip(parts[:half], parts[half:])
    ]
    while len(terms) > 1:
        terms = [a + b for a, b in zip(terms[::2], terms[1::2])]
    return terms[0]


def place_arrivals(here, first, last, parts, gram_ref, low_ref):
    block = parts[0].shape[2]
    slots = here.slots
    core = lax.rem(lax.axis_index("samp"), 2)

    @pl.loop(first, last)
    def _(p):
        row, k = here.link(p)

        @pl.when(row >= 0)
        def _():
            i = p - first
            for position in range(slots):
                l = slot_at(k, position)
                mine = core == position % 2
                value = read_part(parts, mine, (i, span(position // 2, block)))
                value = jnp.where(here.known(here.source(row, l), p), value, 0.0)
                high = value.astype(jnp.bfloat16)
                gram_ref[row, aligned(l, block), aligned(k, block)] = high
                if position:
                    gram_ref[row, aligned(k, block), aligned(l, block)] = high.T
                else:
                    lows = read_part(parts, mine, (i, pl.ds(slots // 2 * block, 16)))
                    low_ref[row, pl.ds(k, 1)] = low_diagonal(value, high) + lows[:1]


def gather_own_kernel(slots, table_ref, *rest):
    *parts, gram_ref, low_ref, sum_ref, row_ref = rest
    block_rows = gram_ref.shape[0]
    block = parts[0].shape[2]
    core = lax.rem(lax.axis_index("samp"), 2)
    here = Pattern(table_ref, block_rows, slots)
    sum_ref[block_rows] = jnp.zeros(sum_ref.shape[1:], sum_ref.dtype)
    row_ref[...] = jnp.zeros(row_ref.shape, row_ref.dtype)
    low_ref[...] = jnp.zeros(low_ref.shape, low_ref.dtype)
    for a in range(block_rows):
        sum_ref[a, block_rows] = jnp.zeros((block, block), sum_ref.dtype)
    for i, two in enumerate(own_pairs(block_rows)):
        for maker, (a, b) in enumerate(two):
            value = read_part(parts, core == maker, (i, slice(0, block)))
            high = value.astype(jnp.bfloat16)
            sum_ref[a, b] = high
            if a == b:
                lows = read_part(parts, core == maker, (i, slice(block, block + 16)))
                row_ref[a : a + 1] = low_diagonal(value, high) + lows[:1]
            else:
                sum_ref[b, a] = high.T

    @pl.loop(0, block_rows)
    def _(j):
        sources = [here.source(j, k) for k in range(slots)]
        rows = [
            jnp.where((x >= 0) & (x < block_rows), x, block_rows) for x in sources
        ]
        for k, a in enumerate(rows):
            low_ref[j, k : k + 1] = row_ref[pl.ds(a, 1)]
            for l, b in enumerate(rows):
                gram_ref[j, span(k, block), span(l, block)] = sum_ref[a, b]


def gather_kernel(groups, ways, slots, table_ref, gram_in_ref, low_in_ref, *rest):
    *parts, gram_ref, low_ref, sem = rest
    copy = pltpu.make_async_copy(gram_in_ref, gram_ref, sem)
    copy.start()
    low_ref[...] = low_in_ref[...]
    here = Pattern(table_ref, gram_ref.shape[0], slots)
    copy.wait()
    for g, (first, last) in enumerate(groups):
        at = slice(2 * ways * g, 2 * ways * (g + 1))
        place_arrivals(here, first, last, parts[at], gram_ref, low_ref)


def send(here, v_ref, out_refs):
    block = v_ref.shape[1]

    def put(out_ref, index, peer):
        row, column = here.sent(peer)
        out_ref[index] = v_ref[row, :, aligned(column, block)].astype(out_ref.dtype).T

    if len(out_refs) > 1:
        core = lax.rem(lax.axis_index("samp"), 2)
        for out_ref, (a, b) in zip(out_refs, TURNS):
            put(out_ref, ..., jnp.where(core == 0, a, b))
    else:

        @pl.loop(0, out_refs[0].shape[0])
        def _(p):
            put(out_refs[0], p, p)


def receive(in_refs, all_ref):
    core = lax.rem(lax.axis_index("samp"), 2)
    mine_ref, other_ref = in_refs
    for turn, (a, b) in enumerate(TURNS):
        mine, other = mine_ref[turn], other_ref[turn]
        all_ref[a] = jnp.where(core == 0, mine, other)
        all_ref[b] = jnp.where(core == 0, other, mine)
    all_ref[0] = jnp.zeros(all_ref.shape[1:], all_ref.dtype)


def multiply_and_send(here, w_ref, gram_ref, low_ref, v_ref, out_refs):
    block_rows, slots, block = here.block_rows, here.slots, v_ref.shape[1]
    v_ref[:, :, slots * block :] = jnp.zeros((block_rows, block, block), jnp.float32)

    @pl.loop(0, block_rows)
    def _(j):
        value = dot_nn(w_ref[j], gram_ref[j])
        for k in range(slots):
            at = span(k, block)
            low = w_ref[j, :, at].astype(jnp.float32) * low_ref[j, k : k + 1]
            v_ref[j, :, at] = value[:, at] + low

    send(here, v_ref, out_refs)


def step_kernel(first, scale, table_ref, omega_ref, v_ref, stepped_ref):
    block_rows, slots, block, _ = omega_ref.shape
    here = Pattern(table_ref, block_rows, slots)

    @pl.loop(0, block_rows)
    def _(j):
        for k in range(slots):
            row, column = here.mate(j, k)
            omega = omega_ref[j, k]
            if first:
                omega = jnp.where(here.source(j, k) >= 0, omega, 0.0)
            mirrored = v_ref[row, :, aligned(column, block)].T
            stepped_ref[j, k] = omega - scale * (v_ref[j, :, span(k, block)] + mirrored)


def first_kernel(group, ways, table_ref, prec_ref, gram_in_ref, low_in_ref, *rest):
    parts, rest = rest[: 2 * ways], rest[2 * ways :]
    gram_ref, low_ref, v_ref, *out_refs, w_ref, sem = rest
    copy = pltpu.make_async_copy(gram_in_ref, gram_ref, sem)
    copy.start()
    low_ref[...] = low_in_ref[...]
    block_rows, slots, block, _ = prec_ref.shape
    here = Pattern(table_ref, block_rows, slots)

    @pl.loop(0, block_rows)
    def _(j):
        for k in range(slots):
            value = jnp.where(here.source(j, k) >= 0, prec_ref[j, k], 0.0)
            w_ref[j, :, span(k, block)] = value.astype(jnp.bfloat16)

    copy.wait()
    place_arrivals(here, *group, parts, gram_ref, low_ref)
    multiply_and_send(here, w_ref, gram_ref, low_ref, v_ref, out_refs)


def soft(m):
    return m - jnp.clip(m, -SHRINK, SHRINK)


def next_omega(here, j, scale, stepped_ref, in_ref, put):
    block = stepped_ref.shape[2]
    for k in range(here.slots):
        m = stepped_ref[j, k]
        if k == 0:
            root = 0.5 * (m + jnp.sqrt(m * m + 4.0 * STEP))
            put(k, jnp.where(eye_of(block), root, soft(m)))
        else:
            arrived = in_ref[here.peer(j, k)].astype(jnp.float32)
            put(k, soft(m - scale * arrived))


def middle_kernel(count, scale, table_ref, stepped_ref, *rest):
    in_refs, rest = rest[:count], rest[count:]
    gram_ref, low_ref, next_ref, v_ref, *out_refs, w_ref, all_ref = rest
    block_rows, slots, block, _ = stepped_ref.shape
    here = Pattern(table_ref, block_rows, slots)
    if count > 1:
        receive(in_refs, all_ref)

    @pl.loop(0, block_rows)
    def _(j):
        def put(k, value):
            next_ref[j, k] = value
            w_ref[j, :, span(k, block)] = value.astype(jnp.bfloat16)

        next_omega(here, j, scale, stepped_ref, all_ref if count > 1 else in_refs[0], put)

    multiply_and_send(here, w_ref, gram_ref, low_ref, v_ref, out_refs)


def last_kernel(count, scale, table_ref, stepped_ref, *rest):
    *in_refs, out_ref, all_ref, row_ref, sems = rest
    block_rows, slots, block, _ = stepped_ref.shape
    here = Pattern(table_ref, block_rows, slots)
    if count > 1:
        receive(in_refs, all_ref)

    def copy(j):
        return pltpu.make_async_copy(row_ref.at[j], out_ref.at[j], sems.at[j])

    @pl.loop(0, block_rows)
    def _(j):
        def put(k, value):
            row_ref[j, k] = value

        next_omega(here, j, scale, stepped_ref, all_ref if count > 1 else in_refs[0], put)
        copy(j).start()

    @pl.loop(0, block_rows)
    def _(j):
        copy(j).wait()


def call(kernel, inputs, outs, scratch, smem=1, left=(), sems=(), out_space=VMEM):
    arrays = (*inputs, *outs, *scratch)
    size = sum(math.prod(x.shape) * jnp.dtype(x.dtype).itemsize for x in arrays)
    specs = [SMEM] * smem + [VMEM] * (len(inputs) - smem)
    for i in left:
        specs[i] = pl.BlockSpec(memory_space=pl.ANY)
    return pl.pallas_call(
        kernel,
        out_shape=outs,
        in_specs=specs,
        out_specs=[out_space] * len(outs),
        scratch_shapes=[*scratch, *sems],
        compiler_params=pltpu.CompilerParams(vmem_limit_bytes=size + (6 << 20)),
        cost_estimate=pl.CostEstimate(flops=1, bytes_accessed=1, transcendentals=0),
    )(*inputs)


def swap(x, bit):
    count = lax.axis_size("samp")
    return lax.ppermute(x, "samp", [(i, i ^ bit) for i in range(count)])


def from_ys(x):
    return [x] + [swap(x, bit) for bit in range(2, lax.axis_size("samp"), 2)]


def both_cores(parts):
    return (*parts, *(swap(x, 1) for x in parts))


def after(x, *earlier):
    return lax.optimization_barrier((x, *earlier))[0]


def fenced(always, part, *args):
    def nothing(*args):
        return jax.tree.map(lambda x: jnp.zeros(x.shape, x.dtype), jax.eval_shape(part, *args))

    return lax.cond(always, part, nothing, *args)


def local(samples, precision, col_blocks):
    row_count = samples.shape[0]
    block_rows, slots, block, _ = precision.shape
    peers = lax.axis_size("feat")
    ways = lax.axis_size("samp") // 2
    scale = 0.5 * STEP / (row_count * lax.axis_size("samp"))
    rounds = peers == 8 and ways == 2
    groups = [(1, 6), (6, 8)] if rounds else [(0, peers)]

    def shape(dims, dtype):
        return jax.ShapeDtypeStruct(dims, dtype)

    bf16, f32 = samples.dtype, jnp.float32
    strip = (block, row_count)
    sem = pltpu.SemaphoreType.DMA(())
    sends = [shape(strip, bf16)] * (peers - 1) if rounds else [shape((peers, *strip), bf16)]
    own, *sends = call(
        functools.partial(pack_kernel, rounds),
        (col_blocks, samples),
        [shape((block_rows, *strip), bf16), *sends],
        [pltpu.SMEM((peers,), jnp.int32)],
    )

    def exchange(x, r):
        return lax.ppermute(x, "feat", [(i, i ^ r) for i in range(peers)])

    grams = [
        shape((block_rows, slots * block, slots * block), bf16),
        shape((block_rows, 8, block), f32),
    ]

    def pattern():
        width = max(peers, block_rows * slots)
        return call(
            functools.partial(pattern_kernel, rounds, peers),
            (col_blocks,),
            [shape((8, width), jnp.int32)],
            [],
            out_space=SMEM,
        )[0]

    def own_list(own, other):
        return call(
            own_gram_kernel,
            (own, other),
            [shape((block_rows * (block_rows + 1) // 4, block + 16, block), bf16)],
            [],
            smem=0,
        )[0]

    def arrival_list(first, last, table, own_pair, arrived, over):
        return call(
            functools.partial(gram_kernel, rounds, first, last),
            (table, *own_pair, *arrived, *over),
            [shape((last - first, slots // 2 * block + 16, block), bf16)],
            [pltpu.VMEM((2, slots // 2 * block, row_count), bf16)],
        )[0]

    def gather_own(table, *parts):
        return call(
            functools.partial(gather_own_kernel, slots),
            (table, *parts),
            grams,
            [
                pltpu.VMEM((block_rows + 1, block_rows + 1, block, block), bf16),
                pltpu.VMEM((8, block), f32),
            ],
        )

    def gather(table, gram, low, *lists):
        return call(
            functools.partial(gather_kernel, groups[:-1], ways, slots),
            (table, gram, low, *sum(lists, ())),
            grams,
            [],
            left=[1],
            sems=[sem],
        )

    def over_of(blocks, earlier):
        return [swap(after(x, earlier), 1) for x in blocks]

    always = col_blocks[0, 0] >= 0
    if rounds:
        other = swap(own, 1)
        own_pair = (own, other)
        ready = [*sends[:2], after(sends[2], other), *sends[3:]]
        arrived = [exchange(ready[r - 1], r) for r in (1, 2, 3, 4, 5)]

        def begin(own, other):
            return own_list(own, other), pattern()

        step, table = fenced(always, begin, own, other)
        over = over_of(arrived, step)
        arrived += [exchange(after(sends[r - 1], arrived[r - 3]), r) for r in (6, 7)]

        def own_part(table, own_list, own_y):
            return gather_own(table, own_list, own_y, swap(own_list, 1), swap(own_y, 1))

        def most(table, own_pair, arrived, over, own_list):
            own_y = swap(own_list, 2)
            out = after(arrival_list(1, 6, table, own_pair, arrived, over), own_y)
            out_y, own_y = swap(out, 2), after(own_y, out)
            gram, low = fenced(always, own_part, table, own_list, own_y)
            out_core = swap(after(out, gram), 1)
            out_both = swap(after(out_y, gram), 1)
            return gram, low, (out, out_y, out_core, out_both)

        gram, low, *lists = fenced(always, most, table, own_pair, arrived[:5], over, step)
        over += over_of(arrived[5:], gram)
        step = arrival_list(6, 8, table, own_pair, arrived, over)
        gram, low = gather(table, after(gram, step), low, *lists)
        last_list = both_cores([step, after(from_ys(step)[1], gram)])
    else:
        other = swap(own, 1)
        table = pattern()
        arrived = lax.all_to_all(sends[0], "feat", 0, 0, tiled=True)
        gram, low = gather_own(table, *both_cores(from_ys(own_list(own, other))))
        last_list = both_cores(
            from_ys(arrival_list(0, peers, table, (own, other), [arrived], [swap(arrived, 1)]))
        )
    blocks = shape(precision.shape, f32)
    swapped = [shape((block, block) if rounds else (peers, block, block), bf16)]
    if rounds:
        swapped *= len(TURNS)
    all_in = pltpu.VMEM((peers, block, block) if rounds else (8, 128), bf16)

    def trade(out):
        if not rounds:
            return [lax.all_to_all(out[0], "feat", 0, 0, tiled=True)]
        got = []
        for x, turn in zip(out, TURNS):
            pairs = [
                (s * peers + f, s * peers + (f ^ turn[s % 2]))
                for s in range(lax.axis_size("samp"))
                for f in range(peers)
            ]
            got.append(lax.ppermute(x, ("samp", "feat"), pairs))
        got = jnp.stack(got)
        return [got, swap(got, 1)]

    weights = pltpu.VMEM((block_rows, block, slots * block), bf16)
    wide = shape((block_rows, block, (slots + 1) * block), f32)
    gram, low, v, *out = call(
        functools.partial(first_kernel, groups[-1], ways),
        (table, precision, gram, low, *last_list),
        [*grams, wide, *swapped],
        [weights],
        left=[2],
        sems=[sem],
    )
    omega = precision
    for iteration in range(ITERS):
        mirrored = trade(out)
        (stepped,) = call(
            functools.partial(step_kernel, iteration == 0, scale), (table, omega, v), [blocks], []
        )
        if iteration + 1 < ITERS:
            omega, v, *out = call(
                functools.partial(middle_kernel, len(mirrored), scale),
                (table, stepped, *mirrored, gram, low),
                [blocks, wide, *swapped],
                [weights, all_in],
            )
    (updated,) = call(
        functools.partial(last_kernel, len(mirrored), scale),
        (table, stepped, *mirrored),
        [blocks],
        [all_in, pltpu.VMEM(precision.shape, f32)],
        sems=[pltpu.SemaphoreType.DMA((block_rows,))],
        out_space=pl.BlockSpec(memory_space=pl.ANY),
    )
    return updated


def solution(mesh):
    return jax.shard_map(
        local,
        mesh=mesh,
        in_specs=(P("samp", "feat"), P("feat", None, None, None), P("feat", None)),
        out_specs=P("feat", None, None, None),
        check_vma=False,
    )
```

```python
import functools
import math

import jax
import jax.numpy as jnp
from jax import lax
from jax.experimental import pallas as pl
from jax.experimental.pallas import tpu as pltpu
from jax.sharding import PartitionSpec as P

ITERS = 3
STEP = 0.2
TURNS = ((2, 7), (3, 5), (2, 6), (1, 4))
SHRINK = 0.05

SMEM = pl.BlockSpec(memory_space=pltpu.SMEM)
VMEM = pl.BlockSpec(memory_space=pltpu.VMEM)


def dot_nt(a, b):
    return lax.dot_general(a, b, (((1,), (1,)), ((), ())), preferred_element_type=jnp.float32)


def dot_nn(a, b):
    return lax.dot_general(a, b, (((1,), (0,)), ((), ())), preferred_element_type=jnp.float32)


class Pattern:
    def __init__(self, table, block_rows, slots):
        self.table = table
        self.block_rows = block_rows
        self.slots = slots

    def link(self, place):
        return self.table[0, place], self.table[1, place]

    def sent(self, peer):
        return self.table[2, peer], self.table[3, peer]

    def source(self, j, k):
        return self.table[4, j * self.slots + k]

    def peer(self, j, k):
        return self.table[5, j * self.slots + k]

    def mate(self, j, k):
        return self.table[6, j * self.slots + k], self.table[7, j * self.slots + k]

    def known(self, source, place):
        return (source >= 0) & (source - self.block_rows <= place)


def find(cb_ref, block_rows, rounds, c):
    me = lax.axis_index("feat")
    safe = jnp.maximum(c, 0)
    holder = lax.div(safe, block_rows)
    place = lax.bitwise_xor(holder, me) if rounds else holder
    return c >= 0, (c >= 0) & (holder == me), lax.rem(safe, block_rows), holder, place


def pattern_kernel(rounds, peers, cb_ref, table_ref):
    block_rows, slots = cb_ref.shape
    me = lax.axis_index("feat")
    for p in range(peers):
        table_ref[0, p] = -1
        table_ref[1, p] = -1
        table_ref[2, p] = 0
        table_ref[3, p] = slots

    @pl.loop(0, block_rows)
    def _(j):
        for k in range(slots):
            filled, own, b, holder, place = find(cb_ref, block_rows, rounds, cb_ref[j, k])
            m = jnp.int32(0)
            for other in range(1, slots):
                m = jnp.where(cb_ref[b, other] == me * block_rows + j, other, m)
            i = j * slots + k
            table_ref[4, i] = jnp.where(filled, jnp.where(own, b, block_rows + place), -1)
            peer, nobody = (place, 0) if rounds else (holder, me)
            table_ref[5, i] = jnp.where(filled & jnp.logical_not(own), peer, nobody)
            table_ref[6, i] = jnp.where(own, b, 0)
            table_ref[7, i] = jnp.where(own, m, slots)

            @pl.when(filled & jnp.logical_not(own))
            def _(k=k, peer=peer, place=place):
                table_ref[0, place] = j
                table_ref[1, place] = k
                table_ref[2, peer] = j
                table_ref[3, peer] = k


def aligned(index, block):
    return pl.ds(pl.multiple_of(index * block, block), block)


def span(k, block):
    return slice(k * block, (k + 1) * block)


def pack_kernel(rounds, cb_ref, x_ref, own_ref, *rest):
    *send_refs, row_ref = rest
    block_rows, block, _ = own_ref.shape
    peers = row_ref.shape[0]
    for p in range(peers):
        row_ref[p] = 0

    @pl.loop(0, block_rows)
    def _(j):
        for k in range(1, cb_ref.shape[1]):
            filled, own, _, _, place = find(cb_ref, block_rows, rounds, cb_ref[j, k])

            @pl.when(filled & jnp.logical_not(own))
            def _(place=place):
                row_ref[place] = j

    for b in range(block_rows):
        own_ref[b] = x_ref[:, span(b, block)].T
    if rounds:
        for r, send_ref in enumerate(send_refs, 1):
            send_ref[...] = own_ref[row_ref[r]]
    else:
        (send_ref,) = send_refs

        @pl.loop(0, peers)
        def _(p):
            send_ref[p] = own_ref[row_ref[p]]


def eye_of(block):
    return lax.broadcasted_iota(jnp.int32, (block, block), 0) == lax.broadcasted_iota(
        jnp.int32, (block, block), 1
    )


def low_diagonal(value, high):
    rest = value - high.astype(jnp.float32)
    return jnp.sum(jnp.where(eye_of(value.shape[0]), rest, 0.0), axis=0, keepdims=True)


def put_low(out_ref, i, value, high):
    low = jnp.broadcast_to(low_diagonal(value, high), (16, value.shape[1]))
    out_ref[i, out_ref.shape[1] - 16 :] = low.astype(jnp.bfloat16)


def own_pairs(block_rows):
    pairs = [(a, b) for a in range(block_rows) for b in range(a, block_rows)]
    return list(zip(pairs[::2], pairs[1::2]))


def own_gram_kernel(mine_ref, other_ref, out_ref):
    core = lax.rem(lax.axis_index("samp"), 2)
    block = mine_ref.shape[1]
    for i, ((a, b), (c, d)) in enumerate(own_pairs(mine_ref.shape[0])):
        x, y = jnp.where(core == 0, a, c), jnp.where(core == 0, b, d)
        value = dot_nt(mine_ref[x], mine_ref[y]) + dot_nt(other_ref[x], other_ref[y])
        high = value.astype(jnp.bfloat16)
        out_ref[i, :block] = high
        put_low(out_ref, i, value, high)


def slot_at(k, position):
    return k if position == 0 else jnp.where(k == position, 0, position)


def gram_kernel(rounds, first, last, table_ref, mine_ref, other_ref, *rest):
    *arrived_refs, out_ref, beside_ref = rest
    block_rows, block, samples = mine_ref.shape
    slots = 2 * (beside_ref.shape[1] // block)
    core = lax.rem(lax.axis_index("samp"), 2)
    here = Pattern(table_ref, block_rows, slots)
    count = len(arrived_refs) // 2

    def arrival(q):
        if rounds:
            return arrived_refs[q - 1][...], arrived_refs[count + q - 1][...]
        return arrived_refs[0][q], arrived_refs[1][q]

    def body(p):
        row, k = here.link(p)

        @pl.when(row >= 0)
        def _():
            for i in range(slots // 2):
                l = jnp.where(core == 0, slot_at(k, 2 * i), slot_at(k, 2 * i + 1))
                source = here.source(row, l)
                at = span(i, block)
                near = jnp.clip(source, 0, block_rows - 1)
                beside_ref[0, at] = mine_ref[near]
                beside_ref[1, at] = other_ref[near]

                def from_arrival(q, at=at, source=source):
                    @pl.when(source == block_rows + q)
                    def _():
                        beside_ref[0, at], beside_ref[1, at] = arrival(q)

                if rounds:
                    for q in range(1, p + 1):
                        from_arrival(q)
                else:

                    @pl.when((source >= block_rows) & (source <= block_rows + p))
                    def _(at=at, source=source):
                        beside_ref[0, at], beside_ref[1, at] = arrival(source - block_rows)

            mine, other = arrival(p)
            value = dot_nt(beside_ref[0], mine) + dot_nt(beside_ref[1], other)
            high = value.astype(jnp.bfloat16)
            out_ref[p - first, : slots // 2 * block] = high
            put_low(out_ref, p - first, value[:block], high[:block])

    if rounds:
        for p in range(first, last):
            body(p)
    else:
        pl.loop(first, last)(body)


def read_part(parts, mine, index):
    half = len(parts) // 2
    terms = [
        jnp.where(mine, a[index], b[index]).astype(jnp.float32)
        for a, b in zip(parts[:half], parts[half:])
    ]
    while len(terms) > 1:
        terms = [a + b for a, b in zip(terms[::2], terms[1::2])]
    return terms[0]


def place_arrivals(here, first, last, parts, gram_ref, low_ref):
    block = parts[0].shape[2]
    slots = here.slots
    core = lax.rem(lax.axis_index("samp"), 2)

    @pl.loop(first, last)
    def _(p):
        row, k = here.link(p)

        @pl.when(row >= 0)
        def _():
            i = p - first
            for position in range(slots):
                l = slot_at(k, position)
                mine = core == position % 2
                value = read_part(parts, mine, (i, span(position // 2, block)))
                value = jnp.where(here.known(here.source(row, l), p), value, 0.0)
                high = value.astype(jnp.bfloat16)
                gram_ref[row, aligned(l, block), aligned(k, block)] = high
                if position:
                    gram_ref[row, aligned(k, block), aligned(l, block)] = high.T
                else:
                    lows = read_part(parts, mine, (i, pl.ds(slots // 2 * block, 16)))
                    low_ref[row, pl.ds(k, 1)] = low_diagonal(value, high) + lows[:1]


def gather_own_kernel(slots, table_ref, *rest):
    *parts, gram_ref, low_ref, sum_ref, row_ref = rest
    block_rows = gram_ref.shape[0]
    block = parts[0].shape[2]
    core = lax.rem(lax.axis_index("samp"), 2)
    here = Pattern(table_ref, block_rows, slots)
    sum_ref[block_rows] = jnp.zeros(sum_ref.shape[1:], sum_ref.dtype)
    row_ref[...] = jnp.zeros(row_ref.shape, row_ref.dtype)
    low_ref[...] = jnp.zeros(low_ref.shape, low_ref.dtype)
    for a in range(block_rows):
        sum_ref[a, block_rows] = jnp.zeros((block, block), sum_ref.dtype)
    for i, two in enumerate(own_pairs(block_rows)):
        for maker, (a, b) in enumerate(two):
            value = read_part(parts, core == maker, (i, slice(0, block)))
            high = value.astype(jnp.bfloat16)
            sum_ref[a, b] = high
            if a == b:
                lows = read_part(parts, core == maker, (i, slice(block, block + 16)))
                row_ref[a : a + 1] = low_diagonal(value, high) + lows[:1]
            else:
                sum_ref[b, a] = high.T

    @pl.loop(0, block_rows)
    def _(j):
        sources = [here.source(j, k) for k in range(slots)]
        rows = [
            jnp.where((x >= 0) & (x < block_rows), x, block_rows) for x in sources
        ]
        for k, a in enumerate(rows):
            low_ref[j, k : k + 1] = row_ref[pl.ds(a, 1)]
            for l, b in enumerate(rows):
                gram_ref[j, span(k, block), span(l, block)] = sum_ref[a, b]


def gather_kernel(groups, ways, slots, table_ref, gram_in_ref, low_in_ref, *rest):
    *parts, gram_ref, low_ref, sem = rest
    copy = pltpu.make_async_copy(gram_in_ref, gram_ref, sem)
    copy.start()
    low_ref[...] = low_in_ref[...]
    here = Pattern(table_ref, gram_ref.shape[0], slots)
    copy.wait()
    for g, (first, last) in enumerate(groups):
        at = slice(2 * ways * g, 2 * ways * (g + 1))
        place_arrivals(here, first, last, parts[at], gram_ref, low_ref)


def send(here, v_ref, out_refs):
    block = v_ref.shape[1]

    def put(out_ref, index, peer):
        row, column = here.sent(peer)
        out_ref[index] = v_ref[row, :, aligned(column, block)].astype(out_ref.dtype).T

    if len(out_refs) > 1:
        core = lax.rem(lax.axis_index("samp"), 2)
        for out_ref, (a, b) in zip(out_refs, TURNS):
            put(out_ref, ..., jnp.where(core == 0, a, b))
    else:

        @pl.loop(0, out_refs[0].shape[0])
        def _(p):
            put(out_refs[0], p, p)


def receive(in_refs, all_ref):
    core = lax.rem(lax.axis_index("samp"), 2)
    mine_ref, other_ref = in_refs
    for turn, (a, b) in enumerate(TURNS):
        mine, other = mine_ref[turn], other_ref[turn]
        all_ref[a] = jnp.where(core == 0, mine, other)
        all_ref[b] = jnp.where(core == 0, other, mine)
    all_ref[0] = jnp.zeros(all_ref.shape[1:], all_ref.dtype)


def multiply_and_send(here, w_ref, gram_ref, low_ref, v_ref, out_refs):
    block_rows, slots, block = here.block_rows, here.slots, v_ref.shape[1]
    v_ref[:, :, slots * block :] = jnp.zeros((block_rows, block, block), jnp.float32)

    @pl.loop(0, block_rows)
    def _(j):
        value = dot_nn(w_ref[j], gram_ref[j])
        for k in range(slots):
            at = span(k, block)
            low = w_ref[j, :, at].astype(jnp.float32) * low_ref[j, k : k + 1]
            v_ref[j, :, at] = value[:, at] + low

    send(here, v_ref, out_refs)


def step_kernel(first, scale, table_ref, omega_ref, v_ref, stepped_ref):
    block_rows, slots, block, _ = omega_ref.shape
    here = Pattern(table_ref, block_rows, slots)

    @pl.loop(0, block_rows)
    def _(j):
        for k in range(slots):
            row, column = here.mate(j, k)
            omega = omega_ref[j, k]
            if first:
                omega = jnp.where(here.source(j, k) >= 0, omega, 0.0)
            mirrored = v_ref[row, :, aligned(column, block)].T
            stepped_ref[j, k] = omega - scale * (v_ref[j, :, span(k, block)] + mirrored)


def weights_kernel(table_ref, prec_ref, w_ref):
    block_rows, slots, block, _ = prec_ref.shape
    here = Pattern(table_ref, block_rows, slots)

    @pl.loop(0, block_rows)
    def _(j):
        for k in range(slots):
            value = jnp.where(here.source(j, k) >= 0, prec_ref[j, k], 0.0)
            w_ref[j, :, span(k, block)] = value.astype(jnp.bfloat16)


def first_kernel(group, ways, table_ref, w_ref, gram_in_ref, low_in_ref, *rest):
    parts, rest = rest[: 2 * ways], rest[2 * ways :]
    gram_ref, low_ref, v_ref, *out_refs, sem = rest
    copy = pltpu.make_async_copy(gram_in_ref, gram_ref, sem)
    copy.start()
    low_ref[...] = low_in_ref[...]
    block_rows, block, width = w_ref.shape
    slots = width // block
    here = Pattern(table_ref, block_rows, slots)

    copy.wait()
    place_arrivals(here, *group, parts, gram_ref, low_ref)
    multiply_and_send(here, w_ref, gram_ref, low_ref, v_ref, out_refs)


def soft(m):
    return m - jnp.clip(m, -SHRINK, SHRINK)


def next_omega(here, j, scale, stepped_ref, in_ref, put):
    block = stepped_ref.shape[2]
    for k in range(here.slots):
        m = stepped_ref[j, k]
        if k == 0:
            root = 0.5 * (m + jnp.sqrt(m * m + 4.0 * STEP))
            put(k, jnp.where(eye_of(block), root, soft(m)))
        else:
            arrived = in_ref[here.peer(j, k)].astype(jnp.float32)
            put(k, soft(m - scale * arrived))


def middle_kernel(count, scale, table_ref, stepped_ref, *rest):
    in_refs, rest = rest[:count], rest[count:]
    gram_ref, low_ref, next_ref, v_ref, *out_refs, w_ref, all_ref = rest
    block_rows, slots, block, _ = stepped_ref.shape
    here = Pattern(table_ref, block_rows, slots)
    if count > 1:
        receive(in_refs, all_ref)

    @pl.loop(0, block_rows)
    def _(j):
        def put(k, value):
            next_ref[j, k] = value
            w_ref[j, :, span(k, block)] = value.astype(jnp.bfloat16)

        next_omega(here, j, scale, stepped_ref, all_ref if count > 1 else in_refs[0], put)

    multiply_and_send(here, w_ref, gram_ref, low_ref, v_ref, out_refs)


def last_kernel(count, scale, table_ref, stepped_ref, *rest):
    *in_refs, out_ref, all_ref, row_ref, sems = rest
    block_rows, slots, block, _ = stepped_ref.shape
    here = Pattern(table_ref, block_rows, slots)
    if count > 1:
        receive(in_refs, all_ref)

    def copy(j):
        return pltpu.make_async_copy(row_ref.at[j], out_ref.at[j], sems.at[j])

    @pl.loop(0, block_rows)
    def _(j):
        def put(k, value):
            row_ref[j, k] = value

        next_omega(here, j, scale, stepped_ref, all_ref if count > 1 else in_refs[0], put)
        copy(j).start()

    @pl.loop(0, block_rows)
    def _(j):
        copy(j).wait()


def call(kernel, inputs, outs, scratch, smem=1, left=(), sems=(), out_space=VMEM):
    arrays = (*inputs, *outs, *scratch)
    size = sum(math.prod(x.shape) * jnp.dtype(x.dtype).itemsize for x in arrays)
    specs = [SMEM] * smem + [VMEM] * (len(inputs) - smem)
    for i in left:
        specs[i] = pl.BlockSpec(memory_space=pl.ANY)
    return pl.pallas_call(
        kernel,
        out_shape=outs,
        in_specs=specs,
        out_specs=[out_space] * len(outs),
        scratch_shapes=[*scratch, *sems],
        compiler_params=pltpu.CompilerParams(vmem_limit_bytes=size + (6 << 20)),
        cost_estimate=pl.CostEstimate(flops=1, bytes_accessed=1, transcendentals=0),
    )(*inputs)


def swap(x, bit):
    count = lax.axis_size("samp")
    return lax.ppermute(x, "samp", [(i, i ^ bit) for i in range(count)])


def from_ys(x):
    return [x] + [swap(x, bit) for bit in range(2, lax.axis_size("samp"), 2)]


def both_cores(parts):
    return (*parts, *(swap(x, 1) for x in parts))


def after(x, *earlier):
    return lax.optimization_barrier((x, *earlier))[0]


def fenced(always, part, *args):
    def nothing(*args):
        return jax.tree.map(lambda x: jnp.zeros(x.shape, x.dtype), jax.eval_shape(part, *args))

    return lax.cond(always, part, nothing, *args)


def local(samples, precision, col_blocks):
    row_count = samples.shape[0]
    block_rows, slots, block, _ = precision.shape
    peers = lax.axis_size("feat")
    ways = lax.axis_size("samp") // 2
    scale = 0.5 * STEP / (row_count * lax.axis_size("samp"))
    rounds = peers == 8 and ways == 2
    groups = [(1, 6), (6, 8)] if rounds else [(0, peers)]

    def shape(dims, dtype):
        return jax.ShapeDtypeStruct(dims, dtype)

    bf16, f32 = samples.dtype, jnp.float32
    strip = (block, row_count)
    sem = pltpu.SemaphoreType.DMA(())
    sends = [shape(strip, bf16)] * (peers - 1) if rounds else [shape((peers, *strip), bf16)]
    own, *sends = call(
        functools.partial(pack_kernel, rounds),
        (col_blocks, samples),
        [shape((block_rows, *strip), bf16), *sends],
        [pltpu.SMEM((peers,), jnp.int32)],
    )

    def exchange(x, r):
        return lax.ppermute(x, "feat", [(i, i ^ r) for i in range(peers)])

    grams = [
        shape((block_rows, slots * block, slots * block), bf16),
        shape((block_rows, 8, block), f32),
    ]

    def pattern():
        width = max(peers, block_rows * slots)
        return call(
            functools.partial(pattern_kernel, rounds, peers),
            (col_blocks,),
            [shape((8, width), jnp.int32)],
            [],
            out_space=SMEM,
        )[0]

    def own_list(own, other):
        return call(
            own_gram_kernel,
            (own, other),
            [shape((block_rows * (block_rows + 1) // 4, block + 16, block), bf16)],
            [],
            smem=0,
        )[0]

    def arrival_list(first, last, table, own_pair, arrived, over):
        return call(
            functools.partial(gram_kernel, rounds, first, last),
            (table, *own_pair, *arrived, *over),
            [shape((last - first, slots // 2 * block + 16, block), bf16)],
            [pltpu.VMEM((2, slots // 2 * block, row_count), bf16)],
        )[0]

    def gather_own(table, *parts):
        return call(
            functools.partial(gather_own_kernel, slots),
            (table, *parts),
            grams,
            [
                pltpu.VMEM((block_rows + 1, block_rows + 1, block, block), bf16),
                pltpu.VMEM((8, block), f32),
            ],
        )

    def gather(table, gram, low, *lists):
        return call(
            functools.partial(gather_kernel, groups[:-1], ways, slots),
            (table, gram, low, *sum(lists, ())),
            grams,
            [],
            left=[1],
            sems=[sem],
        )

    def over_of(blocks, earlier):
        return [swap(after(x, earlier), 1) for x in blocks]

    always = col_blocks[0, 0] >= 0
    if rounds:
        other = swap(own, 1)
        own_pair = (own, other)
        ready = [*sends[:2], after(sends[2], other), *sends[3:]]
        arrived = [exchange(ready[r - 1], r) for r in (1, 2, 3, 4, 5)]

        def begin(own, other):
            return own_list(own, other), pattern()

        step, table = fenced(always, begin, own, other)
        over = over_of(arrived, step)
        arrived += [exchange(after(sends[r - 1], arrived[r - 3]), r) for r in (6, 7)]

        def own_part(table, own_list, own_y):
            return gather_own(table, own_list, own_y, swap(own_list, 1), swap(own_y, 1))

        def most(table, own_pair, arrived, over, own_list):
            own_y = swap(own_list, 2)
            out = after(arrival_list(1, 6, table, own_pair, arrived, over), own_y)
            out_y, own_y = swap(out, 2), after(own_y, out)
            gram, low = fenced(always, own_part, table, own_list, own_y)
            out_core = swap(after(out, gram), 1)
            out_both = swap(after(out_y, gram), 1)
            return gram, low, (out, out_y, out_core, out_both)

        gram, low, *lists = fenced(always, most, table, own_pair, arrived[:5], over, step)
        over += over_of(arrived[5:], gram)
        step = arrival_list(6, 8, table, own_pair, arrived, over)
        gram, low = gather(table, after(gram, step), low, *lists)
        last_list = both_cores([step, after(from_ys(step)[1], gram)])
    else:
        other = swap(own, 1)
        table = pattern()
        arrived = lax.all_to_all(sends[0], "feat", 0, 0, tiled=True)
        gram, low = gather_own(table, *both_cores(from_ys(own_list(own, other))))
        last_list = both_cores(
            from_ys(arrival_list(0, peers, table, (own, other), [arrived], [swap(arrived, 1)]))
        )
    blocks = shape(precision.shape, f32)
    swapped = [shape((block, block) if rounds else (peers, block, block), bf16)]
    if rounds:
        swapped *= len(TURNS)
    all_in = pltpu.VMEM((peers, block, block) if rounds else (8, 128), bf16)

    def trade(out):
        if not rounds:
            return [lax.all_to_all(out[0], "feat", 0, 0, tiled=True)]
        got = []
        for x, turn in zip(out, TURNS):
            pairs = [
                (s * peers + f, s * peers + (f ^ turn[s % 2]))
                for s in range(lax.axis_size("samp"))
                for f in range(peers)
            ]
            got.append(lax.ppermute(x, ("samp", "feat"), pairs))
        got = jnp.stack(got)
        return [got, swap(got, 1)]

    weights = pltpu.VMEM((block_rows, block, slots * block), bf16)
    wide = shape((block_rows, block, (slots + 1) * block), f32)
    (first_weights,) = call(
        weights_kernel, (table, precision), [shape(weights.shape, bf16)], []
    )
    gram, low, v, *out = call(
        functools.partial(first_kernel, groups[-1], ways),
        (table, first_weights, gram, low, *last_list),
        [*grams, wide, *swapped],
        [],
        left=[2],
        sems=[sem],
    )
    omega = precision
    for iteration in range(ITERS):
        mirrored = trade(out)
        (stepped,) = call(
            functools.partial(step_kernel, iteration == 0, scale), (table, omega, v), [blocks], []
        )
        if iteration + 1 < ITERS:
            omega, v, *out = call(
                functools.partial(middle_kernel, len(mirrored), scale),
                (table, stepped, *mirrored, gram, low),
                [blocks, wide, *swapped],
                [weights, all_in],
            )
    (updated,) = call(
        functools.partial(last_kernel, len(mirrored), scale),
        (table, stepped, *mirrored),
        [blocks],
        [all_in, pltpu.VMEM(precision.shape, f32)],
        sems=[pltpu.SemaphoreType.DMA((block_rows,))],
        out_space=pl.BlockSpec(memory_space=pl.ANY),
    )
    return updated


def solution(mesh):
    return jax.shard_map(
        local,
        mesh=mesh,
        in_specs=(P("samp", "feat"), P("feat", None, None, None), P("feat", None)),
        out_specs=P("feat", None, None, None),
        check_vma=False,
    )
```

```python
import functools
import math

import jax
import jax.numpy as jnp
from jax import lax
from jax.experimental import pallas as pl
from jax.experimental.pallas import tpu as pltpu
from jax.sharding import PartitionSpec as P

ITERS = 3
STEP = 0.2
TURNS = ((2, 7), (3, 5), (2, 6), (1, 4))
SHRINK = 0.05

SMEM = pl.BlockSpec(memory_space=pltpu.SMEM)
VMEM = pl.BlockSpec(memory_space=pltpu.VMEM)


def dot_nt(a, b):
    return lax.dot_general(a, b, (((1,), (1,)), ((), ())), preferred_element_type=jnp.float32)


def dot_nn(a, b):
    return lax.dot_general(a, b, (((1,), (0,)), ((), ())), preferred_element_type=jnp.float32)


class Pattern:
    def __init__(self, table, block_rows, slots):
        self.table = table
        self.block_rows = block_rows
        self.slots = slots

    def link(self, place):
        return self.table[0, place], self.table[1, place]

    def sent(self, peer):
        return self.table[2, peer], self.table[3, peer]

    def source(self, j, k):
        return self.table[4, j * self.slots + k]

    def peer(self, j, k):
        return self.table[5, j * self.slots + k]

    def mate(self, j, k):
        return self.table[6, j * self.slots + k], self.table[7, j * self.slots + k]

    def known(self, source, place):
        return (source >= 0) & (source - self.block_rows <= place)


def find(cb_ref, block_rows, rounds, c):
    me = lax.axis_index("feat")
    safe = jnp.maximum(c, 0)
    holder = lax.div(safe, block_rows)
    place = lax.bitwise_xor(holder, me) if rounds else holder
    return c >= 0, (c >= 0) & (holder == me), lax.rem(safe, block_rows), holder, place


def pattern_kernel(rounds, peers, cb_ref, table_ref):
    block_rows, slots = cb_ref.shape
    me = lax.axis_index("feat")
    for p in range(peers):
        table_ref[0, p] = -1
        table_ref[1, p] = -1
        table_ref[2, p] = 0
        table_ref[3, p] = slots

    @pl.loop(0, block_rows)
    def _(j):
        for k in range(slots):
            filled, own, b, holder, place = find(cb_ref, block_rows, rounds, cb_ref[j, k])
            m = jnp.int32(0)
            for other in range(1, slots):
                m = jnp.where(cb_ref[b, other] == me * block_rows + j, other, m)
            i = j * slots + k
            table_ref[4, i] = jnp.where(filled, jnp.where(own, b, block_rows + place), -1)
            peer, nobody = (place, 0) if rounds else (holder, me)
            table_ref[5, i] = jnp.where(filled & jnp.logical_not(own), peer, nobody)
            table_ref[6, i] = jnp.where(own, b, 0)
            table_ref[7, i] = jnp.where(own, m, slots)

            @pl.when(filled & jnp.logical_not(own))
            def _(k=k, peer=peer, place=place):
                table_ref[0, place] = j
                table_ref[1, place] = k
                table_ref[2, peer] = j
                table_ref[3, peer] = k


def aligned(index, block):
    return pl.ds(pl.multiple_of(index * block, block), block)


def span(k, block):
    return slice(k * block, (k + 1) * block)


def pack_kernel(rounds, cb_ref, x_ref, own_ref, *rest):
    *send_refs, row_ref = rest
    block_rows, block, _ = own_ref.shape
    peers = row_ref.shape[0]
    for p in range(peers):
        row_ref[p] = 0

    @pl.loop(0, block_rows)
    def _(j):
        for k in range(1, cb_ref.shape[1]):
            filled, own, _, _, place = find(cb_ref, block_rows, rounds, cb_ref[j, k])

            @pl.when(filled & jnp.logical_not(own))
            def _(place=place):
                row_ref[place] = j

    for b in range(block_rows):
        own_ref[b] = x_ref[:, span(b, block)].T
    if rounds:
        for r, send_ref in enumerate(send_refs, 1):
            send_ref[...] = own_ref[row_ref[r]]
    else:
        (send_ref,) = send_refs

        @pl.loop(0, peers)
        def _(p):
            send_ref[p] = own_ref[row_ref[p]]


def eye_of(block):
    return lax.broadcasted_iota(jnp.int32, (block, block), 0) == lax.broadcasted_iota(
        jnp.int32, (block, block), 1
    )


def low_diagonal(value, high):
    rest = value - high.astype(jnp.float32)
    return jnp.sum(jnp.where(eye_of(value.shape[0]), rest, 0.0), axis=0, keepdims=True)


def put_low(out_ref, i, value, high):
    low = jnp.broadcast_to(low_diagonal(value, high), (16, value.shape[1]))
    out_ref[i, out_ref.shape[1] - 16 :] = low.astype(jnp.bfloat16)


def own_pairs(block_rows):
    pairs = [(a, b) for a in range(block_rows) for b in range(a, block_rows)]
    return list(zip(pairs[::2], pairs[1::2]))


def own_gram_kernel(mine_ref, other_ref, out_ref):
    core = lax.rem(lax.axis_index("samp"), 2)
    block = mine_ref.shape[1]
    for i, ((a, b), (c, d)) in enumerate(own_pairs(mine_ref.shape[0])):
        x, y = jnp.where(core == 0, a, c), jnp.where(core == 0, b, d)
        value = dot_nt(mine_ref[x], mine_ref[y]) + dot_nt(other_ref[x], other_ref[y])
        high = value.astype(jnp.bfloat16)
        out_ref[i, :block] = high
        put_low(out_ref, i, value, high)


def slot_at(k, position):
    return k if position == 0 else jnp.where(k == position, 0, position)


def gram_kernel(rounds, first, last, table_ref, mine_ref, other_ref, *rest):
    *arrived_refs, out_ref, beside_ref = rest
    block_rows, block, samples = mine_ref.shape
    slots = 2 * (beside_ref.shape[1] // block)
    core = lax.rem(lax.axis_index("samp"), 2)
    here = Pattern(table_ref, block_rows, slots)
    count = len(arrived_refs) // 2

    def arrival(q):
        if rounds:
            return arrived_refs[q - 1][...], arrived_refs[count + q - 1][...]
        return arrived_refs[0][q], arrived_refs[1][q]

    def body(p):
        row, k = here.link(p)

        @pl.when(row >= 0)
        def _():
            for i in range(slots // 2):
                l = jnp.where(core == 0, slot_at(k, 2 * i), slot_at(k, 2 * i + 1))
                source = here.source(row, l)
                at = span(i, block)
                near = jnp.clip(source, 0, block_rows - 1)
                beside_ref[0, at] = mine_ref[near]
                beside_ref[1, at] = other_ref[near]

                def from_arrival(q, at=at, source=source):
                    @pl.when(source == block_rows + q)
                    def _():
                        beside_ref[0, at], beside_ref[1, at] = arrival(q)

                if rounds:
                    for q in range(1, p + 1):
                        from_arrival(q)
                else:

                    @pl.when((source >= block_rows) & (source <= block_rows + p))
                    def _(at=at, source=source):
                        beside_ref[0, at], beside_ref[1, at] = arrival(source - block_rows)

            mine, other = arrival(p)
            value = dot_nt(beside_ref[0], mine) + dot_nt(beside_ref[1], other)
            high = value.astype(jnp.bfloat16)
            out_ref[p - first, : slots // 2 * block] = high
            put_low(out_ref, p - first, value[:block], high[:block])

    if rounds:
        for p in range(first, last):
            body(p)
    else:
        pl.loop(first, last)(body)


def read_part(parts, mine, index):
    half = len(parts) // 2
    terms = [
        jnp.where(mine, a[index], b[index]).astype(jnp.float32)
        for a, b in zip(parts[:half], parts[half:])
    ]
    while len(terms) > 1:
        terms = [a + b for a, b in zip(terms[::2], terms[1::2])]
    return terms[0]


def place_arrivals(here, first, last, parts, gram_ref, low_ref):
    block = parts[0].shape[2]
    slots = here.slots
    core = lax.rem(lax.axis_index("samp"), 2)

    @pl.loop(first, last)
    def _(p):
        row, k = here.link(p)

        @pl.when(row >= 0)
        def _():
            i = p - first
            for position in range(slots):
                l = slot_at(k, position)
                mine = core == position % 2
                value = read_part(parts, mine, (i, span(position // 2, block)))
                value = jnp.where(here.known(here.source(row, l), p), value, 0.0)
                high = value.astype(jnp.bfloat16)
                gram_ref[row, aligned(l, block), aligned(k, block)] = high
                if position:
                    gram_ref[row, aligned(k, block), aligned(l, block)] = high.T
                else:
                    lows = read_part(parts, mine, (i, pl.ds(slots // 2 * block, 16)))
                    low_ref[row, pl.ds(k, 1)] = low_diagonal(value, high) + lows[:1]


def gather_own_kernel(slots, table_ref, *rest):
    *parts, gram_ref, low_ref, sum_ref, row_ref = rest
    block_rows = gram_ref.shape[0]
    block = parts[0].shape[2]
    core = lax.rem(lax.axis_index("samp"), 2)
    here = Pattern(table_ref, block_rows, slots)
    sum_ref[block_rows] = jnp.zeros(sum_ref.shape[1:], sum_ref.dtype)
    row_ref[...] = jnp.zeros(row_ref.shape, row_ref.dtype)
    low_ref[...] = jnp.zeros(low_ref.shape, low_ref.dtype)
    for a in range(block_rows):
        sum_ref[a, block_rows] = jnp.zeros((block, block), sum_ref.dtype)
    for i, two in enumerate(own_pairs(block_rows)):
        for maker, (a, b) in enumerate(two):
            value = read_part(parts, core == maker, (i, slice(0, block)))
            high = value.astype(jnp.bfloat16)
            sum_ref[a, b] = high
            if a == b:
                lows = read_part(parts, core == maker, (i, slice(block, block + 16)))
                row_ref[a : a + 1] = low_diagonal(value, high) + lows[:1]
            else:
                sum_ref[b, a] = high.T

    @pl.loop(0, block_rows)
    def _(j):
        sources = [here.source(j, k) for k in range(slots)]
        rows = [
            jnp.where((x >= 0) & (x < block_rows), x, block_rows) for x in sources
        ]
        for k, a in enumerate(rows):
            low_ref[j, k : k + 1] = row_ref[pl.ds(a, 1)]
            for l, b in enumerate(rows):
                gram_ref[j, span(k, block), span(l, block)] = sum_ref[a, b]


def gather_kernel(groups, ways, slots, table_ref, gram_in_ref, low_in_ref, *rest):
    *parts, gram_ref, low_ref, sem = rest
    copy = pltpu.make_async_copy(gram_in_ref, gram_ref, sem)
    copy.start()
    low_ref[...] = low_in_ref[...]
    here = Pattern(table_ref, gram_ref.shape[0], slots)
    copy.wait()
    for g, (first, last) in enumerate(groups):
        at = slice(2 * ways * g, 2 * ways * (g + 1))
        place_arrivals(here, first, last, parts[at], gram_ref, low_ref)


def send(here, v_ref, out_refs):
    block = v_ref.shape[1]

    def put(out_ref, index, peer):
        row, column = here.sent(peer)
        out_ref[index] = v_ref[row, :, aligned(column, block)].astype(out_ref.dtype).T

    if len(out_refs) > 1:
        core = lax.rem(lax.axis_index("samp"), 2)
        for out_ref, (a, b) in zip(out_refs, TURNS):
            put(out_ref, ..., jnp.where(core == 0, a, b))
    else:

        @pl.loop(0, out_refs[0].shape[0])
        def _(p):
            put(out_refs[0], p, p)


def receive(in_refs, all_ref):
    core = lax.rem(lax.axis_index("samp"), 2)
    mine_ref, other_ref = in_refs
    for turn, (a, b) in enumerate(TURNS):
        mine, other = mine_ref[turn], other_ref[turn]
        all_ref[a] = jnp.where(core == 0, mine, other)
        all_ref[b] = jnp.where(core == 0, other, mine)
    all_ref[0] = jnp.zeros(all_ref.shape[1:], all_ref.dtype)


def multiply_and_send(here, w_ref, gram_ref, low_ref, v_ref, out_refs):
    block_rows, slots, block = here.block_rows, here.slots, v_ref.shape[1]
    v_ref[:, :, slots * block :] = jnp.zeros((block_rows, block, block), jnp.float32)

    @pl.loop(0, block_rows)
    def _(j):
        value = dot_nn(w_ref[j], gram_ref[j])
        for k in range(slots):
            at = span(k, block)
            low = w_ref[j, :, at].astype(jnp.float32) * low_ref[j, k : k + 1]
            v_ref[j, :, at] = value[:, at] + low

    send(here, v_ref, out_refs)


def step_kernel(first, scale, table_ref, omega_ref, v_ref, stepped_ref):
    block_rows, slots, block, _ = omega_ref.shape
    here = Pattern(table_ref, block_rows, slots)

    @pl.loop(0, block_rows)
    def _(j):
        for k in range(slots):
            row, column = here.mate(j, k)
            omega = omega_ref[j, k]
            if first:
                omega = jnp.where(here.source(j, k) >= 0, omega, 0.0)
            mirrored = v_ref[row, :, aligned(column, block)].T
            stepped_ref[j, k] = omega - scale * (v_ref[j, :, span(k, block)] + mirrored)


def first_kernel(group, ways, table_ref, prec_ref, gram_in_ref, low_in_ref, *rest):
    parts, rest = rest[: 2 * ways], rest[2 * ways :]
    gram_ref, low_ref, v_ref, *out_refs, w_ref, sem = rest
    copy = pltpu.make_async_copy(gram_in_ref, gram_ref, sem)
    copy.start()
    low_ref[...] = low_in_ref[...]
    block_rows, slots, block, _ = prec_ref.shape
    here = Pattern(table_ref, block_rows, slots)

    @pl.loop(0, block_rows)
    def _(j):
        for k in range(slots):
            value = jnp.where(here.source(j, k) >= 0, prec_ref[j, k], 0.0)
            w_ref[j, :, span(k, block)] = value.astype(jnp.bfloat16)

    copy.wait()
    place_arrivals(here, *group, parts, gram_ref, low_ref)
    multiply_and_send(here, w_ref, gram_ref, low_ref, v_ref, out_refs)


def soft(m):
    return m - jnp.clip(m, -SHRINK, SHRINK)


def next_omega(here, j, scale, stepped_ref, in_ref, put):
    block = stepped_ref.shape[2]
    for k in range(here.slots):
        m = stepped_ref[j, k]
        if k == 0:
            root = 0.5 * (m + jnp.sqrt(m * m + 4.0 * STEP))
            put(k, jnp.where(eye_of(block), root, soft(m)))
        else:
            arrived = in_ref[here.peer(j, k)].astype(jnp.float32)
            put(k, soft(m - scale * arrived))


def middle_kernel(count, scale, table_ref, stepped_ref, *rest):
    in_refs, rest = rest[:count], rest[count:]
    gram_ref, low_ref, next_ref, v_ref, *out_refs, w_ref, all_ref = rest
    block_rows, slots, block, _ = stepped_ref.shape
    here = Pattern(table_ref, block_rows, slots)
    if count > 1:
        receive(in_refs, all_ref)

    @pl.loop(0, block_rows)
    def _(j):
        def put(k, value):
            next_ref[j, k] = value
            w_ref[j, :, span(k, block)] = value.astype(jnp.bfloat16)

        next_omega(here, j, scale, stepped_ref, all_ref if count > 1 else in_refs[0], put)

    multiply_and_send(here, w_ref, gram_ref, low_ref, v_ref, out_refs)


def last_kernel(count, scale, table_ref, stepped_ref, *rest):
    *in_refs, out_ref, all_ref, row_ref, sems = rest
    block_rows, slots, block, _ = stepped_ref.shape
    here = Pattern(table_ref, block_rows, slots)
    if count > 1:
        receive(in_refs, all_ref)

    def copy(j):
        return pltpu.make_async_copy(row_ref.at[j], out_ref.at[j], sems.at[j])

    @pl.loop(0, block_rows)
    def _(j):
        def put(k, value):
            row_ref[j, k] = value

        next_omega(here, j, scale, stepped_ref, all_ref if count > 1 else in_refs[0], put)
        copy(j).start()

    @pl.loop(0, block_rows)
    def _(j):
        copy(j).wait()


def call(kernel, inputs, outs, scratch, smem=1, left=(), sems=(), out_space=VMEM):
    arrays = (*inputs, *outs, *scratch)
    size = sum(math.prod(x.shape) * jnp.dtype(x.dtype).itemsize for x in arrays)
    specs = [SMEM] * smem + [VMEM] * (len(inputs) - smem)
    for i in left:
        specs[i] = pl.BlockSpec(memory_space=pl.ANY)
    return pl.pallas_call(
        kernel,
        out_shape=outs,
        in_specs=specs,
        out_specs=[out_space] * len(outs),
        scratch_shapes=[*scratch, *sems],
        compiler_params=pltpu.CompilerParams(vmem_limit_bytes=size + (6 << 20)),
        cost_estimate=pl.CostEstimate(flops=1, bytes_accessed=1, transcendentals=0),
    )(*inputs)


def swap(x, bit):
    count = lax.axis_size("samp")
    return lax.ppermute(x, "samp", [(i, i ^ bit) for i in range(count)])


def from_ys(x):
    return [x] + [swap(x, bit) for bit in range(2, lax.axis_size("samp"), 2)]


def both_cores(parts):
    return (*parts, *(swap(x, 1) for x in parts))


def after(x, *earlier):
    return lax.optimization_barrier((x, *earlier))[0]


def fenced(always, part, *args):
    def nothing(*args):
        return jax.tree.map(lambda x: jnp.zeros(x.shape, x.dtype), jax.eval_shape(part, *args))

    return lax.cond(always, part, nothing, *args)


def local(samples, precision, col_blocks):
    row_count = samples.shape[0]
    block_rows, slots, block, _ = precision.shape
    peers = lax.axis_size("feat")
    ways = lax.axis_size("samp") // 2
    scale = 0.5 * STEP / (row_count * lax.axis_size("samp"))
    rounds = peers == 8 and ways == 2
    groups = [(1, 6), (6, 8)] if rounds else [(0, peers)]

    def shape(dims, dtype):
        return jax.ShapeDtypeStruct(dims, dtype)

    bf16, f32 = samples.dtype, jnp.float32
    strip = (block, row_count)
    sem = pltpu.SemaphoreType.DMA(())
    sends = [shape(strip, bf16)] * (peers - 1) if rounds else [shape((peers, *strip), bf16)]
    own, *sends = call(
        functools.partial(pack_kernel, rounds),
        (col_blocks, samples),
        [shape((block_rows, *strip), bf16), *sends],
        [pltpu.SMEM((peers,), jnp.int32)],
    )

    def exchange(x, r):
        return lax.ppermute(x, "feat", [(i, i ^ r) for i in range(peers)])

    grams = [
        shape((block_rows, slots * block, slots * block), bf16),
        shape((block_rows, 8, block), f32),
    ]

    def pattern():
        width = max(peers, block_rows * slots)
        return call(
            functools.partial(pattern_kernel, rounds, peers),
            (col_blocks,),
            [shape((8, width), jnp.int32)],
            [],
            out_space=SMEM,
        )[0]

    def own_list(own, other):
        return call(
            own_gram_kernel,
            (own, other),
            [shape((block_rows * (block_rows + 1) // 4, block + 16, block), bf16)],
            [],
            smem=0,
        )[0]

    def arrival_list(first, last, table, own_pair, arrived, over):
        return call(
            functools.partial(gram_kernel, rounds, first, last),
            (table, *own_pair, *arrived, *over),
            [shape((last - first, slots // 2 * block + 16, block), bf16)],
            [pltpu.VMEM((2, slots // 2 * block, row_count), bf16)],
        )[0]

    def gather_own(table, *parts):
        return call(
            functools.partial(gather_own_kernel, slots),
            (table, *parts),
            grams,
            [
                pltpu.VMEM((block_rows + 1, block_rows + 1, block, block), bf16),
                pltpu.VMEM((8, block), f32),
            ],
        )

    def gather(table, gram, low, *lists):
        return call(
            functools.partial(gather_kernel, groups[:-1], ways, slots),
            (table, gram, low, *sum(lists, ())),
            grams,
            [],
            left=[1],
            sems=[sem],
        )

    def over_of(blocks, earlier):
        return [swap(after(x, earlier), 1) for x in blocks]

    if rounds:
        other = swap(own, 1)
        own_pair = (own, other)
        ready = [*sends[:2], after(sends[2], other), *sends[3:]]
        arrived = [exchange(ready[r - 1], r) for r in (1, 2, 3, 4, 5)]

        always = after(col_blocks, arrived[0])[0, 0] >= 0

        def begin(own, other):
            return own_list(own, other), pattern()

        step, table = fenced(always, begin, own, other)
        over = over_of(arrived, step)
        arrived += [exchange(after(sends[r - 1], arrived[r - 3]), r) for r in (6, 7)]

        def own_part(table, own_list, own_y):
            return gather_own(table, own_list, own_y, swap(own_list, 1), swap(own_y, 1))

        def most(table, own_pair, arrived, over, own_list):
            own_y = swap(own_list, 2)
            out = after(arrival_list(1, 6, table, own_pair, arrived, over), own_y)
            out_y, own_y = swap(out, 2), after(own_y, out)
            gram, low = fenced(always, own_part, table, own_list, own_y)
            out_core = swap(after(out, gram), 1)
            out_both = swap(after(out_y, gram), 1)
            return gram, low, (out, out_y, out_core, out_both)

        gram, low, *lists = fenced(always, most, table, own_pair, arrived[:5], over, step)
        over += over_of(arrived[5:], gram)
        step = arrival_list(6, 8, table, own_pair, arrived, over)
        gram, low = gather(table, after(gram, step), low, *lists)
        last_list = both_cores([step, after(from_ys(step)[1], gram)])
    else:
        other = swap(own, 1)
        table = pattern()
        arrived = lax.all_to_all(sends[0], "feat", 0, 0, tiled=True)
        gram, low = gather_own(table, *both_cores(from_ys(own_list(own, other))))
        last_list = both_cores(
            from_ys(arrival_list(0, peers, table, (own, other), [arrived], [swap(arrived, 1)]))
        )
    blocks = shape(precision.shape, f32)
    swapped = [shape((block, block) if rounds else (peers, block, block), bf16)]
    if rounds:
        swapped *= len(TURNS)
    all_in = pltpu.VMEM((peers, block, block) if rounds else (8, 128), bf16)

    def trade(out):
        if not rounds:
            return [lax.all_to_all(out[0], "feat", 0, 0, tiled=True)]
        got = []
        for x, turn in zip(out, TURNS):
            pairs = [
                (s * peers + f, s * peers + (f ^ turn[s % 2]))
                for s in range(lax.axis_size("samp"))
                for f in range(peers)
            ]
            got.append(lax.ppermute(x, ("samp", "feat"), pairs))
        got = jnp.stack(got)
        return [got, swap(got, 1)]

    weights = pltpu.VMEM((block_rows, block, slots * block), bf16)
    wide = shape((block_rows, block, (slots + 1) * block), f32)
    gram, low, v, *out = call(
        functools.partial(first_kernel, groups[-1], ways),
        (table, precision, gram, low, *last_list),
        [*grams, wide, *swapped],
        [weights],
        left=[2],
        sems=[sem],
    )
    omega = precision
    for iteration in range(ITERS):
        mirrored = trade(out)
        (stepped,) = call(
            functools.partial(step_kernel, iteration == 0, scale), (table, omega, v), [blocks], []
        )
        if iteration + 1 < ITERS:
            omega, v, *out = call(
                functools.partial(middle_kernel, len(mirrored), scale),
                (table, stepped, *mirrored, gram, low),
                [blocks, wide, *swapped],
                [weights, all_in],
            )
    (updated,) = call(
        functools.partial(last_kernel, len(mirrored), scale),
        (table, stepped, *mirrored),
        [blocks],
        [all_in, pltpu.VMEM(precision.shape, f32)],
        sems=[pltpu.SemaphoreType.DMA((block_rows,))],
        out_space=pl.BlockSpec(memory_space=pl.ANY),
    )
    return updated


def solution(mesh):
    return jax.shard_map(
        local,
        mesh=mesh,
        in_specs=(P("samp", "feat"), P("feat", None, None, None), P("feat", None)),
        out_specs=P("feat", None, None, None),
        check_vma=False,
    )
```
